32 devices in a mesh: section: 4 (over y, x), batch: 8 (over z, core).
Axes of the slice: x: 2, y: 2, z: 4, core: 2. Of those that a mesh axis runs over, the one named last changes fastest.
Arguments:
- inputs: bfloat16 [2, 6144, 768], P(None, 'batch', 'section'), may hold values from -6 to 6
- in_weight: float32 [4, 768, 3072], P('section')
- down_weight: float32 [6144, 768], P('section'), may hold values from -0.109375 to 0.109375
- out_bias: float32 [4, 768], P('section'), may hold values from -3 to 3
- norm_gains: float32 [4, 768], P('section'), may hold values from 0.5 to 1.5
- norm_shifts: float32 [4, 768], P('section'), may hold values from -2 to 2
- projection: float32 [768, 128], P(None, 'section'), may hold values from -0.21875 to 0.21875
- passage_lengths: int32 [2, 8, 3], P(None, 'batch'), may hold values from 1 to 512, 640 in all within a row
- positive: int32 [2, 32], P(None, 'batch'), may hold values from 0 to 2
Outputs:
- total_loss: float32 [], replicated
- input_grad: float32 [2, 6144, 768], P(None, 'batch', 'section')
- in_weight_grad: float32 [4, 768, 3072], P('section')
- down_weight_grad: float32 [6144, 768], P('section')
- out_bias_grad: float32 [4, 768], P('section')
- norm_gain_grad: float32 [4, 768], P('section')
- norm_shift_grad: float32 [4, 768], P('section')
- projection_grad: float32 [768, 128], P(None, 'section')
The draws below stay inside these ranges and needn't reach their ends.
Inputs may be any that keep to these rules, and one draw needn't show every extreme that they name: `passage_lengths`: passage lengths of one micro-batch on one batch device sum to 640; one of them is 512.
All inputs are finite; a program needn't handle non-finite values.
Results may differ from the reference program's by a relative error of at most 0.018.
Values may be sent and summed in bfloat16 or wider, within the bound.
A program may use at most 256 MiB of HBM per device.

```python
import math
import jax
import jax.numpy as jnp
import numpy as np
from jax import lax

D = 768
HEADS = 12
FF = 3072
DIM = 128
QUERY_LENGTH = 32
QUERY_COUNT = 4
PASSAGE_COUNT = 3
PLEN = 512
PASSAGE_TOKENS = 640
MICRO_BATCHES = 2
ROWS = 768
N_SECTION = 4
N_BATCH = 8


def draw_in_weight(key, part):
    key = jax.random.fold_in(key, 7)
    base = jax.random.normal(key, (N_SECTION, D, FF), jnp.float32)
    section_ids = jnp.arange(N_SECTION)[:, None, None]
    columns = jnp.arange(FF)[None, None, :]
    boost = jnp.where((section_ids % 2 == 0) & (columns >= 3 * D), 3.0, 1.0)
    return base * boost * D ** (-0.5)


def set_ends(entries, rng, least, top_value):
    longest = entries.shape.index(max(entries.shape))
    spots = []
    for shift in (0, 1):
        where = [jax.random.randint(jax.random.fold_in(rng, axis), (), 0, length) for axis, length in enumerate(entries.shape)]
        where[longest] = (where[longest] + shift) % entries.shape[longest]
        spots.append(tuple(where))
    return entries.at[spots[0]].set(least).at[spots[1]].set(top_value)


def steps_of(rng, shape, cuts, low, top_value):
    def one(axis_at, shards_of):
        draws = jax.random.uniform(jax.random.fold_in(jax.random.fold_in(rng, 6), axis_at), (shards_of,), jnp.float32, low / len(cuts), top_value / len(cuts))
        return jnp.repeat(jnp.exp(draws), shape[axis_at] // shards_of).reshape((-1,) + (1,) * (len(shape) - axis_at - 1))

    level = one(*cuts[0])
    for cut in cuts[1:]:
        level = level * one(*cut)
    return level


def split_up(number_of, total, reach, skew):
    weights = [(1 << 20) // math.isqrt(grade ** skew) + 1 for grade in range(2, number_of + 1)]
    surplus, counts = total - reach - (number_of - 1), [1] * (number_of - 1)
    while surplus > 0:
        free = [i for i in range(number_of - 1) if counts[i] < reach]
        whole, budget = sum([weights[i] for i in free]), surplus
        for i in free:
            extra = min(reach - counts[i], max(1, budget * weights[i] // whole), surplus)
            counts[i] = counts[i] + extra
            surplus = surplus - extra
    return np.array([reach] + counts)


def uneven(own_key, count, total, reach, skew):
    if count == 2:
        one = jax.random.randint(own_key, (), max(1, total - reach), min(reach, total - 1) + 1)
        return jnp.stack([one, total - one])
    sizes = jnp.asarray(split_up(count, total, reach, skew), jnp.int32)
    pairs = (count - 1) // 2
    donor, receiver = sizes[1:1 + 2 * pairs:2], sizes[2:2 + 2 * pairs:2]
    margin = jnp.minimum(donor - 1, reach - receiver)
    moved = jax.random.randint(jax.random.fold_in(own_key, 1), (pairs,), 0, 1 << 20) % (margin + 1)
    sizes = sizes.at[1:1 + 2 * pairs:2].set(donor - moved).at[2:2 + 2 * pairs:2].set(receiver + moved)
    return sizes[jax.random.permutation(jax.random.fold_in(own_key, 2), count)]


def normal_values(stream_key, dims, scale, reach, split=(), kind=jnp.bfloat16):
    entries = jax.random.normal(stream_key, dims, jnp.float32) * scale
    if len(split) > 0:
        entries = steps_of(stream_key, dims, split, -0.22, 0.18) * entries
    return jnp.clip(entries, min=-reach, max=reach).astype(kind)


def setup_inputs(seed: int = 0) -> dict:
    key_of = jax.random.split(jax.random.key(seed), 10)
    return {
        "inputs": normal_values(key_of[0], (MICRO_BATCHES, N_BATCH * ROWS, D), 1.0, 6.0, ((1, 8), (2, 4))),
        "in_weight": draw_in_weight(jax.random.fold_in(key_of[9], 71), 0),
        "down_weight": normal_values(key_of[2], (N_SECTION * FF // 2, D), FF ** -0.5, 0.109375, ((0, 4),), jnp.float32),
        "out_bias": normal_values(key_of[3], (N_SECTION, D), 0.5, 3.0, ((0, 4),), jnp.float32),
        "norm_gains": jnp.clip(1.0 + 0.1 * jax.random.normal(key_of[4], (N_SECTION, D), jnp.float32), 0.5, 1.5),
        "norm_shifts": normal_values(key_of[5], (N_SECTION, D), 0.3, 2.0, ((0, 4),), jnp.float32),
        "projection": normal_values(key_of[6], (D, DIM), D ** -0.5, 0.21875, ((1, 4),), jnp.float32),
        "passage_lengths": jax.vmap(lambda own: uneven(own, PASSAGE_COUNT, PASSAGE_TOKENS, PLEN, 2))(jax.random.split(key_of[7], MICRO_BATCHES * N_BATCH)).reshape((MICRO_BATCHES, N_BATCH, PASSAGE_COUNT)).astype(jnp.int32),
        "positive": set_ends(jax.random.randint(key_of[8], (MICRO_BATCHES, N_BATCH * QUERY_COUNT), 0, PASSAGE_COUNT), jax.random.fold_in(key_of[8], 1), 0, PASSAGE_COUNT - 1).astype(jnp.int32),
    }


SOFTMAX_DIVISOR = 0.1
SIMILARITY_SCALE = 0.25
NORM_EPSILON = 1e-06

@jax.custom_vjp
def low(v):
    return lax.optimization_barrier(v.astype(jnp.bfloat16)).astype(jnp.float32)

@jax.custom_vjp
def low_back(v):
    return v

def low_keep(v):
    return (low(v), None)

def low_pass(kept, grad):
    return (grad,)

def back_keep(v):
    return (v, None)

def reduced_precision_gradient(kept, grad):
    return (low(grad),)
low.defvjp(low_keep, low_pass)
low_back.defvjp(back_keep, reduced_precision_gradient)

def matmul(left, right):
    return jnp.dot(left, right, precision=lax.Precision.HIGHEST)

def layer_norm(residual, gain, shift):
    row_mean = lax.optimization_barrier(jnp.mean(residual, -1, keepdims=True))
    centered = residual - row_mean
    return centered * lax.rsqrt(lax.optimization_barrier(jnp.mean(centered * centered, -1, keepdims=True)) + NORM_EPSILON) * gain + shift

def sequence_masks(lengths):
    segment_ends = jnp.cumsum(lengths).astype(jnp.int32)
    starts = segment_ends - lengths.astype(jnp.int32)
    token_positions = jnp.arange(PASSAGE_TOKENS, dtype=jnp.int32)
    document_word_validity = (token_positions[None, :] >= starts[:, None]) & (token_positions[None, :] < segment_ends[:, None])
    passage_token_ids = lax.optimization_barrier(jnp.sum((token_positions[:, None] >= segment_ends[None, :]).astype(jnp.int32), 1)) + QUERY_COUNT
    query_token_ids = jnp.arange(QUERY_COUNT * QUERY_LENGTH, dtype=jnp.int32) // QUERY_LENGTH
    sequence_ids = jnp.concatenate([query_token_ids, passage_token_ids])
    return (document_word_validity, sequence_ids[:, None] == sequence_ids[None, :])

def maxsim_loss(word_pair_affinity, document_word_validity, positive):
    divided_logit_matrix = jnp.where(document_word_validity[None, :, :], word_pair_affinity[:, None, :] / SOFTMAX_DIVISOR, -1000000000.0)
    softened_largest_value = SOFTMAX_DIVISOR * jax.nn.logsumexp(divided_logit_matrix, -1)
    passage_scores = lax.optimization_barrier(jnp.sum(softened_largest_value.reshape(QUERY_COUNT, QUERY_LENGTH, -1), 1)) * SIMILARITY_SCALE
    choose = jnp.arange(passage_scores.shape[1], dtype=jnp.int32)[None, :] == positive[:, None]
    picked = lax.optimization_barrier(jnp.sum(jnp.where(choose, passage_scores, 0.0), 1))
    return jnp.sum(jax.nn.logsumexp(passage_scores, -1) - picked)

def attention_block(encoder_part_entry, weight_in, bias_out, norm_gain, norm_shift, same_sequence):
    head_dim = D // HEADS
    row_total_count = encoder_part_entry.shape[0]
    projected = matmul(encoder_part_entry, weight_in[:, :3 * D])
    queries = low(low_back(projected[:, :D])).reshape(row_total_count, HEADS, head_dim)
    keys = low(low_back(projected[:, D:2 * D])).reshape(row_total_count, HEADS, head_dim)
    values = low(low_back(projected[:, 2 * D:])).reshape(row_total_count, HEADS, head_dim)
    raw = jnp.einsum('qhd,khd->hqk', queries, keys, precision=lax.Precision.HIGHEST)
    passage_scores = low_back(raw * head_dim ** (-0.5))
    passage_scores = jnp.where(same_sequence[None], passage_scores, -1000000000.0)
    attn_probs = jnp.exp(passage_scores - jax.nn.logsumexp(passage_scores, -1, keepdims=True))
    context = jnp.einsum('hqk,khd->qhd', low(attn_probs), values, precision=lax.Precision.HIGHEST)
    context = low(low_back(context.reshape(row_total_count, D)))
    attended = low_back(matmul(context, weight_in[:, 3 * D:])) + bias_out
    return layer_norm(encoder_part_entry + attended, norm_gain, norm_shift)

def feed_forward(encoder_part_entry, weight_in, weight_down, bias_out, norm_gain, norm_shift):
    hidden_pre = low_back(matmul(encoder_part_entry, weight_in))
    hidden_low = low(jax.nn.gelu(hidden_pre, approximate=False))
    branch_out = low_back(matmul(hidden_low, weight_down)) + bias_out
    return layer_norm(encoder_part_entry + branch_out, norm_gain, norm_shift)

def head_loss(layer_out, projector, document_word_validity, positive):
    embed_in = low(layer_out)
    projected = low_back(matmul(embed_in, projector))
    normed = projected * lax.rsqrt(lax.optimization_barrier(jnp.sum(projected * projected, -1, keepdims=True)) + NORM_EPSILON)
    embedded = low(normed)
    query_row_block = QUERY_COUNT * QUERY_LENGTH
    word_pair_affinity = low_back(matmul(embedded[:query_row_block], embedded[query_row_block:].T))
    return maxsim_loss(word_pair_affinity, document_word_validity, positive)

def forward(inputs, in_weight, down_weight, out_bias, norm_gains, norm_shifts, projection, passage_lengths, positive):
    weights_low = low(in_weight)
    downs_low = low(down_weight).reshape(2, FF, D)
    projector = low(projection)
    group_labels = MICRO_BATCHES * N_BATCH
    row_total_count = QUERY_COUNT * QUERY_LENGTH + PASSAGE_TOKENS
    group_inputs = inputs.reshape(group_labels, row_total_count, D)
    group_lengths = passage_lengths.reshape(group_labels, PASSAGE_COUNT)
    positive_target = positive.reshape(group_labels, QUERY_COUNT)

    def one_group(group_item):
        tokens_in, lengths, chosen = group_item
        document_word_validity, same_sequence = sequence_masks(lengths)
        hidden = low(tokens_in)
        hidden = low(low_back(attention_block(hidden, weights_low[0], out_bias[0], norm_gains[0], norm_shifts[0], same_sequence)))
        hidden = low(low_back(feed_forward(hidden, weights_low[1], downs_low[0], out_bias[1], norm_gains[1], norm_shifts[1])))
        hidden = low(low_back(attention_block(hidden, weights_low[2], out_bias[2], norm_gains[2], norm_shifts[2], same_sequence)))
        layer_out = feed_forward(hidden, weights_low[3], downs_low[1], out_bias[3], norm_gains[3], norm_shifts[3])
        return head_loss(layer_out, projector, document_word_validity, chosen)
    query_losses = lax.map(jax.checkpoint(one_group), (group_inputs, group_lengths, positive_target))
    return jnp.sum(query_losses) / (group_labels * QUERY_COUNT)

def reference(inputs, in_weight, down_weight, out_bias, norm_gains, norm_shifts, projection, passage_lengths, positive):

    def with_integers(tokens_in, weight_in, weight_down, bias_out, gains, shifts, projector):
        return forward(tokens_in, weight_in, weight_down, bias_out, gains, shifts, projector, passage_lengths, positive)
    loss_value, loss_pull = jax.vjp(with_integers, inputs.astype(jnp.float32), in_weight, down_weight, out_bias, norm_gains, norm_shifts, projection)
    gradients = loss_pull(jnp.ones_like(loss_value))
    return (loss_value, gradients[0], gradients[1], gradients[2], gradients[3], gradients[4], gradients[5], gradients[6])
```

```python
from functools import partial

import jax
import jax.numpy as jnp
from jax import lax
from jax.experimental import pallas as pl
from jax.experimental.pallas import tpu as pltpu
from jax.sharding import PartitionSpec as P

D = 768
HEADS = 12
FF = 3072
DIM = 128
QUERY_LENGTH = 32
QUERY_COUNT = 4
PASSAGE_COUNT = 3
PASSAGE_TOKENS = 640
PLEN = 512
QROWS = QUERY_LENGTH * QUERY_COUNT
ROWS = QROWS + PASSAGE_TOKENS
REST = PASSAGE_TOKENS - PLEN
SOFTMAX_DIVISOR = 0.1
SIMILARITY_SCALE = 0.25
NORM_EPSILON = 1e-06
MASKED = -1000000000.0
BF = jnp.bfloat16
F32 = jnp.float32
BLOCKS = ((0, QROWS), (QROWS, PLEN), (QROWS + PLEN, REST))
PAIRS = HEADS // 4
HALF = D // 2


def mm(a, b, dims=((1,), (0,))):
    return lax.dot_general(a, b, (dims, ((), ())), preferred_element_type=F32)


def block_mask(which, bound, rows):
    t = lax.broadcasted_iota(jnp.int32, (rows, rows), 0)
    r = lax.broadcasted_iota(jnp.int32, (rows, rows), 1)
    if which == 0:
        return (t // QUERY_LENGTH) == (r // QUERY_LENGTH)
    return (t < bound) == (r < bound)


def attention_kernel(bound_ref, qkv_ref, ctx_ref, lse_ref):
    lane = lax.broadcasted_iota(jnp.int32, (1, 128), 1)
    for which, (start, size) in enumerate(BLOCKS):
        chunk = min(size, 256)
        k = qkv_ref[start : start + size, 128:256]
        v = qkv_ref[start : start + size, 256:384]
        for at in range(start, start + size, chunk):
            q = qkv_ref[at : at + chunk, 0:128]
            total = None
            for head in range(2):
                mine = (lane < 64) if head == 0 else (lane >= 64)
                qm = jnp.where(mine, q, jnp.zeros_like(q)) * BF(0.125)
                vm = jnp.where(mine, v, jnp.zeros_like(v))
                s = mm(k, qm, ((1,), (1,)))
                if which != 1:
                    s = jnp.where(block_mask(which, bound_ref[0], size), s, MASKED)
                top = jnp.max(s, axis=0, keepdims=True)
                e = jnp.exp(s - top)
                weight = jnp.sum(e, axis=0, keepdims=True)
                part = mm(vm, e.astype(BF), ((0,), (0,))) * (1.0 / weight)
                total = part if total is None else total + part
                lse_ref[0, head : head + 1, at : at + chunk] = top + jnp.log(weight)
            ctx_ref[at : at + chunk, :] = total.T.astype(BF)


def attention(qkv, bound):
    return pl.pallas_call(
        attention_kernel,
        grid=(PAIRS,),
        in_specs=[
            pl.BlockSpec(memory_space=pltpu.SMEM),
            pl.BlockSpec((ROWS, 384), lambda i: (0, i)),
        ],
        out_specs=[
            pl.BlockSpec((ROWS, 128), lambda i: (0, i)),
            pl.BlockSpec((1, 8, ROWS), lambda i: (i, 0, 0)),
        ],
        out_shape=[
            jax.ShapeDtypeStruct((ROWS, HALF), BF),
            jax.ShapeDtypeStruct((PAIRS, 8, ROWS), F32),
        ],
        compiler_params=pltpu.CompilerParams(vmem_limit_bytes=32 * 1024 * 1024),
        cost_estimate=pl.CostEstimate(
            flops=12 * 4 * 512 * 512 * 64, bytes_accessed=3000000, transcendentals=2000000
        ),
    )(bound, qkv)


def attention_back_kernel(bound_ref, qkv_ref, dc_ref, lse_ref, out_ref):
    lane = lax.broadcasted_iota(jnp.int32, (1, 128), 1)
    for which, (start, size) in enumerate(BLOCKS):
        chunk = min(size, 256)
        k = qkv_ref[start : start + size, 128:256]
        v = qkv_ref[start : start + size, 256:384]
        dk = jnp.zeros((size, 128), F32)
        dv = jnp.zeros((size, 128), F32)
        for at in range(start, start + size, chunk):
            q = qkv_ref[at : at + chunk, 0:128]
            dc = dc_ref[at : at + chunk, :]
            dq = None
            for head in range(2):
                mine = (lane < 64) if head == 0 else (lane >= 64)
                qm = jnp.where(mine, q, jnp.zeros_like(q)) * BF(0.125)
                dcm = jnp.where(mine, dc, jnp.zeros_like(dc))
                km = jnp.where(mine, k, jnp.zeros_like(k))
                s = mm(k, qm, ((1,), (1,)))
                if which != 1:
                    s = jnp.where(block_mask(which, bound_ref[0], size), s, MASKED)
                p = jnp.exp(s - lse_ref[0, head : head + 1, at : at + chunk])
                dp = mm(v, dcm, ((1,), (1,)))
                inner = jnp.sum(p * dp, axis=0, keepdims=True)
                ds = (p * (dp - inner)).astype(BF)
                dv = dv + mm(p.astype(BF), dcm)
                dk = dk + mm(ds, qm)
                part = mm(km, ds, ((0,), (0,)))
                dq = part if dq is None else dq + part
            out_ref[at : at + chunk, 0:128] = (dq.T * 0.125).astype(BF)
        out_ref[start : start + size, 128:256] = dk.astype(BF)
        out_ref[start : start + size, 256:384] = dv.astype(BF)


def attention_back(qkv, dc, lse, bound):
    return pl.pallas_call(
        attention_back_kernel,
        grid=(PAIRS,),
        in_specs=[
            pl.BlockSpec(memory_space=pltpu.SMEM),
            pl.BlockSpec((ROWS, 384), lambda i: (0, i)),
            pl.BlockSpec((ROWS, 128), lambda i: (0, i)),
            pl.BlockSpec((1, 8, ROWS), lambda i: (i, 0, 0)),
        ],
        out_specs=pl.BlockSpec((ROWS, 384), lambda i: (0, i)),
        out_shape=jax.ShapeDtypeStruct((ROWS, 3 * HALF), BF),
        compiler_params=pltpu.CompilerParams(vmem_limit_bytes=32 * 1024 * 1024),
        cost_estimate=pl.CostEstimate(
            flops=12 * 10 * 512 * 512 * 64, bytes_accessed=5000000, transcendentals=2000000
        ),
    )(bound, qkv, dc, lse)


MESH = pl.DeviceIdType.MESH
EXTRA = 32
FRONT = 1152


def neighbours():
    s, b = lax.axis_index("section"), lax.axis_index("batch")
    x = s + 1 - 2 * (s % 2)
    y = s + 2 - 4 * (s // 2)
    xy = 3 - s
    return s, b, x, y, xy


def greet(layers):
    s, b, x, y, xy = neighbours()
    z, core = b // 2, b % 2
    barrier = pltpu.get_barrier_semaphore()

    def signal(to):
        pl.semaphore_signal(barrier, inc=1, device_id=to, device_id_type=MESH)

    signal((x, b))
    signal((y, b))
    signal((xy, b))
    signal((s, b + 1 - 2 * core))
    if layers > 1:

        @pl.when(z > 0)
        def _():
            signal((s, b - 2))

        @pl.when(z < layers - 1)
        def _():
            signal((s, b + 2))

        ends = (layers - 1 - z) // (layers - 1) + z // (layers - 1)
        pl.semaphore_wait(barrier, 6 - ends)
    else:
        pl.semaphore_wait(barrier, 4)


def fetch_kernel(
    layers,
    spread,
    w_ref,
    down_ref,
    tail_ref,
    vec_ref,
    slices_ref,
    ints_ref,
    first_all,
    rest_all,
    vec_all,
    parts_all,
    ints_other,
    wide,
    out_stage,
    down_stage,
    first,
    rest,
    load_sem,
    own_sem,
    send_sem,
    recv_sem,
    z_send,
    z_recv,
    in_send,
    in_recv,
):
    s, b, x, y, xy = neighbours()
    z, core = b // 2, b % 2
    micro = s // 2
    mine = core == s % 2
    twin = b + 1 - 2 * core

    def load(src, dst, i):
        return pltpu.make_async_copy(src, dst, load_sem.at[i])

    loads = [load(down_ref.at[pl.ds(core * D, D), :], down_stage, 0)]
    even, odd = [], []
    for i in range(PAIRS):
        for t in range(3):
            at = pl.multiple_of(t * D + core * HALF + i * 128, 128)
            to = (3 * i + t) * 128
            even.append(
                load(w_ref.at[:, pl.ds(at, 128)], wide.at[:, pl.ds(to, 128)], 1 + 3 * i + t)
            )
    even.append(load(w_ref.at[pl.ds(core * HALF, HALF), pl.ds(3 * D, D)], out_stage, 10))
    for i in range(2):
        at = pl.multiple_of(i * 2 * D + core * D, 128)
        odd.append(load(w_ref.at[:, pl.ds(at, D)], wide.at[:, pl.ds(i * D, D)], 11 + i))
    loads[0].start()

    @pl.when(s % 2 == 0)
    def _():
        for copy in even:
            copy.start()

    @pl.when(s % 2 == 1)
    def _():
        for copy in odd:
            copy.start()

    tail = pltpu.make_async_copy(
        tail_ref, rest.at[pl.ds(FRONT, EXTRA), :], load_sem.at[13]
    )
    tail.start()
    greet(layers)

    def feature(i, which, section, to):
        return pltpu.make_async_remote_copy(
            src_ref=slices_ref.at[which],
            dst_ref=parts_all.at[section],
            send_sem=in_send.at[i],
            recv_sem=in_recv.at[i],
            device_id=(to, b),
            device_id_type=MESH,
        )

    def to_twin(i, src, dst):
        return pltpu.make_async_remote_copy(
            src_ref=src,
            dst_ref=dst,
            send_sem=in_send.at[i],
            recv_sem=in_recv.at[i],
            device_id=(s, twin),
            device_id_type=MESH,
        )

    def quarter_to_twin(i, f):
        return to_twin(i, parts_all.at[f], parts_all.at[f])

    swap_ints = to_twin(7, ints_ref, ints_other)
    own_quarter = pltpu.make_async_copy(slices_ref.at[micro], parts_all.at[s], load_sem.at[14])
    swap_ints.start()

    @pl.when(mine)
    def _():
        own_quarter.start()
        feature(1, 1 - micro, s, y).start()

    @pl.when(jnp.logical_not(mine))
    def _():
        feature(0, micro, s, x).start()
        feature(2, 1 - micro, s, xy).start()

    loads[0].wait()

    @pl.loop(0, D // 96)
    def _(i):
        rows = pl.ds(pl.multiple_of(i * 96, 16), 96)
        to = pl.ds(pl.multiple_of(HALF + i * 96, 16), 96)
        rest[to, :] = down_stage[rows, :].astype(BF)

    @pl.when(s % 2 == 0)
    def _():
        for copy in even:
            copy.wait()

        @pl.loop(0, HALF // 96)
        def _(i):
            rows = pl.ds(pl.multiple_of(i * 96, 16), 96)
            rest[rows, :] = out_stage[rows, :].astype(BF)

    @pl.when(s % 2 == 1)
    def _():
        for copy in odd:
            copy.wait()
        for i in range(3):
            for j in range(6):
                block = wide[j * 128 : (j + 1) * 128, FRONT + i * 128 : FRONT + (i + 1) * 128]
                rest[i * 128 : (i + 1) * 128, j * 128 : (j + 1) * 128] = block.T.astype(BF)

    @pl.loop(0, D // 96)
    def _(i):
        rows = pl.ds(pl.multiple_of(i * 96, 16), 96)
        first[rows, :] = wide[rows, 0:FRONT].astype(BF)

    tail.wait()

    quarter = D // 4
    firsts = [(first, first_all, i * quarter, quarter, i < 2) for i in range(4)]
    seconds = [(rest, rest_all, i * 192, 192, i == 0) for i in range(2)]
    small = [
        (rest, rest_all, FRONT, EXTRA, True),
        (vec_ref, vec_all, 0, 8, False),
    ]
    if spread:
        share = D // layers
        at = pl.multiple_of(HALF + z * share, 16)
        half = share // 2
        slices = [
            (rest, rest_all, at, half, True),
            (rest, rest_all, pl.multiple_of(at + half, 16), share - half, False),
        ]
    else:
        slices = [(rest, rest_all, HALF + i * 192, 192, i < 2) for i in range(4)]
    pieces = slices + firsts + seconds + small

    def part(n, ref):
        unused, unused, row, rows, unused = pieces[n]
        return ref.at[pl.ds(row, rows), :]

    def remote(n, kind, src, dst, to):
        return pltpu.make_async_remote_copy(
            src_ref=src,
            dst_ref=dst,
            send_sem=send_sem.at[kind, n],
            recv_sem=recv_sem.at[kind, n],
            device_id=(to, b),
            device_id_type=MESH,
        )

    def direct(n, kind):
        mine, every = pieces[n][:2]
        return remote(n, kind, part(n, mine), part(n, every.at[s]), y if kind else x)

    def arrived(n, kind):
        every = pieces[n][1]
        owner = (x, y, xy)[kind]
        here = part(n, every.at[owner])
        remote(n, kind, here, here, x).wait_recv()

    def relay(n):
        every, by_x = pieces[n][1], pieces[n][4]
        source = part(n, every.at[x if by_x else y])
        return remote(n, 2, source, source, y if by_x else x)

    def pass_on(n):
        arrived(n, 0 if pieces[n][4] else 1)
        relay(n).start()

    count = len(pieces)
    by_x = [n for n in range(count) if pieces[n][4]]
    by_y = [n for n in range(count) if not pieces[n][4]]
    small_n = list(range(count - 2, count))

    def early(n):
        direct(n, 0 if pieces[n][4] else 1).start()

    def late(n):
        direct(n, 1 if pieces[n][4] else 0).start()

    own = [
        pltpu.make_async_copy(first, first_all.at[s], own_sem.at[0]),
        pltpu.make_async_copy(rest, rest_all.at[s], own_sem.at[1]),
        pltpu.make_async_copy(vec_ref, vec_all.at[s], own_sem.at[2]),
    ]

    z_width = D // layers if spread else 0

    def z_part(section, owner_z):
        at = pl.multiple_of(HALF + owner_z * z_width, 16)
        return rest_all.at[section, pl.ds(at, z_width), :]

    def z_copy(way, step, k, owner_z, to_b):
        source = z_part((x, y, xy)[k], owner_z)
        return pltpu.make_async_remote_copy(
            src_ref=source,
            dst_ref=source,
            send_sem=z_send.at[way, step, k],
            recv_sem=z_recv.at[way, step, k],
            device_id=(s, to_b),
            device_id_type=MESH,
        )

    def z_first(k):
        @pl.when(z < layers - 1)
        def _():
            z_copy(0, 0, k, z, b + 2).start()

        @pl.when(z > 0)
        def _():
            z_copy(1, 0, k, z, b - 2).start()

    def z_step(step):
        @pl.when(z >= step)
        def _():
            for k in range(3):
                z_copy(0, step - 1, k, z - step, b).wait_recv()

                @pl.when(z < layers - 1)
                def _():
                    z_copy(0, step, k, z - step, b + 2).start()

        @pl.when(z < layers - step)
        def _():
            for k in range(3):
                z_copy(1, step - 1, k, z + step, b).wait_recv()

                @pl.when(z > 0)
                def _():
                    z_copy(1, step, k, z + step, b - 2).start()

    def z_drain():
        for step in range(layers - 1):

            @pl.when((z < layers - 1) & (z >= step))
            def _():
                for k in range(3):
                    z_copy(0, step, k, z - step, b + 2).wait_send()

            @pl.when((z > 0) & (z + step < layers))
            def _():
                for k in range(3):
                    z_copy(1, step, k, z + step, b - 2).wait_send()

    queue_x = [n for n in by_x]
    queue_y = [n for n in by_y]
    for n in queue_x[:2] + queue_y[:2]:
        early(n)
    for copy in own:
        copy.start()

    @pl.when(mine)
    def _():
        own_quarter.wait()
        quarter_to_twin(3, s).start()
        for i, owner in enumerate((x, y, xy)):
            feature(i, 0, owner, x).wait_recv()
            quarter_to_twin(4 + i, owner).start()
    rounds = max(len(queue_x), len(queue_y))
    late_x, late_y = list(queue_y), list(queue_x)
    z_at = 1
    for i in range(rounds):
        for queue in (queue_x, queue_y):
            if i < len(queue):
                pass_on(queue[i])
                if i + 2 < len(queue):
                    early(queue[i + 2])
                else:
                    other = late_x if queue is queue_x else late_y
                    if other:
                        late(other.pop(0))
        if spread and i == 0:
            for n, kind in ((0, 1), (1, 0)):
                late(n)
                (late_x if kind == 0 else late_y).remove(n)
        if spread and i == 1:
            arrived(0, 1)
            arrived(1, 0)
            z_first(0)
            z_first(1)
            arrived(0, 2)
            arrived(1, 2)
            z_first(2)
        if spread and i >= 2 and z_at < layers - 1:
            z_step(z_at)
            z_at += 1
    for n in late_x + late_y:
        late(n)
    done = set()
    if spread:
        done = {(0, 1), (1, 0), (0, 2), (1, 2)}
        while z_at < layers:
            z_step(z_at)
            z_at += 1
    for n in range(count):
        for kind in range(3):
            if kind == 2 or kind == (1 if pieces[n][4] else 0):
                if (n, kind) not in done:
                    arrived(n, kind)
    for n in range(count):
        direct(n, 0).wait_send()
        direct(n, 1).wait_send()
        relay(n).wait_send()
    if spread:
        z_drain()
    for copy in own:
        copy.wait()
    swap_ints.wait()

    @pl.when(mine)
    def _():
        feature(1, 1 - micro, s, y).wait_send()
        for i, owner in enumerate((s, x, y, xy)):
            quarter_to_twin(3 + i, owner).wait_send()

    @pl.when(jnp.logical_not(mine))
    def _():
        feature(0, micro, s, x).wait_send()
        feature(2, 1 - micro, s, xy).wait_send()
        for i, owner in enumerate((s, x, y, xy)):
            quarter_to_twin(3 + i, owner).wait_recv()


def fetch_weights(w, down, tail, vec, slices, ints, layers):
    spread = layers > 1 and D % (32 * layers) == 0
    anywhere = pl.BlockSpec(memory_space=pl.ANY)
    pieces = 12 if not spread else 10
    steps = max(layers - 1, 1) if spread else 1
    return pl.pallas_call(
        partial(fetch_kernel, layers, spread),
        in_specs=[anywhere] * 6,
        out_specs=[anywhere] * 5,
        out_shape=[
            jax.ShapeDtypeStruct((4, D, FRONT), BF),
            jax.ShapeDtypeStruct((4, FRONT + EXTRA, D), BF),
            jax.ShapeDtypeStruct((4, 8, D), F32),
            jax.ShapeDtypeStruct((4,) + slices.shape[1:], BF),
            jax.ShapeDtypeStruct(ints.shape, jnp.int32),
        ],
        scratch_shapes=[
            pltpu.VMEM((D, 2 * D), F32),
            pltpu.VMEM((HALF, D), F32),
            pltpu.VMEM((D, D), F32),
            pltpu.VMEM((D, FRONT), BF),
            pltpu.VMEM((FRONT + EXTRA, D), BF),
            pltpu.SemaphoreType.DMA((15,)),
            pltpu.SemaphoreType.DMA((3,)),
            pltpu.SemaphoreType.DMA((3, pieces)),
            pltpu.SemaphoreType.DMA((3, pieces)),
            pltpu.SemaphoreType.DMA((2, steps, 3)),
            pltpu.SemaphoreType.DMA((2, steps, 3)),
            pltpu.SemaphoreType.DMA((8,)),
            pltpu.SemaphoreType.DMA((8,)),
        ],
        compiler_params=pltpu.CompilerParams(
            collective_id=1, has_side_effects=True, vmem_limit_bytes=40 * 1024 * 1024
        ),
    )(w, down, tail, vec, slices, ints)


TAIL = 48
SIDE = HALF + TAIL
STREAMS = ((D, FRONT, 32, True), (SIDE, D, 16, True), (D, D, 32, False))
CHUNKS = tuple(rows // step for rows, unused, step, unused2 in STREAMS)
ONE_LOW, ONE_HIGH, TWO, INWARD, BACK, TWIN = 0, 3, 6, 9, 12, 15


def backward_kernel(layers, lags, *refs):
    hs, xhats, scales = refs[0:4], refs[4:8], refs[8:12]
    qkvs, ctxs, lses, acts, slopes = refs[12:14], refs[14:16], refs[16:18], refs[18:20], refs[20:22]
    first_all, rest_all, tails, bound_ref, vec_ref, dw_ref = refs[22:28]
    outs, out_back = refs[28:31], refs[31]
    sums, ones, twos, ins, backs = refs[32:35], refs[35:38], refs[38:41], refs[41:44], refs[44:47]
    (
        h_f,
        xhat_f,
        scale_f,
        slope,
        up_first,
        up_second,
        act_ring,
        down_ring,
        h_a,
        xhat_a,
        scale_a,
        qkv,
        ctx,
        lse,
        att_first,
        att_second,
        proj,
        dy,
        dc,
        part_out,
        part_in,
        shares,
        load_sem,
        ring_sem,
        part_send,
        part_recv,
        send_sem,
        recv_sem,
        keep_sem,
        in_send,
        in_recv,
    ) = refs[47:]
    s, b, x, y, xy = neighbours()
    z, core = b // 2, b % 2
    half = s // 2
    parity = s % 2
    mine = core == parity
    twin = b + 1 - 2 * core
    middle = max(layers // 2 - 1, 0)
    upper = z // max(layers // 2, 1)
    depth = z + upper * (layers - 1 - 2 * z)
    toward = b + 2 - 4 * upper
    outward = b - 2 + 4 * upper
    lag_z, lag_step = lags

    def load(src, dst, i):
        return pltpu.make_async_copy(src, dst, load_sem.at[i])

    def loads_ffn(l):
        t = 2 * l + 1
        return [
            load(hs[t], h_f, 0),
            load(xhats[t], xhat_f, 1),
            load(scales[t], scale_f, 2),
            load(slopes[l], slope, 3),
            load(first_all.at[t], up_first, 4),
            load(rest_all.at[t, pl.ds(0, HALF), :], up_second, 5),
        ]

    def loads_attention(l):
        t = 2 * l
        return [
            load(hs[t], h_a, 6),
            load(xhats[t], xhat_a, 7),
            load(scales[t], scale_a, 8),
            load(qkvs[l], qkv, 9),
            load(ctxs[l], ctx, 10),
            load(lses[l], lse, 11),
            load(first_all.at[t], att_first, 12),
            load(rest_all.at[t, pl.ds(0, HALF), :], att_second, 13),
        ]

    def ring(l, j):
        slot = j % 2
        rows = pl.ds(HALF + (j % 2) * HALF, HALF)
        return (
            pltpu.make_async_copy(
                acts[l].at[:, pl.ds(j * HALF, HALF)], act_ring.at[slot], ring_sem.at[0, slot]
            ),
            pltpu.make_async_copy(
                rest_all.at[2 * l + j // 2, rows, :], down_ring.at[slot], ring_sem.at[1, slot]
            ),
        )

    def start(copies):
        for copy in copies:
            copy.start()

    def wait(copies):
        for copy in copies:
            copy.wait()

    start_loads = [
        load(rest_all.at[t, pl.ds(FRONT, EXTRA), :], proj.at[pl.ds(t * EXTRA, EXTRA), :], 14 + t)
        for t in range(4)
    ] + [load(tails.at[t], sums[1].at[t, pl.ds(HALF, TAIL), :], 18 + t) for t in range(4)]
    start(start_loads)
    start(loads_ffn(1))
    start(ring(1, 0))
    start(ring(1, 1))
    start(loads_attention(1))
    greet(layers)
    wait(start_loads)

    def remote(kind, chunk, src, dst, to):
        return pltpu.make_async_remote_copy(
            src_ref=src,
            dst_ref=dst,
            send_sem=send_sem.at[kind, chunk],
            recv_sem=recv_sem.at[kind, chunk],
            device_id=to,
            device_id_type=MESH,
        )

    def rows_of(which, chunk):
        size = STREAMS[which][2]
        return pl.ds(pl.multiple_of(chunk * size, 16), size)

    def one(which, chunk, l):
        rows = rows_of(which, chunk)
        kind = (ONE_HIGH if l else ONE_LOW) + which
        if STREAMS[which][3]:
            src = sums[which].at[2 * l + 1 - parity, rows, :]
            return remote(kind, chunk, src, ones[which].at[l, rows, :], (x, b))
        src = sums[which].at[2 * (1 - half) + l, rows, :]
        return remote(kind, chunk, src, ones[which].at[l, rows, :], (y, b))

    def forwarded(which):
        return 2 * (1 - half) + parity if STREAMS[which][3] else 2 * half + 1 - parity

    def two(which, chunk):
        rows = rows_of(which, chunk)
        src = sums[which].at[forwarded(which), rows, :]
        to = y if STREAMS[which][3] else x
        return remote(TWO + which, chunk, src, twos[which].at[rows, :], (to, b))

    def inward(which, chunk, swap):
        rows = rows_of(which, chunk)
        src = sums[which].at[s, rows, :]
        if swap:
            return remote(BACK + which, chunk, src, backs[which].at[rows, :], (s, toward))
        return remote(INWARD + which, chunk, src, ins[which].at[rows, :], (s, toward))

    def final(which, at_middle):
        return sums[which].at[s] if at_middle else backs[which]

    def outward_copy(which, chunk, at_middle):
        rows = rows_of(which, chunk)
        src = final(which, at_middle).at[rows, :]
        return remote(BACK + which, chunk, src, backs[which].at[rows, :], (s, outward))

    def twin_copy(which, chunk, at_middle):
        rows = rows_of(which, chunk)
        src = final(which, at_middle).at[rows, :]
        return remote(TWIN + which, chunk, src, outs[which].at[core, rows, :], (s, twin))

    def keep_copy(which, chunk, at_middle):
        rows = rows_of(which, chunk)
        src = final(which, at_middle).at[rows, :]
        return pltpu.make_async_copy(
            src, outs[which].at[core, rows, :], keep_sem.at[which, chunk]
        )

    def plus(*values):
        total = values[0].astype(F32)
        for value in values[1:]:
            total = total + value.astype(F32)
        return total

    def send_x_first(which, l, start_row, rows):
        size = STREAMS[which][2]

        def body(c, unused):
            one(which, c, l).start()
            return unused

        lax.fori_loop(start_row // size, (start_row + rows) // size, body, 0)

    def send_y_first(which, layer, p, start_row, rows):
        size = STREAMS[which][2]

        @pl.when(half != layer)
        def _():
            def body(c, unused):
                one(which, c, p).start()
                return unused

            lax.fori_loop(start_row // size, (start_row + rows) // size, body, 0)

    def swap_copy(t, i):
        rows = pl.ds(i * 256, 256)
        return pltpu.make_async_remote_copy(
            src_ref=part_out.at[rows, :],
            dst_ref=part_in.at[t % 2, rows, :],
            send_sem=part_send.at[t, i],
            recv_sem=part_recv.at[t, i],
            device_id=(s, twin),
            device_id_type=MESH,
        )

    def norm_back(t, grad_of, xhat, scale):
        gain = vec_ref[t, 1:2, :]

        def body(i, carry):
            rows = pl.ds(pl.multiple_of(i * 128, 128), 128)
            grad = grad_of(rows)
            xh = xhat[rows, :].astype(F32)
            weighted = grad * gain
            mean_1 = jnp.mean(weighted, -1, keepdims=True)
            mean_2 = jnp.mean(weighted * xh, -1, keepdims=True)
            du = scale[rows, 0:1] * (weighted - mean_1 - xh * mean_2)
            dy[rows, :] = du.astype(BF)
            return (
                carry[0] + jnp.sum(du, 0, keepdims=True),
                carry[1] + jnp.sum(grad * xh, 0, keepdims=True),
                carry[2] + jnp.sum(grad, 0, keepdims=True),
            )

        zero = jnp.zeros((1, D), F32)
        carry = (zero, zero, zero)
        for i in range(3):
            if t < 3:
                swap_copy(t + 1, i).wait_recv()
            carry = lax.fori_loop(2 * i, 2 * i + 2, body, carry)
        row = lax.broadcasted_iota(jnp.int32, (16, 1), 0)
        block = sums[1][t, HALF : HALF + 16, :].astype(F32)
        for i in range(3):
            block = jnp.where(row == i, carry[i], block)
        sums[1][t, HALF : HALF + 16, :] = block.astype(BF)

    def grad_from_head(rows):
        return mm(dw_ref[rows, :], proj[...])

    def grad_from(t):
        def grad_of(rows):
            total = plus(dy[rows, :], part_out[rows, :], part_in[t % 2, rows, :])
            return total.astype(BF).astype(F32)

        return grad_of

    def ffn_back(l):
        t = 2 * l + 1
        for j in range(4):
            wait(ring(l, j))
            slot = j % 2
            columns = slice(j * HALF, (j + 1) * HALF)
            low = dy[...]
            to = (j % 2) * HALF
            sums[2][2 * l + j // 2, to : to + HALF, :] = mm(
                act_ring[slot], low, ((0,), (0,))
            ).astype(BF)
            send_y_first(2, l, j // 2, to, HALF)
            for i in range(3):
                rows = slice(i * 256, (i + 1) * 256)
                grad = mm(dy[rows, :], down_ring[slot], ((1,), (1,)))
                slope[rows, columns] = (grad * slope[rows, columns].astype(F32)).astype(BF)
            if j < 2:
                start(ring(l, j + 2))
        for i in range(3):
            rows = slice(i * 256, (i + 1) * 256)
            if t < 3:
                swap_copy(t + 1, i).wait_send()
            part = mm(slope[rows, 0:FRONT], up_first[...], ((1,), (1,)))
            part = part + mm(slope[rows, FRONT:], up_second[...])
            part_out[rows, :] = part.astype(BF)
            swap_copy(t, i).start()
        for i in range(3):
            rows = slice(i * 256, (i + 1) * 256)
            sums[0][t, rows, :] = mm(h_f[:, rows], slope[:, 0:FRONT], ((0,), (0,))).astype(BF)
        sums[1][t, 0:HALF, :] = mm(slope[:, FRONT:], h_f[...], ((0,), (0,))).astype(BF)

    def attention_pair(i, unused):
        lane = lax.broadcasted_iota(jnp.int32, (1, 128), 1)
        base = pl.multiple_of(i * 384, 128)
        q_at, k_at, v_at = (
            pl.ds(base, 128),
            pl.ds(pl.multiple_of(base + 128, 128), 128),
            pl.ds(pl.multiple_of(base + 256, 128), 128),
        )
        c_at = pl.ds(pl.multiple_of(i * 128, 128), 128)
        for which, (begin, size) in enumerate(BLOCKS):
            chunk = min(size, 256)
            span = slice(begin, begin + size)
            k = qkv[span, k_at]
            v = qkv[span, v_at]
            dk = jnp.zeros((size, 128), F32)
            dv = jnp.zeros((size, 128), F32)
            for at in range(begin, begin + size, chunk):
                rows = slice(at, at + chunk)
                q = qkv[rows, q_at]
                dcs = dc[rows, c_at]
                dq = None
                for head in range(2):
                    own = (lane < 64) if head == 0 else (lane >= 64)
                    qm = jnp.where(own, q, jnp.zeros_like(q)) * BF(0.125)
                    dcm = jnp.where(own, dcs, jnp.zeros_like(dcs))
                    km = jnp.where(own, k, jnp.zeros_like(k))
                    score = mm(k, qm, ((1,), (1,)))
                    if which != 1:
                        score = jnp.where(block_mask(which, bound_ref[0], size), score, MASKED)
                    p = jnp.exp(score - lse[i, head : head + 1, rows])
                    dp = mm(v, dcm, ((1,), (1,)))
                    inner = jnp.sum(p * dp, axis=0, keepdims=True)
                    ds = (p * (dp - inner)).astype(BF)
                    dv = dv + mm(p.astype(BF), dcm)
                    dk = dk + mm(ds, qm)
                    part = mm(km, ds, ((0,), (0,)))
                    dq = part if dq is None else dq + part
                qkv[rows, q_at] = (dq.T * 0.125).astype(BF)
            qkv[span, k_at] = dk.astype(BF)
            qkv[span, v_at] = dv.astype(BF)
        return unused

    def attention_grads(l):
        t = 2 * l
        sums[1][t, 0:HALF, :] = mm(ctx[...], dy[...], ((0,), (0,))).astype(BF)
        for i in range(3):
            rows = slice(i * 256, (i + 1) * 256)
            dc[rows, :] = mm(dy[rows, :], att_second[...], ((1,), (1,))).astype(BF)
        lax.fori_loop(0, PAIRS, attention_pair, 0)
        for i in range(3):
            rows = slice(i * 256, (i + 1) * 256)
            swap_copy(t + 1, i).wait_send()
            part_out[rows, :] = mm(qkv[rows, :], att_first[...], ((1,), (1,))).astype(BF)
            swap_copy(t, i).start()
        for i in range(3):
            rows = slice(i * 256, (i + 1) * 256)
            sums[0][t, rows, :] = mm(h_a[:, rows], qkv[...], ((0,), (0,))).astype(BF)

    def start_x_first(t):
        l, p = t // 2, t % 2

        @pl.when(parity != p)
        def _():
            for which in (1, 0):
                send_x_first(which, l, 0, STREAMS[which][0])

    wait(loads_ffn(1))
    norm_back(3, grad_from_head, xhat_f, scale_f)
    ffn_back(1)
    start_x_first(3)
    start(loads_ffn(0))
    start(ring(0, 0))
    start(ring(0, 1))
    wait(loads_attention(1))
    norm_back(2, grad_from(3), xhat_a, scale_a)
    attention_grads(1)
    start_x_first(2)
    start(loads_attention(0))
    wait(loads_ffn(0))
    norm_back(1, grad_from(2), xhat_f, scale_f)
    ffn_back(0)
    start_x_first(1)
    wait(loads_attention(0))
    norm_back(0, grad_from(1), xhat_a, scale_a)
    attention_grads(0)
    start_x_first(0)

    width = shares.shape[2]
    for i in range(3):
        swap_copy(0, i).wait_recv()

        def body(j, unused):
            rows = pl.ds(pl.multiple_of(j * 64, 64), 64)
            total = plus(dy[rows, :], part_out[rows, :], part_in[0, rows, :])
            for f in range(4):
                shares[f, rows, :] = total[:, f * width : (f + 1) * width].astype(BF)
            return unused

        lax.fori_loop(4 * i, 4 * i + 4, body, 0)

    def back_to(i, to):
        return pltpu.make_async_remote_copy(
            src_ref=shares.at[to],
            dst_ref=out_back.at[i],
            send_sem=in_send.at[i],
            recv_sem=in_recv.at[i],
            device_id=(to, b),
            device_id_type=MESH,
        )

    own_share = pltpu.make_async_copy(shares.at[s], out_back.at[3], in_send.at[3])
    own_share.start()

    @pl.when(mine)
    def _():
        for i, to in enumerate((x, y, xy)):
            back_to(i, to).start()

    def came_one(which, chunk, l):
        one(which, chunk, l).wait_recv()

    def start_two(which, chunk):
        rows = rows_of(which, chunk)
        t = forwarded(which)
        if STREAMS[which][3]:
            came_one(which, chunk, 0)
            came_one(which, chunk, 1)
            got = ones[which][1 - half, rows, :]
        else:
            came_one(which, chunk, 0)
            came_one(which, chunk, 1)
            got = ones[which][1 - parity, rows, :]
        sums[which][t, rows, :] = plus(sums[which][t, rows, :], got).astype(BF)
        two(which, chunk).start()

    def start_z(which, chunk):
        rows = rows_of(which, chunk)
        two(which, chunk).wait_recv()
        got = ones[which][half if STREAMS[which][3] else parity, rows, :]
        total = plus(sums[which][s, rows, :], got, twos[which][rows, :])
        if layers == 1:
            sums[which][s, rows, :] = total.astype(BF)
            twin_copy(which, chunk, True).start()
            keep_copy(which, chunk, True).start()
            return
        if middle > 0:

            @pl.when(depth > 0)
            def _():
                inward(which, chunk, False).wait_recv()
                sums[which][s, rows, :] = plus(total, ins[which][rows, :]).astype(BF)

            @pl.when(depth == 0)
            def _():
                sums[which][s, rows, :] = total.astype(BF)

            @pl.when(depth < middle)
            def _():
                inward(which, chunk, False).start()

        else:
            sums[which][s, rows, :] = total.astype(BF)

        @pl.when(depth == middle)
        def _():
            inward(which, chunk, True).start()

    def finish(which, chunk):
        rows = rows_of(which, chunk)
        inward(which, chunk, True).wait_recv()

        @pl.when(depth == middle)
        def _():
            inward(which, chunk, True).wait_send()
            sums[which][s, rows, :] = plus(
                sums[which][s, rows, :], backs[which][rows, :]
            ).astype(BF)
            if middle > 0:
                outward_copy(which, chunk, True).start()
            twin_copy(which, chunk, True).start()
            keep_copy(which, chunk, True).start()

        if middle > 0:

            @pl.when(depth < middle)
            def _():
                @pl.when(depth > 0)
                def _():
                    outward_copy(which, chunk, False).start()

                twin_copy(which, chunk, False).start()
                keep_copy(which, chunk, False).start()

    lag3 = lag_z + lag_step * depth
    lag5 = lag_z + lag_step * (middle + 1) + lag_step * (middle - depth)
    slots = max(CHUNKS) + lag_z + (lag_step * (2 * middle + 1) if layers > 1 else 0)

    def guarded(chunk, step):
        for which, count in enumerate(CHUNKS):

            @pl.when((chunk >= 0) & (chunk < count))
            def _():
                step(which, chunk)

    def slot(k, unused):
        guarded(k, start_two)
        guarded(k - lag3, start_z)
        if layers > 1:
            guarded(k - lag5, finish)
        return unused

    lax.fori_loop(0, slots, slot, 0)

    def drain(which, chunk):
        twin_copy(which, chunk, True).wait_recv()
        twin_copy(which, chunk, True).wait_send()
        keep_copy(which, chunk, True).wait()
        if STREAMS[which][3]:
            one(which, chunk, 0).wait_send()
            one(which, chunk, 1).wait_send()
        else:
            one(which, chunk, 0).wait_send()
            one(which, chunk, 1).wait_send()
        two(which, chunk).wait_send()
        if layers > 1 and middle > 0:

            @pl.when(depth < middle)
            def _():
                inward(which, chunk, False).wait_send()

            @pl.when(depth > 0)
            def _():
                outward_copy(which, chunk, True).wait_send()

    def last(k, unused):
        guarded(k, drain)
        return unused

    lax.fori_loop(0, max(CHUNKS), last, 0)
    for i in range(3):
        swap_copy(0, i).wait_send()
    own_share.wait()

    @pl.when(mine)
    def _():
        for i, to in enumerate((x, y, xy)):
            back_to(i, to).wait_send()
        back_to(1, y).wait_recv()

    @pl.when(jnp.logical_not(mine))
    def _():
        back_to(0, x).wait_recv()
        back_to(2, xy).wait_recv()


def backward(hs, xhats, scales, kept, first_all, rest_all, tails, bound, vec, dw, width, layers, lags=(1, 1)):
    anywhere = pl.BlockSpec(memory_space=pl.ANY)
    inside = pl.BlockSpec(memory_space=pltpu.VMEM)
    shapes = [(rows, columns) for rows, columns, unused, unused2 in STREAMS]
    most = max(CHUNKS)
    return pl.pallas_call(
        partial(backward_kernel, layers, lags),
        in_specs=[anywhere] * 25
        + [pl.BlockSpec(memory_space=pltpu.SMEM), inside, inside],
        out_specs=[anywhere] * 4,
        out_shape=[jax.ShapeDtypeStruct((2,) + shape, BF) for shape in shapes]
        + [jax.ShapeDtypeStruct((4, ROWS, width), BF)],
        scratch_shapes=[pltpu.VMEM((4,) + shape, BF) for shape in shapes]
        + [pltpu.VMEM((2,) + shape, BF) for shape in shapes]
        + [pltpu.VMEM(shape, BF) for shape in shapes] * 3
        + [
            pltpu.VMEM((ROWS, D), BF),
            pltpu.VMEM((ROWS, D), BF),
            pltpu.VMEM((ROWS, 128), F32),
            pltpu.VMEM((ROWS, 2 * D), BF),
            pltpu.VMEM((D, FRONT), BF),
            pltpu.VMEM((HALF, D), BF),
            pltpu.VMEM((2, ROWS, HALF), BF),
            pltpu.VMEM((2, HALF, D), BF),
            pltpu.VMEM((ROWS, D), BF),
            pltpu.VMEM((ROWS, D), BF),
            pltpu.VMEM((ROWS, 128), F32),
            pltpu.VMEM((ROWS, FRONT), BF),
            pltpu.VMEM((ROWS, HALF), BF),
            pltpu.VMEM((PAIRS, 8, ROWS), F32),
            pltpu.VMEM((D, FRONT), BF),
            pltpu.VMEM((HALF, D), BF),
            pltpu.VMEM((4 * EXTRA, D), BF),
            pltpu.VMEM((ROWS, D), BF),
            pltpu.VMEM((ROWS, HALF), BF),
            pltpu.VMEM((ROWS, D), BF),
            pltpu.VMEM((2, ROWS, D), BF),
            pltpu.VMEM((4, ROWS, width), BF),
            pltpu.SemaphoreType.DMA((22,)),
            pltpu.SemaphoreType.DMA((2, 2)),
            pltpu.SemaphoreType.DMA((4, 3)),
            pltpu.SemaphoreType.DMA((4, 3)),
            pltpu.SemaphoreType.DMA((18, most)),
            pltpu.SemaphoreType.DMA((18, most)),
            pltpu.SemaphoreType.DMA((3, most)),
            pltpu.SemaphoreType.DMA((4,)),
            pltpu.SemaphoreType.DMA((4,)),
        ],
        compiler_params=pltpu.CompilerParams(
            collective_id=2, has_side_effects=True, vmem_limit_bytes=62 * 1024 * 1024
        ),
    )(*hs, *xhats, *scales, *kept, first_all, rest_all, tails, bound, vec, dw)


def assemble_kernel(first_ref, rest_ref, out_ref):
    is_ffn = lax.axis_index("section") % 2
    row = pl.program_id(0)

    @pl.when(is_ffn == 0)
    def _():
        for core in range(2):
            for i in range(PAIRS):
                for t in range(3):
                    to = t * D + core * HALF + i * 128
                    at = (3 * i + t) * 128
                    out_ref[:, to : to + 128] = first_ref[core, :, at : at + 128].astype(F32)
        from_core = row // 3
        at = pl.multiple_of((row % 3) * 128, 128)
        out_ref[:, 3 * D :] = rest_ref[from_core, pl.ds(at, 128), :].astype(F32)

    @pl.when(is_ffn == 1)
    def _():
        lanes = pl.ds(pl.multiple_of(row * 128, 128), 128)
        for core in range(2):
            out_ref[:, core * D : (core + 1) * D] = first_ref[core, :, 0:D].astype(F32)
            at = 2 * D + core * D
            out_ref[:, at : at + HALF] = first_ref[core, :, D:].astype(F32)
            out_ref[:, at + HALF : at + D] = rest_ref[core, 0:HALF, lanes].astype(F32).T


def assemble(first_sum, rest_sum):
    return pl.pallas_call(
        assemble_kernel,
        grid=(D // 128,),
        in_specs=[
            pl.BlockSpec((2, 128, FRONT), lambda i: (0, i, 0)),
            pl.BlockSpec((2, SIDE, D), lambda i: (0, 0, 0)),
        ],
        out_specs=pl.BlockSpec((128, 4 * D), lambda i: (i, 0)),
        out_shape=jax.ShapeDtypeStruct((D, 4 * D), F32),
        compiler_params=pltpu.CompilerParams(vmem_limit_bytes=32 * 1024 * 1024),
    )(first_sum, rest_sum)


def layer_norm(residual, gain, shift):
    row_mean = jnp.mean(residual, -1, keepdims=True)
    centered = residual - row_mean
    return (
        centered * lax.rsqrt(jnp.mean(centered * centered, -1, keepdims=True) + NORM_EPSILON) * gain
        + shift
    )


def normalize(projected):
    return projected * lax.rsqrt(jnp.sum(projected * projected, -1, keepdims=True) + NORM_EPSILON)


def gelu_and_slope(z):
    upper = 0.5 * (1.0 + lax.erf(z * 0.7071067811865476))
    density = jnp.exp(-0.5 * z * z) * 0.3989422804014327
    return (z * upper).astype(BF), (upper + z * density).astype(BF)


def maxsim_loss(affinity, valid, positive):
    logits = jnp.where(valid[None, :, :], affinity[:, None, :] / SOFTMAX_DIVISOR, MASKED)
    soft = SOFTMAX_DIVISOR * jax.nn.logsumexp(logits, -1)
    scores = jnp.sum(soft.reshape(QUERY_COUNT, QUERY_LENGTH, -1), 1) * SIMILARITY_SCALE
    choose = jnp.arange(scores.shape[1], dtype=jnp.int32)[None, :] == positive[:, None]
    picked = jnp.sum(jnp.where(choose, scores, 0.0), 1)
    return jnp.sum(jax.nn.logsumexp(scores, -1) - picked)


def on_device(
    inputs,
    in_weight,
    down_weight,
    out_bias,
    norm_gains,
    norm_shifts,
    projection,
    passage_lengths,
    positive,
):
    batches = lax.axis_size("batch")
    layers = batches // 2
    s = lax.axis_index("section")
    b = lax.axis_index("batch")
    core = b % 2
    groups = inputs.shape[0] * batches
    queries_all = groups * QUERY_COUNT

    def other_core(value):
        return lax.ppermute(value, "batch", [(j, j ^ 1) for j in range(batches)])

    def pick(table, index):
        return lax.dynamic_index_in_dim(table, index, 0, keepdims=False)

    mine = core == s % 2
    micro = s // 2
    lengths_all = passage_lengths[:, 0]

    def long_start(lengths):
        return jnp.where(
            lengths[0] == PLEN, 0, jnp.where(lengths[1] == PLEN, lengths[0], lengths[0] + lengths[1])
        )

    def rolled(rows, start):
        passages = rows[QROWS:]
        doubled = jnp.concatenate([passages, passages[:REST]], 0)
        return jnp.concatenate(
            [rows[:QROWS], lax.dynamic_slice_in_dim(doubled, start, PASSAGE_TOKENS, 0)], 0
        )

    def unrolled(rows, start):
        passages = rows[QROWS:]
        doubled = jnp.concatenate([passages[PLEN:], passages], 0)
        return jnp.concatenate(
            [rows[:QROWS], lax.dynamic_slice_in_dim(doubled, REST - start, PASSAGE_TOKENS, 0)], 0
        )

    slices = jnp.stack([rolled(inputs[m], long_start(lengths_all[m])) for m in range(2)])
    ints = jnp.pad(
        jnp.concatenate([lengths_all, positive], 1),
        ((0, 6), (0, 128 - PASSAGE_COUNT - QUERY_COUNT)),
    )
    vec = jnp.concatenate([out_bias, norm_gains, norm_shifts, jnp.zeros((5, D), F32)], 0)
    first_all, rest_all, vectors, parts_all, ints_other = fetch_weights(
        in_weight[0], down_weight, projection.T.astype(BF), vec, slices, ints, layers
    )
    packs = [
        (first_all[t], rest_all[t, :HALF], rest_all[t, HALF:FRONT]) for t in range(4)
    ]
    projector = jnp.concatenate([rest_all[t, FRONT:] for t in range(4)], 0).T
    entry = jnp.concatenate([parts_all[f] for f in range(4)], 1)
    ints = pick(jnp.where(mine, ints, ints_other), micro)
    lengths = ints[:PASSAGE_COUNT]
    chosen = ints[PASSAGE_COUNT : PASSAGE_COUNT + QUERY_COUNT]
    long_index = jnp.where(lengths[0] == PLEN, 0, jnp.where(lengths[1] == PLEN, 1, 2))
    after = (long_index + 1) % 3
    bound = pick(lengths, after)
    at = jnp.arange(PASSAGE_TOKENS, dtype=jnp.int32)
    owner = jnp.where(at < PLEN, long_index, jnp.where(at < PLEN + bound, after, (after + 1) % 3))
    valid = owner[None, :] == jnp.arange(PASSAGE_COUNT, dtype=jnp.int32)[:, None]
    bound = bound.reshape(1)

    def summed(part):
        own = part.astype(BF)
        return own.astype(F32) + other_core(own).astype(F32)

    h = entry
    hs, xhats, scales, kept = [], [], [], [[], [], [], [], []]
    for t in range(4):
        one, two, three = packs[t]
        bias, gain, shift = vectors[t, 0], vectors[t, 1], vectors[t, 2]
        if t % 2 == 0:
            qkv = mm(h, one).astype(BF)
            ctx, lse = attention(qkv, bound)
            branch = summed(mm(ctx, two))
            saved = (qkv, ctx, lse)
        else:
            down = jnp.concatenate([packs[t - 1][2], three], 0)
            z = jnp.concatenate([mm(h, one), mm(h, two, ((1,), (1,)))], 1)
            act, slope = gelu_and_slope(z)
            branch = summed(mm(act, down))
            saved = (None, None, None, act, slope)
        residual = h.astype(F32) + branch + bias
        centered = residual - jnp.mean(residual, -1, keepdims=True)
        scale = lax.rsqrt(jnp.mean(centered * centered, -1, keepdims=True) + NORM_EPSILON)
        xhat = centered * scale
        hs.append(h)
        xhats.append(xhat.astype(BF))
        scales.append(jnp.broadcast_to(scale, (ROWS, 128)))
        for i, value in enumerate(saved):
            if value is not None:
                kept[i].append(value)
        h = (xhat * gain + shift).astype(BF)

    projected = mm(h, projector)
    normed, norm_pull = jax.vjp(normalize, projected)
    embedded = normed.astype(BF)
    affinity = mm(embedded[:QROWS], embedded[QROWS:], ((1,), (1,)))
    loss, loss_pull = jax.vjp(partial(maxsim_loss, valid=valid, positive=chosen), affinity)
    left, steps = loss, []
    for unit in (8.0, 0.5, 2.0**-5, 2.0**-9, 2.0**-13, 2.0**-17):
        steps.append(jnp.floor(left / unit) * unit)
        left = left - steps[-1]
    loss_row = jnp.pad(jnp.stack(steps), (0, D - len(steps)))
    grad_sim = loss_pull(jnp.asarray(1.0 / queries_all, F32))[0].astype(BF)
    grad_embedded = jnp.concatenate(
        [mm(grad_sim, embedded[QROWS:]), mm(grad_sim, embedded[:QROWS], ((0,), (0,)))], 0
    )
    grad_projected = norm_pull(grad_embedded)[0].astype(BF)
    grad_projector = mm(h, grad_projected, ((0,), (0,)))

    columns = projection.shape[1]
    tails = jnp.stack(
        [
            jnp.concatenate(
                [
                    jnp.zeros((3, D), F32),
                    loss_row[None],
                    jnp.zeros((12, D), F32),
                    lax.slice_in_dim(grad_projector, t * columns, (t + 1) * columns, axis=1).T,
                ],
                0,
            )
            for t in range(4)
        ]
    ).astype(BF)
    first_sum, side_sum, down_sum, back = backward(
        hs,
        xhats,
        scales,
        sum(kept, []),
        first_all,
        rest_all,
        tails,
        bound,
        vectors,
        grad_projected,
        inputs.shape[2],
        layers,
    )
    in_grad = assemble(first_sum, side_sum)
    down_grad = down_sum.reshape(2 * D, D).astype(F32)
    extra = side_sum[0, HALF:].astype(F32)
    total_loss = jnp.sum(extra[3, :6]) / queries_all
    same_micro = jnp.where(mine, back[3], back[0])
    other_micro = jnp.where(mine, back[1], back[2])
    by_micro = [jnp.where(micro == m, same_micro, other_micro).astype(F32) for m in range(2)]
    input_grad = jnp.stack([unrolled(by_micro[m], long_start(lengths_all[m])) for m in range(2)])

    return (
        total_loss,
        input_grad,
        in_grad[None],
        down_grad,
        extra[0:1],
        extra[1:2],
        extra[2:3],
        extra[16:].T,
    )


def solution(mesh):
    in_specs = (
        P(None, "batch", "section"),
        P("section", None, None),
        P("section", None),
        P("section", None),
        P("section", None),
        P("section", None),
        P(None, "section"),
        P(None, "batch", None),
        P(None, "batch"),
    )
    out_specs = (
        P(),
        P(None, "batch", "section"),
        P("section", None, None),
        P("section", None),
        P("section", None),
        P("section", None),
        P("section", None),
        P(None, "section"),
    )
    return jax.shard_map(
        on_device, mesh=mesh, in_specs=in_specs, out_specs=out_specs, check_vma=False
    )
```

```python
from functools import partial

import jax
import jax.numpy as jnp
from jax import lax
from jax.experimental import pallas as pl
from jax.experimental.pallas import tpu as pltpu
from jax.sharding import PartitionSpec as P

D = 768
HEADS = 12
FF = 3072
DIM = 128
QUERY_LENGTH = 32
QUERY_COUNT = 4
PASSAGE_COUNT = 3
PASSAGE_TOKENS = 640
PLEN = 512
QROWS = QUERY_LENGTH * QUERY_COUNT
ROWS = QROWS + PASSAGE_TOKENS
REST = PASSAGE_TOKENS - PLEN
SOFTMAX_DIVISOR = 0.1
SIMILARITY_SCALE = 0.25
NORM_EPSILON = 1e-06
MASKED = -1000000000.0
BF = jnp.bfloat16
F32 = jnp.float32
BLOCKS = ((0, QROWS), (QROWS, PLEN), (QROWS + PLEN, REST))
PAIRS = HEADS // 4
HALF = D // 2


def mm(a, b, dims=((1,), (0,))):
    return lax.dot_general(a, b, (dims, ((), ())), preferred_element_type=F32)


def block_mask(which, bound, rows):
    t = lax.broadcasted_iota(jnp.int32, (rows, rows), 0)
    r = lax.broadcasted_iota(jnp.int32, (rows, rows), 1)
    if which == 0:
        return (t // QUERY_LENGTH) == (r // QUERY_LENGTH)
    return ((t.astype(F32) < bound).astype(F32) - (r.astype(F32) < bound).astype(F32)) == 0.0


MESH = pl.DeviceIdType.MESH
EXTRA = 32
FRONT = 1152


def neighbours():
    s, b = lax.axis_index("section"), lax.axis_index("batch")
    x = s + 1 - 2 * (s % 2)
    y = s + 2 - 4 * (s // 2)
    xy = 3 - s
    return s, b, x, y, xy


def greet(layers):
    s, b, x, y, xy = neighbours()
    z, core = b // 2, b % 2
    barrier = pltpu.get_barrier_semaphore()

    def signal(to):
        pl.semaphore_signal(barrier, inc=1, device_id=to, device_id_type=MESH)

    signal((x, b))
    signal((y, b))
    signal((xy, b))
    signal((s, b + 1 - 2 * core))
    if layers > 1:

        @pl.when(z > 0)
        def _():
            signal((s, b - 2))

        @pl.when(z < layers - 1)
        def _():
            signal((s, b + 2))

        ends = (layers - 1 - z) // (layers - 1) + z // (layers - 1)
        pl.semaphore_wait(barrier, 6 - ends)
    else:
        pl.semaphore_wait(barrier, 4)


def forward_kernel(layers, spread, queries_all, *refs):
    w_ref, down_ref, tail_ref, vec_ref, slices_ref, ints_ref = refs[0:6]
    first_out, rest_out, vec_out, h_out, xhat_out, scale_out, qkv_out, ctx_out = refs[6:14]
    lse_out, act_out, slope_out, dw_out, tails_out, bound_out = refs[14:20]
    (
        first_all,
        rest_all,
        vec_all,
        parts_all,
        ints_other,
        wide,
        out_stage,
        down_stage,
        hs,
        xhats,
        scales,
        qkvs,
        ctxs,
        lses,
        acts,
        slopes,
        part_out,
        part_in,
        proj,
        embedded,
        unit,
        length,
        grad_unit,
        grad_low,
        tails,
        load_sem,
        send_sem,
        recv_sem,
        z_send,
        z_recv,
        in_send,
        in_recv,
        part_send,
        part_recv,
        save_sem,
    ) = refs[20:]
    s, b, x, y, xy = neighbours()
    z, core = b // 2, b % 2
    micro = s // 2
    mine = core == s % 2
    twin = b + 1 - 2 * core

    def load(src, dst, i):
        return pltpu.make_async_copy(src, dst, load_sem.at[i])

    loads = [load(down_ref.at[pl.ds(core * D, D), :], down_stage, 0)]
    even, odd = [], []
    for i in range(PAIRS):
        for t in range(3):
            at = pl.multiple_of(t * D + core * HALF + i * 128, 128)
            to = (3 * i + t) * 128
            even.append(
                load(w_ref.at[:, pl.ds(at, 128)], wide.at[:, pl.ds(to, 128)], 1 + 3 * i + t)
            )
    even.append(load(w_ref.at[pl.ds(core * HALF, HALF), pl.ds(3 * D, D)], out_stage, 10))
    for i in range(2):
        at = pl.multiple_of(i * 2 * D + core * D, 128)
        odd.append(load(w_ref.at[:, pl.ds(at, D)], wide.at[:, pl.ds(i * D, D)], 11 + i))
    loads[0].start()

    @pl.when(s % 2 == 0)
    def _():
        for copy in even:
            copy.start()

    @pl.when(s % 2 == 1)
    def _():
        for copy in odd:
            copy.start()

    first, rest = first_all.at[s], rest_all.at[s]
    tail = pltpu.make_async_copy(
        tail_ref, rest.at[pl.ds(FRONT, EXTRA), :], load_sem.at[13]
    )
    own_vec = pltpu.make_async_copy(vec_ref, vec_all.at[s], load_sem.at[15])
    own_vec.start()
    tail.start()
    greet(layers)

    def feature_copy(i, which, section, to):
        return pltpu.make_async_remote_copy(
            src_ref=slices_ref.at[which],
            dst_ref=parts_all.at[section],
            send_sem=in_send.at[i],
            recv_sem=in_recv.at[i],
            device_id=(to, b),
            device_id_type=MESH,
        )

    def to_twin(i, src, dst):
        return pltpu.make_async_remote_copy(
            src_ref=src,
            dst_ref=dst,
            send_sem=in_send.at[i],
            recv_sem=in_recv.at[i],
            device_id=(s, twin),
            device_id_type=MESH,
        )

    def quarter_to_twin(i, f):
        return to_twin(i, parts_all.at[f], parts_all.at[f])

    swap_ints = to_twin(7, ints_ref, ints_other)
    own_quarter = pltpu.make_async_copy(slices_ref.at[micro], parts_all.at[s], load_sem.at[14])
    swap_ints.start()

    @pl.when(mine)
    def _():
        own_quarter.start()
        feature_copy(1, 1 - micro, s, y).start()

    @pl.when(jnp.logical_not(mine))
    def _():
        feature_copy(0, micro, s, x).start()
        feature_copy(2, 1 - micro, s, xy).start()

    loads[0].wait()

    @pl.loop(0, D // 96)
    def _(i):
        rows = pl.ds(pl.multiple_of(i * 96, 16), 96)
        to = pl.ds(pl.multiple_of(HALF + i * 96, 16), 96)
        rest[to, :] = down_stage[rows, :].astype(BF)

    @pl.when(s % 2 == 0)
    def _():
        for copy in even:
            copy.wait()

        @pl.loop(0, HALF // 96)
        def _(i):
            rows = pl.ds(pl.multiple_of(i * 96, 16), 96)
            rest[rows, :] = out_stage[rows, :].astype(BF)

    @pl.when(s % 2 == 1)
    def _():
        for copy in odd:
            copy.wait()
        for i in range(3):
            for j in range(6):
                block = wide[j * 128 : (j + 1) * 128, FRONT + i * 128 : FRONT + (i + 1) * 128]
                rest[i * 128 : (i + 1) * 128, j * 128 : (j + 1) * 128] = block.T.astype(BF)

    @pl.loop(0, D // 96)
    def _(i):
        rows = pl.ds(pl.multiple_of(i * 96, 16), 96)
        first[rows, :] = wide[rows, 0:FRONT].astype(BF)

    tail.wait()

    quarter = D // 4
    firsts = [(first, first_all, i * quarter, quarter, i < 2) for i in range(4)]
    seconds = [(rest, rest_all, i * 192, 192, i == 0) for i in range(2)]
    small = [
        (rest, rest_all, FRONT, EXTRA, True),
        (vec_ref, vec_all, 0, 8, False),
    ]
    if spread:
        share = D // layers
        at = pl.multiple_of(HALF + z * share, 16)
        half = share // 2
        slices = [
            (rest, rest_all, at, half, True),
            (rest, rest_all, pl.multiple_of(at + half, 16), share - half, False),
        ]
    else:
        slices = [(rest, rest_all, HALF + i * 192, 192, i < 2) for i in range(4)]
    pieces = slices + firsts + seconds + small

    def part(n, ref):
        unused, unused, row, rows, unused = pieces[n]
        return ref.at[pl.ds(row, rows), :]

    def remote(n, kind, src, dst, to):
        return pltpu.make_async_remote_copy(
            src_ref=src,
            dst_ref=dst,
            send_sem=send_sem.at[kind, n],
            recv_sem=recv_sem.at[kind, n],
            device_id=(to, b),
            device_id_type=MESH,
        )

    def direct(n, kind):
        mine, every = pieces[n][:2]
        return remote(n, kind, part(n, mine), part(n, every.at[s]), y if kind else x)

    def arrived(n, kind):
        every = pieces[n][1]
        owner = (x, y, xy)[kind]
        here = part(n, every.at[owner])
        remote(n, kind, here, here, x).wait_recv()

    def relay(n):
        every, by_x = pieces[n][1], pieces[n][4]
        source = part(n, every.at[x if by_x else y])
        return remote(n, 2, source, source, y if by_x else x)

    def pass_on(n):
        arrived(n, 0 if pieces[n][4] else 1)
        relay(n).start()

    count = len(pieces)
    by_x = [n for n in range(count) if pieces[n][4]]
    by_y = [n for n in range(count) if not pieces[n][4]]
    small_n = list(range(count - 2, count))

    def early(n):
        direct(n, 0 if pieces[n][4] else 1).start()

    def late(n):
        direct(n, 1 if pieces[n][4] else 0).start()

    z_width = D // layers if spread else 0

    def z_part(section, owner_z):
        at = pl.multiple_of(HALF + owner_z * z_width, 16)
        return rest_all.at[section, pl.ds(at, z_width), :]

    def z_copy(way, step, k, owner_z, to_b):
        source = z_part((x, y, xy)[k], owner_z)
        return pltpu.make_async_remote_copy(
            src_ref=source,
            dst_ref=source,
            send_sem=z_send.at[way, step, k],
            recv_sem=z_recv.at[way, step, k],
            device_id=(s, to_b),
            device_id_type=MESH,
        )

    def z_first(k):
        @pl.when(z < layers - 1)
        def _():
            z_copy(0, 0, k, z, b + 2).start()

        @pl.when(z > 0)
        def _():
            z_copy(1, 0, k, z, b - 2).start()

    def z_step(step):
        @pl.when(z >= step)
        def _():
            for k in range(3):
                z_copy(0, step - 1, k, z - step, b).wait_recv()

                @pl.when(z < layers - 1)
                def _():
                    z_copy(0, step, k, z - step, b + 2).start()

        @pl.when(z < layers - step)
        def _():
            for k in range(3):
                z_copy(1, step - 1, k, z + step, b).wait_recv()

                @pl.when(z > 0)
                def _():
                    z_copy(1, step, k, z + step, b - 2).start()

    def z_drain():
        for step in range(layers - 1):

            @pl.when((z < layers - 1) & (z >= step))
            def _():
                for k in range(3):
                    z_copy(0, step, k, z - step, b + 2).wait_send()

            @pl.when((z > 0) & (z + step < layers))
            def _():
                for k in range(3):
                    z_copy(1, step, k, z + step, b - 2).wait_send()

    queue_x = [n for n in by_x]
    queue_y = [n for n in by_y]
    for n in queue_x[:2] + queue_y[:2]:
        early(n)

    @pl.when(mine)
    def _():
        own_quarter.wait()
        quarter_to_twin(3, s).start()
        for i, owner in enumerate((x, y, xy)):
            feature_copy(i, 0, owner, x).wait_recv()
            quarter_to_twin(4 + i, owner).start()
    rounds = max(len(queue_x), len(queue_y))
    late_x, late_y = list(queue_y), list(queue_x)
    z_at = 1
    for i in range(rounds):
        for queue in (queue_x, queue_y):
            if i < len(queue):
                pass_on(queue[i])
                if i + 2 < len(queue):
                    early(queue[i + 2])
                else:
                    other = late_x if queue is queue_x else late_y
                    if other:
                        late(other.pop(0))
        if spread and i == 0:
            for n, kind in ((0, 1), (1, 0)):
                late(n)
                (late_x if kind == 0 else late_y).remove(n)
        if spread and i == 1:
            arrived(0, 1)
            arrived(1, 0)
            z_first(0)
            z_first(1)
            arrived(0, 2)
            arrived(1, 2)
            z_first(2)
        if spread and i >= 2 and z_at < layers - 1:
            z_step(z_at)
            z_at += 1
    for n in late_x + late_y:
        late(n)
    done = set()
    if spread:
        done = {(0, 1), (1, 0), (0, 2), (1, 2)}
        while z_at < layers - 1:
            z_step(z_at)
            z_at += 1
    for n in range(count):
        for kind in range(3):
            if kind == 2 or kind == (1 if pieces[n][4] else 0):
                if (n, kind) not in done:
                    arrived(n, kind)
    swap_ints.wait()
    own_vec.wait()

    @pl.when(jnp.logical_not(mine))
    def _():
        for i, owner in enumerate((s, x, y, xy)):
            quarter_to_twin(3 + i, owner).wait_recv()

    row = jnp.where(
        mine, ints_ref[pl.ds(micro, 1), :].astype(F32), ints_other[pl.ds(micro, 1), :].astype(F32)
    )
    lane = lax.broadcasted_iota(jnp.int32, (1, 128), 1)

    def entry(i):
        return jnp.sum(jnp.where(lane == i, row, 0.0), axis=1, keepdims=True)

    sizes = [entry(i) for i in range(PASSAGE_COUNT)]
    is_long = [
        (sizes[0] == float(PLEN)).astype(F32),
        (sizes[1] == float(PLEN)).astype(F32),
        (sizes[2] == float(PLEN)).astype(F32),
    ]
    bound = is_long[0] * sizes[1] + is_long[1] * sizes[2] + is_long[2] * sizes[0]
    long_index = is_long[1] + 2.0 * is_long[2]

    saves = []

    def save(src, dst):
        copy = pltpu.make_async_copy(src, dst, save_sem.at[len(saves)])
        copy.start()
        saves.append(copy)

    save(vec_all, vec_out)
    save(first_all, first_out)

    def swap_copy(t, i):
        rows = pl.ds(i * 256, 256)
        return pltpu.make_async_remote_copy(
            src_ref=part_out.at[rows, :],
            dst_ref=part_in.at[t % 2, rows, :],
            send_sem=part_send.at[t, i],
            recv_sem=part_recv.at[t, i],
            device_id=(s, twin),
            device_id_type=MESH,
        )

    for i in range(6):
        rows = slice(i * 128, (i + 1) * 128)
        hs[0, rows, :] = jnp.concatenate([parts_all[f, rows, :] for f in range(4)], axis=1)
    save(hs.at[0], h_out.at[0])

    def norm_rows(t, i):
        bias, gain, shift = vec_all[t, 0:1, :], vec_all[t, 1:2, :], vec_all[t, 2:3, :]
        swap_copy(t, i).wait_recv()

        def body(j, unused):
            rows = pl.ds(pl.multiple_of(j * 128, 128), 128)
            u = (
                hs[t, rows, :].astype(F32)
                + part_out[rows, :].astype(F32)
                + part_in[t % 2, rows, :].astype(F32)
                + bias
            )
            centered = u - jnp.mean(u, -1, keepdims=True)
            scale = lax.rsqrt(jnp.mean(centered * centered, -1, keepdims=True) + NORM_EPSILON)
            xhat = centered * scale
            xhats[t, rows, :] = xhat.astype(BF)
            scales[t, rows, :] = jnp.broadcast_to(scale, (128, 128))
            hs[t + 1, rows, :] = (xhat * gain + shift).astype(BF)
            return unused

        lax.fori_loop(2 * i, 2 * i + 2, body, 0)

    def save_norm(t):
        save(xhats.at[t], xhat_out.at[t])
        save(scales.at[t], scale_out.at[t])
        if t < 3:
            save(hs.at[t + 1], h_out.at[t + 1])

    def attention_pair(l):
        def pair(i, unused):
            base = pl.multiple_of(i * 384, 128)
            q_at = pl.ds(base, 128)
            k_at = pl.ds(pl.multiple_of(base + 128, 128), 128)
            v_at = pl.ds(pl.multiple_of(base + 256, 128), 128)
            c_at = pl.ds(pl.multiple_of(i * 128, 128), 128)
            for which, (begin, size) in enumerate(BLOCKS):
                chunk = min(size, 256)
                span = slice(begin, begin + size)
                k = qkvs[l, span, k_at]
                v = qkvs[l, span, v_at]
                for at in range(begin, begin + size, chunk):
                    rows = slice(at, at + chunk)
                    q = qkvs[l, rows, q_at]
                    total = None
                    for head in range(2):
                        own = (lane < 64) if head == 0 else (lane >= 64)
                        qm = jnp.where(own, q, jnp.zeros_like(q)) * BF(0.125)
                        vm = jnp.where(own, v, jnp.zeros_like(v))
                        score = mm(k, qm, ((1,), (1,)))
                        if which != 1:
                            score = jnp.where(block_mask(which, bound, size), score, MASKED)
                        top = jnp.max(score, axis=0, keepdims=True)
                        e = jnp.exp(score - top)
                        weight = jnp.sum(e, axis=0, keepdims=True)
                        part = mm(vm, e.astype(BF), ((0,), (0,))) * (1.0 / weight)
                        total = part if total is None else total + part
                        lses[l, i, head : head + 1, rows] = top + jnp.log(weight)
                    ctxs[l, rows, c_at] = total.T.astype(BF)
            return unused

        lax.fori_loop(0, PAIRS, pair, 0)

    def attention_layer(l):
        t = 2 * l
        for i in range(3):
            rows = slice(i * 256, (i + 1) * 256)
            if t > 0:
                norm_rows(t - 1, i)
            qkvs[l, rows, :] = mm(hs[t, rows, :], first_all[t]).astype(BF)
        if t > 0:
            save_norm(t - 1)
        save(qkvs.at[l], qkv_out.at[l])
        attention_pair(l)
        save(ctxs.at[l], ctx_out.at[l])
        save(lses.at[l], lse_out.at[l])
        for i in range(3):
            rows = slice(i * 256, (i + 1) * 256)
            if t > 0:
                swap_copy(t - 1, i).wait_send()
            part_out[rows, :] = mm(ctxs[l, rows, :], rest_all[t, 0:HALF, :]).astype(BF)
            swap_copy(t, i).start()

    def ffn_layer(l):
        t = 2 * l + 1
        for i in range(3):
            rows = slice(i * 256, (i + 1) * 256)
            norm_rows(t - 1, i)
            x_rows = hs[t, rows, :]
            for j in range(4):
                columns = slice(j * HALF, (j + 1) * HALF)
                if j < 3:
                    value = mm(x_rows, first_all[t, :, columns])
                else:
                    value = mm(x_rows, rest_all[t, 0:HALF, :], ((1,), (1,)))
                act, slope = gelu_and_slope(value)
                acts[l, rows, columns] = act
                slopes[l, rows, columns] = slope
            swap_copy(t - 1, i).wait_send()
            part = mm(acts[l, rows, 0:D], rest_all[2 * l, HALF:FRONT, :])
            part = part + mm(acts[l, rows, D:], rest_all[2 * l + 1, HALF:FRONT, :])
            part_out[rows, :] = part.astype(BF)
            swap_copy(t, i).start()
        save_norm(t - 1)
        save(acts.at[l], act_out.at[l])
        save(slopes.at[l], slope_out.at[l])

    attention_layer(0)
    if spread:
        while z_at < layers:
            z_step(z_at)
            z_at += 1
    save(rest_all, rest_out)
    ffn_layer(0)
    attention_layer(1)
    ffn_layer(1)

    for t in range(4):
        proj[t * EXTRA : (t + 1) * EXTRA, :] = rest_all[t, FRONT : FRONT + EXTRA, :]
    for i in range(3):
        rows = slice(i * 256, (i + 1) * 256)
        norm_rows(3, i)
        w = mm(hs[4, rows, :], proj[...], ((1,), (1,)))
        r = lax.rsqrt(jnp.sum(w * w, -1, keepdims=True) + NORM_EPSILON)
        unit[rows, :] = w * r
        length[rows, :] = jnp.broadcast_to(r, (256, 128))
        embedded[rows, :] = (w * r).astype(BF)
    save_norm(3)
    queries, passages = embedded[0:QROWS, :], embedded[QROWS:, :]
    logits = mm(queries, passages, ((1,), (1,))) * (1.0 / SOFTMAX_DIVISOR)
    column = lax.broadcasted_iota(jnp.int32, (1, REST), 1).astype(F32)
    token = lax.broadcasted_iota(jnp.int32, (QROWS, 1), 0)
    before = column < bound
    softs, shares = [], []
    for p in range(3):
        if p == 0:
            score = logits[:, 0:PLEN]
            top = jnp.max(score, -1, keepdims=True)
            e = jnp.exp(score - top)
        else:
            score = logits[:, PLEN:]
            inside = before if p == 1 else jnp.logical_not(before)
            score = jnp.where(inside, score, MASKED)
            top = jnp.max(score, -1, keepdims=True)
            e = jnp.where(inside, jnp.exp(score - top), 0.0)
        weight = jnp.sum(e, -1, keepdims=True)
        softs.append(SOFTMAX_DIVISOR * (top + jnp.log(weight)))
        shares.append(e * (1.0 / weight))
    loss = jnp.zeros((1, 1), F32)
    grad_softs = [jnp.zeros((QROWS, 1), F32) for p in range(3)]
    for q in range(QUERY_COUNT):
        mine_rows = (token // QUERY_LENGTH) == q
        scores = [
            SIMILARITY_SCALE * jnp.sum(jnp.where(mine_rows, soft, 0.0), 0, keepdims=True)
            for soft in softs
        ]
        top = jnp.maximum(jnp.maximum(scores[0], scores[1]), scores[2])
        es = [jnp.exp(score - top) for score in scores]
        weight = es[0] + es[1] + es[2]
        wanted = entry(PASSAGE_COUNT + q) - long_index
        wanted = jnp.where(wanted < 0.0, wanted + 3.0, wanted)
        chosen = [(wanted == float(p)).astype(F32) for p in range(3)]
        picked = chosen[0] * scores[0] + chosen[1] * scores[1] + chosen[2] * scores[2]
        loss = loss + top + jnp.log(weight) - picked
        for p in range(3):
            grad = (es[p] / weight - chosen[p]) * (SIMILARITY_SCALE / queries_all)
            grad_softs[p] = jnp.where(mine_rows, grad, grad_softs[p])
    grad_logits = jnp.concatenate(
        [grad_softs[0] * shares[0], grad_softs[1] * shares[1] + grad_softs[2] * shares[2]], axis=1
    ).astype(BF)
    grad_unit[0:QROWS, :] = mm(grad_logits, passages)
    grad_unit[QROWS:, :] = mm(grad_logits, queries, ((0,), (0,)))
    for i in range(3):
        rows = slice(i * 256, (i + 1) * 256)
        n, dn = unit[rows, :], grad_unit[rows, :]
        inner = jnp.sum(n * dn, -1, keepdims=True)
        grad_low[rows, :] = (length[rows, :] * (dn - n * inner)).astype(BF)
    save(grad_low, dw_out)
    grad_proj = mm(grad_low[...], hs[4], ((0,), (0,)))
    feature = lax.broadcasted_iota(jnp.int32, (16, D), 1)
    line = lax.broadcasted_iota(jnp.int32, (16, D), 0)
    head_rows = jnp.zeros((16, D), F32)
    left = loss
    for i, step in enumerate((8.0, 0.5, 2.0**-5, 2.0**-9, 2.0**-13, 2.0**-17)):
        value = jnp.floor(left * (1.0 / step)) * step
        left = left - value
        head_rows = jnp.where((line == 3) & (feature == i), value, head_rows)
    for t in range(4):
        tails[t, 0:16, :] = head_rows.astype(BF)
        tails[t, 16:TAIL, :] = grad_proj[t * EXTRA : (t + 1) * EXTRA, :].astype(BF)
    save(tails, tails_out)
    unit[0:8, :] = jnp.broadcast_to(bound, (8, 128))
    save(unit.at[pl.ds(0, 8), :], bound_out)

    for copy in saves:
        copy.wait()
    for i in range(3):
        swap_copy(3, i).wait_send()
    for n in range(count):
        direct(n, 0).wait_send()
        direct(n, 1).wait_send()
        relay(n).wait_send()
    if spread:
        z_drain()

    @pl.when(mine)
    def _():
        feature_copy(1, 1 - micro, s, y).wait_send()
        for i, owner in enumerate((s, x, y, xy)):
            quarter_to_twin(3 + i, owner).wait_send()

    @pl.when(jnp.logical_not(mine))
    def _():
        feature_copy(0, micro, s, x).wait_send()
        feature_copy(2, 1 - micro, s, xy).wait_send()


def forward(w, down, tail, vec, slices, ints, layers, queries_all):
    spread = layers > 1 and D % (32 * layers) == 0
    anywhere = pl.BlockSpec(memory_space=pl.ANY)
    inside = pl.BlockSpec(memory_space=pltpu.VMEM)
    pieces = 12 if not spread else 10
    steps = max(layers - 1, 1) if spread else 1
    kept = [
        ((4, D, FRONT), BF),
        ((4, FRONT + EXTRA, D), BF),
        ((4, 8, D), F32),
        ((4, ROWS, D), BF),
        ((4, ROWS, D), BF),
        ((4, ROWS, 128), F32),
        ((2, ROWS, FRONT), BF),
        ((2, ROWS, HALF), BF),
        ((2, PAIRS, 8, ROWS), F32),
        ((2, ROWS, 2 * D), BF),
        ((2, ROWS, 2 * D), BF),
        ((ROWS, DIM), BF),
        ((4, TAIL, D), BF),
        ((8, 128), F32),
    ]
    return pl.pallas_call(
        partial(forward_kernel, layers, spread, queries_all),
        in_specs=[anywhere] * 3 + [inside, anywhere, inside],
        out_specs=[anywhere] * len(kept),
        out_shape=[jax.ShapeDtypeStruct(shape, kind) for shape, kind in kept],
        scratch_shapes=[
            pltpu.VMEM((4, D, FRONT), BF),
            pltpu.VMEM((4, FRONT + EXTRA, D), BF),
            pltpu.VMEM((4, 8, D), F32),
            pltpu.VMEM((4,) + slices.shape[1:], BF),
            pltpu.VMEM(ints.shape, jnp.int32),
            pltpu.VMEM((D, 2 * D), F32),
            pltpu.VMEM((HALF, D), F32),
            pltpu.VMEM((D, D), F32),
            pltpu.VMEM((5, ROWS, D), BF),
            pltpu.VMEM((4, ROWS, D), BF),
            pltpu.VMEM((4, ROWS, 128), F32),
            pltpu.VMEM((2, ROWS, FRONT), BF),
            pltpu.VMEM((2, ROWS, HALF), BF),
            pltpu.VMEM((2, PAIRS, 8, ROWS), F32),
            pltpu.VMEM((2, ROWS, 2 * D), BF),
            pltpu.VMEM((2, ROWS, 2 * D), BF),
            pltpu.VMEM((ROWS, D), BF),
            pltpu.VMEM((2, ROWS, D), BF),
            pltpu.VMEM((DIM, D), BF),
            pltpu.VMEM((ROWS, DIM), BF),
            pltpu.VMEM((ROWS, DIM), F32),
            pltpu.VMEM((ROWS, DIM), F32),
            pltpu.VMEM((ROWS, DIM), F32),
            pltpu.VMEM((ROWS, DIM), BF),
            pltpu.VMEM((4, TAIL, D), BF),
            pltpu.SemaphoreType.DMA((16,)),
            pltpu.SemaphoreType.DMA((3, pieces)),
            pltpu.SemaphoreType.DMA((3, pieces)),
            pltpu.SemaphoreType.DMA((2, steps, 3)),
            pltpu.SemaphoreType.DMA((2, steps, 3)),
            pltpu.SemaphoreType.DMA((8,)),
            pltpu.SemaphoreType.DMA((8,)),
            pltpu.SemaphoreType.DMA((4, 3)),
            pltpu.SemaphoreType.DMA((4, 3)),
            pltpu.SemaphoreType.DMA((32,)),
        ],
        compiler_params=pltpu.CompilerParams(
            collective_id=1, has_side_effects=True, vmem_limit_bytes=62 * 1024 * 1024
        ),
    )(w, down, tail, vec, slices, ints)


TAIL = 48
SIDE = HALF + TAIL
STREAMS = ((D, FRONT, 64, True), (SIDE, D, 48, False), (D, D, 64, True))
CHUNKS = tuple(rows // step for rows, unused, step, unused2 in STREAMS)
OFFSETS = (CHUNKS[2], CHUNKS[2] + CHUNKS[0], 0)
ONE_LOW, ONE_HIGH, TWO, INWARD, BACK, TWIN = 0, 3, 6, 9, 12, 15


def backward_kernel(layers, lags, *refs):
    first_all, rest_all, hs, xhats, scales, qkvs, ctxs, lses, acts, slopes, tails = refs[0:11]
    bound_ref, vec_ref, dw_ref = refs[11:14]
    outs, out_back = refs[14:17], refs[17]
    sums, ones, twos, ins, backs = refs[18:21], refs[21:24], refs[24:27], refs[27:30], refs[30:33]
    (
        h_f,
        xhat_f,
        scale_f,
        slope,
        up_first,
        up_second,
        act_ring,
        down_ring,
        h_a,
        xhat_a,
        scale_a,
        qkv,
        ctx,
        lse,
        att_first,
        att_second,
        proj,
        dy,
        dc,
        part_out,
        part_in,
        shares,
        load_sem,
        ring_sem,
        part_send,
        part_recv,
        send_sem,
        recv_sem,
        keep_sem,
        in_send,
        in_recv,
    ) = refs[33:]
    s, b, x, y, xy = neighbours()
    z, core = b // 2, b % 2
    half = s // 2
    parity = s % 2
    mine = core == parity
    twin = b + 1 - 2 * core
    middle = max(layers // 2 - 1, 0)
    upper = z // max(layers // 2, 1)
    depth = z + upper * (layers - 1 - 2 * z)
    toward = b + 2 - 4 * upper
    outward = b - 2 + 4 * upper
    lag_z, lag_step = lags

    def load(src, dst, i):
        return pltpu.make_async_copy(src, dst, load_sem.at[i])

    def loads_ffn(l):
        t = 2 * l + 1
        return [
            load(hs.at[t], h_f, 0),
            load(xhats.at[t], xhat_f, 1),
            load(scales.at[t], scale_f, 2),
            load(slopes.at[l], slope, 3),
            load(first_all.at[t], up_first, 4),
            load(rest_all.at[t, pl.ds(0, HALF), :], up_second, 5),
        ]

    def loads_attention(l):
        t = 2 * l
        return [
            load(hs.at[t], h_a, 6),
            load(xhats.at[t], xhat_a, 7),
            load(scales.at[t], scale_a, 8),
            load(qkvs.at[l], qkv, 9),
            load(ctxs.at[l], ctx, 10),
            load(lses.at[l], lse, 11),
            load(first_all.at[t], att_first, 12),
            load(rest_all.at[t, pl.ds(0, HALF), :], att_second, 13),
        ]

    def ring(l, j):
        slot = j % 2
        rows = pl.ds(HALF + (j % 2) * HALF, HALF)
        return (
            pltpu.make_async_copy(
                acts.at[l, :, pl.ds(j * HALF, HALF)], act_ring.at[slot], ring_sem.at[0, slot]
            ),
            pltpu.make_async_copy(
                rest_all.at[2 * l + j // 2, rows, :], down_ring.at[slot], ring_sem.at[1, slot]
            ),
        )

    def start(copies):
        for copy in copies:
            copy.start()

    def wait(copies):
        for copy in copies:
            copy.wait()

    start_loads = [
        load(rest_all.at[t, pl.ds(FRONT, EXTRA), :], proj.at[pl.ds(t * EXTRA, EXTRA), :], 14 + t)
        for t in range(4)
    ] + [load(tails.at[t], sums[1].at[t, pl.ds(HALF, TAIL), :], 18 + t) for t in range(4)]
    start(start_loads)
    start(loads_ffn(1))
    start(ring(1, 0))
    start(ring(1, 1))
    start(loads_attention(1))
    greet(layers)
    wait(start_loads)

    def remote(kind, chunk, src, dst, to):
        return pltpu.make_async_remote_copy(
            src_ref=src,
            dst_ref=dst,
            send_sem=send_sem.at[kind, chunk],
            recv_sem=recv_sem.at[kind, chunk],
            device_id=to,
            device_id_type=MESH,
        )

    def rows_of(which, chunk):
        size = STREAMS[which][2]
        return pl.ds(pl.multiple_of(chunk * size, 16), size)

    def one(which, chunk, l):
        rows = rows_of(which, chunk)
        kind = (ONE_HIGH if l else ONE_LOW) + which
        if STREAMS[which][3]:
            src = sums[which].at[2 * l + 1 - parity, rows, :]
            return remote(kind, chunk, src, ones[which].at[l, rows, :], (x, b))
        src = sums[which].at[2 * (1 - half) + l, rows, :]
        return remote(kind, chunk, src, ones[which].at[l, rows, :], (y, b))

    def forwarded(which):
        return 2 * (1 - half) + parity if STREAMS[which][3] else 2 * half + 1 - parity

    def two(which, chunk):
        rows = rows_of(which, chunk)
        src = sums[which].at[forwarded(which), rows, :]
        to = y if STREAMS[which][3] else x
        return remote(TWO + which, chunk, src, twos[which].at[rows, :], (to, b))

    def inward(which, chunk, swap):
        rows = rows_of(which, chunk)
        src = sums[which].at[s, rows, :]
        if swap:
            return remote(BACK + which, chunk, src, backs[which].at[rows, :], (s, toward))
        return remote(INWARD + which, chunk, src, ins[which].at[rows, :], (s, toward))

    def final(which, at_middle):
        return sums[which].at[s] if at_middle else backs[which]

    def outward_copy(which, chunk, at_middle):
        rows = rows_of(which, chunk)
        src = final(which, at_middle).at[rows, :]
        return remote(BACK + which, chunk, src, backs[which].at[rows, :], (s, outward))

    def twin_copy(which, chunk, at_middle):
        rows = rows_of(which, chunk)
        src = final(which, at_middle).at[rows, :]
        return remote(TWIN + which, chunk, src, outs[which].at[core, rows, :], (s, twin))

    def keep_copy(which, chunk, at_middle):
        rows = rows_of(which, chunk)
        src = final(which, at_middle).at[rows, :]
        return pltpu.make_async_copy(
            src, outs[which].at[core, rows, :], keep_sem.at[which, chunk]
        )

    def plus(*values):
        total = values[0].astype(F32)
        for value in values[1:]:
            total = total + value.astype(F32)
        return total

    def send_block(which, t, start_row, rows):
        size = STREAMS[which][2]
        by_x = STREAMS[which][3]

        @pl.when(parity != t % 2 if by_x else half != t // 2)
        def _():
            def body(c, unused):
                one(which, c, t // 2 if by_x else t % 2).start()
                return unused

            lax.fori_loop(start_row // size, (start_row + rows) // size, body, 0)

    def swap_copy(t, i):
        rows = pl.ds(i * 256, 256)
        return pltpu.make_async_remote_copy(
            src_ref=part_out.at[rows, :],
            dst_ref=part_in.at[t % 2, rows, :],
            send_sem=part_send.at[t, i],
            recv_sem=part_recv.at[t, i],
            device_id=(s, twin),
            device_id_type=MESH,
        )

    def norm_back(t, grad_of, xhat, scale):
        gain = vec_ref[t, 1:2, :]

        def body(i, carry):
            rows = pl.ds(pl.multiple_of(i * 128, 128), 128)
            grad = grad_of(rows)
            xh = xhat[rows, :].astype(F32)
            weighted = grad * gain
            mean_1 = jnp.mean(weighted, -1, keepdims=True)
            mean_2 = jnp.mean(weighted * xh, -1, keepdims=True)
            du = scale[rows, 0:1] * (weighted - mean_1 - xh * mean_2)
            dy[rows, :] = du.astype(BF)
            return (
                carry[0] + jnp.sum(du, 0, keepdims=True),
                carry[1] + jnp.sum(grad * xh, 0, keepdims=True),
                carry[2] + jnp.sum(grad, 0, keepdims=True),
            )

        zero = jnp.zeros((1, D), F32)
        carry = (zero, zero, zero)
        for i in range(3):
            if t < 3:
                swap_copy(t + 1, i).wait_recv()
            carry = lax.fori_loop(2 * i, 2 * i + 2, body, carry)
        row = lax.broadcasted_iota(jnp.int32, (16, 1), 0)
        block = sums[1][t, HALF : HALF + 16, :].astype(F32)
        for i in range(3):
            block = jnp.where(row == i, carry[i], block)
        sums[1][t, HALF : HALF + 16, :] = block.astype(BF)

    def grad_from_head(rows):
        return mm(dw_ref[rows, :], proj[...])

    def grad_from(t):
        def grad_of(rows):
            total = plus(dy[rows, :], part_out[rows, :], part_in[t % 2, rows, :])
            return total.astype(BF).astype(F32)

        return grad_of

    def ffn_back(l):
        t = 2 * l + 1
        for j in range(4):
            wait(ring(l, j))
            slot = j % 2
            columns = slice(j * HALF, (j + 1) * HALF)
            low = dy[...]
            to = (j % 2) * HALF
            sums[2][2 * l + j // 2, to : to + HALF, :] = mm(
                act_ring[slot], low, ((0,), (0,))
            ).astype(BF)
            send_block(2, 2 * l + j // 2, to, HALF)
            for i in range(3):
                rows = slice(i * 256, (i + 1) * 256)
                grad = mm(dy[rows, :], down_ring[slot], ((1,), (1,)))
                slope[rows, columns] = (grad * slope[rows, columns].astype(F32)).astype(BF)
            if j < 2:
                start(ring(l, j + 2))
        for i in range(3):
            rows = slice(i * 256, (i + 1) * 256)
            if t < 3:
                swap_copy(t + 1, i).wait_send()
            part = mm(slope[rows, 0:FRONT], up_first[...], ((1,), (1,)))
            part = part + mm(slope[rows, FRONT:], up_second[...])
            part_out[rows, :] = part.astype(BF)
            swap_copy(t, i).start()
        for i in range(3):
            rows = slice(i * 256, (i + 1) * 256)
            sums[0][t, rows, :] = mm(h_f[:, rows], slope[:, 0:FRONT], ((0,), (0,))).astype(BF)
        sums[1][t, 0:HALF, :] = mm(slope[:, FRONT:], h_f[...], ((0,), (0,))).astype(BF)

    def attention_pair(i, unused):
        lane = lax.broadcasted_iota(jnp.int32, (1, 128), 1)
        base = pl.multiple_of(i * 384, 128)
        q_at, k_at, v_at = (
            pl.ds(base, 128),
            pl.ds(pl.multiple_of(base + 128, 128), 128),
            pl.ds(pl.multiple_of(base + 256, 128), 128),
        )
        c_at = pl.ds(pl.multiple_of(i * 128, 128), 128)
        for which, (begin, size) in enumerate(BLOCKS):
            chunk = min(size, 256)
            span = slice(begin, begin + size)
            k = qkv[span, k_at]
            v = qkv[span, v_at]
            dk = jnp.zeros((size, 128), F32)
            dv = jnp.zeros((size, 128), F32)
            for at in range(begin, begin + size, chunk):
                rows = slice(at, at + chunk)
                q = qkv[rows, q_at]
                dcs = dc[rows, c_at]
                dq = None
                for head in range(2):
                    own = (lane < 64) if head == 0 else (lane >= 64)
                    qm = jnp.where(own, q, jnp.zeros_like(q)) * BF(0.125)
                    dcm = jnp.where(own, dcs, jnp.zeros_like(dcs))
                    km = jnp.where(own, k, jnp.zeros_like(k))
                    score = mm(k, qm, ((1,), (1,)))
                    if which != 1:
                        score = jnp.where(block_mask(which, bound_ref[0:1, 0:1], size), score, MASKED)
                    p = jnp.exp(score - lse[i, head : head + 1, rows])
                    dp = mm(v, dcm, ((1,), (1,)))
                    inner = jnp.sum(p * dp, axis=0, keepdims=True)
                    ds = (p * (dp - inner)).astype(BF)
                    dv = dv + mm(p.astype(BF), dcm)
                    dk = dk + mm(ds, qm)
                    part = mm(km, ds, ((0,), (0,)))
                    dq = part if dq is None else dq + part
                qkv[rows, q_at] = (dq.T * 0.125).astype(BF)
            qkv[span, k_at] = dk.astype(BF)
            qkv[span, v_at] = dv.astype(BF)
        return unused

    def attention_grads(l):
        t = 2 * l
        sums[1][t, 0:HALF, :] = mm(ctx[...], dy[...], ((0,), (0,))).astype(BF)
        for i in range(3):
            rows = slice(i * 256, (i + 1) * 256)
            dc[rows, :] = mm(dy[rows, :], att_second[...], ((1,), (1,))).astype(BF)
        lax.fori_loop(0, PAIRS, attention_pair, 0)
        for i in range(3):
            rows = slice(i * 256, (i + 1) * 256)
            swap_copy(t + 1, i).wait_send()
            part_out[rows, :] = mm(qkv[rows, :], att_first[...], ((1,), (1,))).astype(BF)
            swap_copy(t, i).start()
        for i in range(3):
            rows = slice(i * 256, (i + 1) * 256)
            sums[0][t, rows, :] = mm(h_a[:, rows], qkv[...], ((0,), (0,))).astype(BF)

    def send_sections(t):
        for which in (1, 0):
            send_block(which, t, 0, STREAMS[which][0])

    def came_one(which, chunk, l):
        one(which, chunk, l).wait_recv()

    def start_two(which, chunk):
        rows = rows_of(which, chunk)
        t = forwarded(which)
        if STREAMS[which][3]:
            came_one(which, chunk, 0)
            came_one(which, chunk, 1)
            got = ones[which][1 - half, rows, :]
        else:
            came_one(which, chunk, 0)
            came_one(which, chunk, 1)
            got = ones[which][1 - parity, rows, :]
        sums[which][t, rows, :] = plus(sums[which][t, rows, :], got).astype(BF)
        two(which, chunk).start()

    wait(loads_ffn(1))
    norm_back(3, grad_from_head, xhat_f, scale_f)
    ffn_back(1)
    send_sections(3)
    start(loads_ffn(0))
    start(ring(0, 0))
    start(ring(0, 1))
    wait(loads_attention(1))
    norm_back(2, grad_from(3), xhat_a, scale_a)
    attention_grads(1)
    send_sections(2)
    start(loads_attention(0))
    wait(loads_ffn(0))
    norm_back(1, grad_from(2), xhat_f, scale_f)
    ffn_back(0)
    send_sections(1)
    wait(loads_attention(0))
    norm_back(0, grad_from(1), xhat_a, scale_a)

    attention_grads(0)
    send_sections(0)

    width = shares.shape[2]
    for i in range(3):
        swap_copy(0, i).wait_recv()

        def body(j, unused):
            rows = pl.ds(pl.multiple_of(j * 64, 64), 64)
            total = plus(dy[rows, :], part_out[rows, :], part_in[0, rows, :])
            for f in range(4):
                shares[f, rows, :] = total[:, f * width : (f + 1) * width].astype(BF)
            return unused

        lax.fori_loop(4 * i, 4 * i + 4, body, 0)

    def back_to(i, to):
        return pltpu.make_async_remote_copy(
            src_ref=shares.at[to],
            dst_ref=out_back.at[i],
            send_sem=in_send.at[i],
            recv_sem=in_recv.at[i],
            device_id=(to, b),
            device_id_type=MESH,
        )

    own_share = pltpu.make_async_copy(shares.at[s], out_back.at[3], in_send.at[3])
    own_share.start()

    @pl.when(mine)
    def _():
        for i, to in enumerate((x, y, xy)):
            back_to(i, to).start()

    def start_z(which, chunk):
        rows = rows_of(which, chunk)
        two(which, chunk).wait_recv()
        got = ones[which][half if STREAMS[which][3] else parity, rows, :]
        total = plus(sums[which][s, rows, :], got, twos[which][rows, :])
        if layers == 1:
            sums[which][s, rows, :] = total.astype(BF)
            twin_copy(which, chunk, True).start()
            keep_copy(which, chunk, True).start()
            return
        if middle > 0:

            @pl.when(depth > 0)
            def _():
                inward(which, chunk, False).wait_recv()
                sums[which][s, rows, :] = plus(total, ins[which][rows, :]).astype(BF)

            @pl.when(depth == 0)
            def _():
                sums[which][s, rows, :] = total.astype(BF)

            @pl.when(depth < middle)
            def _():
                inward(which, chunk, False).start()

        else:
            sums[which][s, rows, :] = total.astype(BF)

        @pl.when(depth == middle)
        def _():
            inward(which, chunk, True).start()

    def finish(which, chunk):
        rows = rows_of(which, chunk)
        inward(which, chunk, True).wait_recv()

        @pl.when(depth == middle)
        def _():
            inward(which, chunk, True).wait_send()
            sums[which][s, rows, :] = plus(
                sums[which][s, rows, :], backs[which][rows, :]
            ).astype(BF)
            if middle > 0:
                outward_copy(which, chunk, True).start()
            twin_copy(which, chunk, True).start()
            keep_copy(which, chunk, True).start()

        if middle > 0:

            @pl.when(depth < middle)
            def _():
                @pl.when(depth > 0)
                def _():
                    outward_copy(which, chunk, False).start()

                twin_copy(which, chunk, False).start()
                keep_copy(which, chunk, False).start()

    lag3 = lag_z + lag_step * depth
    lag5 = lag_z + lag_step * (middle + 1) + lag_step * (middle - depth)
    slots = sum(CHUNKS) + lag_z + (lag_step * (2 * middle + 1) if layers > 1 else 0)

    def guarded(position, step):
        for which, count in enumerate(CHUNKS):
            chunk = position - OFFSETS[which]

            @pl.when((chunk >= 0) & (chunk < count))
            def _():
                step(which, chunk)

    def slot(k, unused):
        guarded(k, start_two)
        guarded(k - lag3, start_z)
        if layers > 1:
            guarded(k - lag5, finish)
        return unused

    lax.fori_loop(0, slots, slot, 0)

    def drain(which, chunk):
        twin_copy(which, chunk, True).wait_recv()
        twin_copy(which, chunk, True).wait_send()
        keep_copy(which, chunk, True).wait()
        if STREAMS[which][3]:
            one(which, chunk, 0).wait_send()
            one(which, chunk, 1).wait_send()
        else:
            one(which, chunk, 0).wait_send()
            one(which, chunk, 1).wait_send()
        two(which, chunk).wait_send()
        if layers > 1 and middle > 0:

            @pl.when(depth < middle)
            def _():
                inward(which, chunk, False).wait_send()

            @pl.when(depth > 0)
            def _():
                outward_copy(which, chunk, True).wait_send()

    def last(k, unused):
        guarded(k, drain)
        return unused

    lax.fori_loop(0, sum(CHUNKS), last, 0)
    for i in range(3):
        swap_copy(0, i).wait_send()
    own_share.wait()

    @pl.when(mine)
    def _():
        for i, to in enumerate((x, y, xy)):
            back_to(i, to).wait_send()
        back_to(1, y).wait_recv()

    @pl.when(jnp.logical_not(mine))
    def _():
        back_to(0, x).wait_recv()
        back_to(2, xy).wait_recv()


def backward(first_all, rest_all, vec, kept, dw, tails, bound, width, layers, lags=(3, 2)):
    anywhere = pl.BlockSpec(memory_space=pl.ANY)
    inside = pl.BlockSpec(memory_space=pltpu.VMEM)
    shapes = [(rows, columns) for rows, columns, unused, unused2 in STREAMS]
    most = max(CHUNKS)
    return pl.pallas_call(
        partial(backward_kernel, layers, lags),
        in_specs=[anywhere] * 11 + [inside] * 3,
        out_specs=[anywhere] * 4,
        out_shape=[jax.ShapeDtypeStruct((2,) + shape, BF) for shape in shapes]
        + [jax.ShapeDtypeStruct((4, ROWS, width), BF)],
        scratch_shapes=[pltpu.VMEM((4,) + shape, BF) for shape in shapes]
        + [pltpu.VMEM((2,) + shape, BF) for shape in shapes]
        + [pltpu.VMEM(shape, BF) for shape in shapes] * 3
        + [
            pltpu.VMEM((ROWS, D), BF),
            pltpu.VMEM((ROWS, D), BF),
            pltpu.VMEM((ROWS, 128), F32),
            pltpu.VMEM((ROWS, 2 * D), BF),
            pltpu.VMEM((D, FRONT), BF),
            pltpu.VMEM((HALF, D), BF),
            pltpu.VMEM((2, ROWS, HALF), BF),
            pltpu.VMEM((2, HALF, D), BF),
            pltpu.VMEM((ROWS, D), BF),
            pltpu.VMEM((ROWS, D), BF),
            pltpu.VMEM((ROWS, 128), F32),
            pltpu.VMEM((ROWS, FRONT), BF),
            pltpu.VMEM((ROWS, HALF), BF),
            pltpu.VMEM((PAIRS, 8, ROWS), F32),
            pltpu.VMEM((D, FRONT), BF),
            pltpu.VMEM((HALF, D), BF),
            pltpu.VMEM((4 * EXTRA, D), BF),
            pltpu.VMEM((ROWS, D), BF),
            pltpu.VMEM((ROWS, HALF), BF),
            pltpu.VMEM((ROWS, D), BF),
            pltpu.VMEM((2, ROWS, D), BF),
            pltpu.VMEM((4, ROWS, width), BF),
            pltpu.SemaphoreType.DMA((22,)),
            pltpu.SemaphoreType.DMA((2, 2)),
            pltpu.SemaphoreType.DMA((4, 3)),
            pltpu.SemaphoreType.DMA((4, 3)),
            pltpu.SemaphoreType.DMA((18, most)),
            pltpu.SemaphoreType.DMA((18, most)),
            pltpu.SemaphoreType.DMA((3, most)),
            pltpu.SemaphoreType.DMA((4,)),
            pltpu.SemaphoreType.DMA((4,)),
        ],
        compiler_params=pltpu.CompilerParams(
            collective_id=2, has_side_effects=True, vmem_limit_bytes=62 * 1024 * 1024
        ),
    )(first_all, rest_all, *kept, tails, bound, vec, dw)


def assemble_kernel(first_ref, rest_ref, out_ref):
    is_ffn = lax.axis_index("section") % 2
    row = pl.program_id(0)

    @pl.when(is_ffn == 0)
    def _():
        for core in range(2):
            for i in range(PAIRS):
                for t in range(3):
                    to = t * D + core * HALF + i * 128
                    at = (3 * i + t) * 128
                    out_ref[:, to : to + 128] = first_ref[core, :, at : at + 128].astype(F32)
        from_core = row // 3
        at = pl.multiple_of((row % 3) * 128, 128)
        out_ref[:, 3 * D :] = rest_ref[from_core, pl.ds(at, 128), :].astype(F32)

    @pl.when(is_ffn == 1)
    def _():
        lanes = pl.ds(pl.multiple_of(row * 128, 128), 128)
        for core in range(2):
            out_ref[:, core * D : (core + 1) * D] = first_ref[core, :, 0:D].astype(F32)
            at = 2 * D + core * D
            out_ref[:, at : at + HALF] = first_ref[core, :, D:].astype(F32)
            out_ref[:, at + HALF : at + D] = rest_ref[core, 0:HALF, lanes].astype(F32).T


def assemble(first_sum, rest_sum):
    return pl.pallas_call(
        assemble_kernel,
        grid=(D // 128,),
        in_specs=[
            pl.BlockSpec((2, 128, FRONT), lambda i: (0, i, 0)),
            pl.BlockSpec((2, SIDE, D), lambda i: (0, 0, 0)),
        ],
        out_specs=pl.BlockSpec((128, 4 * D), lambda i: (i, 0)),
        out_shape=jax.ShapeDtypeStruct((D, 4 * D), F32),
        compiler_params=pltpu.CompilerParams(vmem_limit_bytes=32 * 1024 * 1024),
    )(first_sum, rest_sum)


def gelu_and_slope(z):
    upper = 0.5 * (1.0 + lax.erf(z * 0.7071067811865476))
    density = jnp.exp(-0.5 * z * z) * 0.3989422804014327
    return (z * upper).astype(BF), (upper + z * density).astype(BF)


def on_device(
    inputs,
    in_weight,
    down_weight,
    out_bias,
    norm_gains,
    norm_shifts,
    projection,
    passage_lengths,
    positive,
):
    batches = lax.axis_size("batch")
    layers = batches // 2
    s = lax.axis_index("section")
    b = lax.axis_index("batch")
    core = b % 2
    groups = inputs.shape[0] * batches
    queries_all = groups * QUERY_COUNT

    def other_core(value):
        return lax.ppermute(value, "batch", [(j, j ^ 1) for j in range(batches)])

    def pick(table, index):
        return lax.dynamic_index_in_dim(table, index, 0, keepdims=False)

    mine = core == s % 2
    micro = s // 2
    lengths_all = passage_lengths[:, 0]

    def long_start(lengths):
        return jnp.where(
            lengths[0] == PLEN, 0, jnp.where(lengths[1] == PLEN, lengths[0], lengths[0] + lengths[1])
        )

    def rolled(rows, start):
        passages = rows[QROWS:]
        doubled = jnp.concatenate([passages, passages[:REST]], 0)
        return jnp.concatenate(
            [rows[:QROWS], lax.dynamic_slice_in_dim(doubled, start, PASSAGE_TOKENS, 0)], 0
        )

    def unrolled(rows, start):
        passages = rows[QROWS:]
        doubled = jnp.concatenate([passages[PLEN:], passages], 0)
        return jnp.concatenate(
            [rows[:QROWS], lax.dynamic_slice_in_dim(doubled, REST - start, PASSAGE_TOKENS, 0)], 0
        )

    slices = jnp.stack([rolled(inputs[m], long_start(lengths_all[m])) for m in range(2)])
    ints = jnp.pad(
        jnp.concatenate([lengths_all, positive], 1),
        ((0, 6), (0, 128 - PASSAGE_COUNT - QUERY_COUNT)),
    )
    vec = jnp.concatenate([out_bias, norm_gains, norm_shifts, jnp.zeros((5, D), F32)], 0)
    first_all, rest_all, vectors, *kept, dw, tails, bound = forward(
        in_weight[0],
        down_weight,
        projection.T.astype(BF),
        vec,
        slices,
        ints,
        layers,
        queries_all,
    )
    first_sum, side_sum, down_sum, back = backward(
        first_all, rest_all, vectors, kept, dw, tails, bound, inputs.shape[2], layers
    )
    in_grad = assemble(first_sum, side_sum)
    down_grad = down_sum.reshape(2 * D, D).astype(F32)
    extra = side_sum[0, HALF:].astype(F32)
    total_loss = jnp.sum(extra[3, :6]) / queries_all
    same_micro = jnp.where(mine, back[3], back[0])
    other_micro = jnp.where(mine, back[1], back[2])
    by_micro = [jnp.where(micro == m, same_micro, other_micro).astype(F32) for m in range(2)]
    input_grad = jnp.stack([unrolled(by_micro[m], long_start(lengths_all[m])) for m in range(2)])

    return (
        total_loss,
        input_grad,
        in_grad[None],
        down_grad,
        extra[0:1],
        extra[1:2],
        extra[2:3],
        extra[16:].T,
    )


def solution(mesh):
    in_specs = (
        P(None, "batch", "section"),
        P("section", None, None),
        P("section", None),
        P("section", None),
        P("section", None),
        P("section", None),
        P(None, "section"),
        P(None, "batch", None),
        P(None, "batch"),
    )
    out_specs = (
        P(),
        P(None, "batch", "section"),
        P("section", None, None),
        P("section", None),
        P("section", None),
        P("section", None),
        P("section", None),
        P(None, "section"),
    )
    return jax.shard_map(
        on_device, mesh=mesh, in_specs=in_specs, out_specs=out_specs, check_vma=False
    )
```

```python
from functools import partial

import jax
import jax.numpy as jnp
from jax import lax
from jax.experimental import pallas as pl
from jax.experimental.pallas import tpu as pltpu
from jax.sharding import PartitionSpec as P

D = 768
HEADS = 12
FF = 3072
DIM = 128
QUERY_LENGTH = 32
QUERY_COUNT = 4
PASSAGE_COUNT = 3
PASSAGE_TOKENS = 640
PLEN = 512
QROWS = QUERY_LENGTH * QUERY_COUNT
ROWS = QROWS + PASSAGE_TOKENS
REST = PASSAGE_TOKENS - PLEN
SOFTMAX_DIVISOR = 0.1
SIMILARITY_SCALE = 0.25
NORM_EPSILON = 1e-06
MASKED = -1000000000.0
BF = jnp.bfloat16
F32 = jnp.float32
BLOCKS = ((0, QROWS), (QROWS, PLEN), (QROWS + PLEN, REST))
PAIRS = HEADS // 4
HALF = D // 2


def mm(a, b, dims=((1,), (0,))):
    return lax.dot_general(a, b, (dims, ((), ())), preferred_element_type=F32)


def block_mask(which, bound, rows):
    t = lax.broadcasted_iota(jnp.int32, (rows, rows), 0)
    r = lax.broadcasted_iota(jnp.int32, (rows, rows), 1)
    if which == 0:
        return (t // QUERY_LENGTH) == (r // QUERY_LENGTH)
    return ((t.astype(F32) < bound).astype(F32) - (r.astype(F32) < bound).astype(F32)) == 0.0


def unit_matrix(n):
    r = lax.broadcasted_iota(jnp.int32, (n, n), 0)
    c = lax.broadcasted_iota(jnp.int32, (n, n), 1)
    return (r == c).astype(F32).astype(BF)


def rotation(i, begins):
    r = lax.broadcasted_iota(jnp.int32, (128, PASSAGE_TOKENS), 0).astype(F32) + float(i * 128)
    c = lax.broadcasted_iota(jnp.int32, (128, PASSAGE_TOKENS), 1).astype(F32)
    ahead = c - r - begins
    total = float(PASSAGE_TOKENS)
    return ((ahead == 0.0) | (ahead == -total) | (ahead == total)).astype(F32).astype(BF)


MESH = pl.DeviceIdType.MESH
EXTRA = 32
FRONT = 1152


def neighbours():
    s, b = lax.axis_index("section"), lax.axis_index("batch")
    x = s + 1 - 2 * (s % 2)
    y = s + 2 - 4 * (s // 2)
    xy = 3 - s
    return s, b, x, y, xy


def greet(layers):
    s, b, x, y, xy = neighbours()
    z, core = b // 2, b % 2
    barrier = pltpu.get_barrier_semaphore()

    def signal(to):
        pl.semaphore_signal(barrier, inc=1, device_id=to, device_id_type=MESH)

    signal((x, b))
    signal((y, b))
    signal((xy, b))
    signal((s, b + 1 - 2 * core))
    if layers > 1:

        @pl.when(z > 0)
        def _():
            signal((s, b - 2))

        @pl.when(z < layers - 1)
        def _():
            signal((s, b + 2))

        ends = (layers - 1 - z) // (layers - 1) + z // (layers - 1)
        pl.semaphore_wait(barrier, 6 - ends)
    else:
        pl.semaphore_wait(barrier, 4)


def forward_kernel(layers, spread, queries_all, *refs):
    w_ref, down_ref, slices_ref, projection_ref = refs[0:4]
    bias_ref, gain_ref, shift_ref, lengths_ref, positive_ref = refs[4:9]
    first_out, rest_out, vec_out, h_out, xhat_out, scale_out, qkv_out, ctx_out = refs[9:17]
    lse_out, act_out, slope_out, dw_out, tails_out, bound_out = refs[17:23]
    (
        first_all,
        rest_all,
        vec_all,
        tokens,
        ints_ref,
        ints_other,
        vec_ref,
        wide,
        out_stage,
        down_stage,
        hs,
        xhats,
        scales,
        qkvs,
        ctxs,
        lses,
        acts,
        slopes,
        part_out,
        part_in,
        proj,
        embedded,
        unit,
        length,
        grad_unit,
        grad_low,
        tails,
        load_sem,
        send_sem,
        recv_sem,
        z_send,
        z_recv,
        in_send,
        in_recv,
        part_send,
        part_recv,
        save_sem,
    ) = refs[23:]
    s, b, x, y, xy = neighbours()
    z, core = b // 2, b % 2
    micro = s // 2
    mine = core == s % 2
    twin = b + 1 - 2 * core

    def load(src, dst, i):
        return pltpu.make_async_copy(src, dst, load_sem.at[i])

    loads = [load(down_ref.at[pl.ds(core * D, D), :], down_stage, 0)]
    even, odd = [], []
    for i in range(PAIRS):
        for t in range(3):
            at = pl.multiple_of(t * D + core * HALF + i * 128, 128)
            to = (3 * i + t) * 128
            even.append(
                load(w_ref.at[:, pl.ds(at, 128)], wide.at[:, pl.ds(to, 128)], 1 + 3 * i + t)
            )
    even.append(load(w_ref.at[pl.ds(core * HALF, HALF), pl.ds(3 * D, D)], out_stage, 10))
    for i in range(2):
        at = pl.multiple_of(i * 2 * D + core * D, 128)
        odd.append(load(w_ref.at[:, pl.ds(at, D)], wide.at[:, pl.ds(i * D, D)], 11 + i))
    loads[0].start()

    @pl.when(s % 2 == 0)
    def _():
        for copy in even:
            copy.start()

    @pl.when(s % 2 == 1)
    def _():
        for copy in odd:
            copy.start()

    first, rest = first_all.at[s], rest_all.at[s]
    ints_ref[...] = jnp.zeros_like(ints_ref)
    ints_ref[0:2, 0:PASSAGE_COUNT] = lengths_ref[...]
    ints_ref[8:10, 0:QUERY_COUNT] = positive_ref[...]
    vec_ref[0:1, :] = bias_ref[...]
    vec_ref[1:2, :] = gain_ref[...]
    vec_ref[2:3, :] = shift_ref[...]
    vec_ref[3:8, :] = jnp.zeros((5, D), F32)
    own_vec = pltpu.make_async_copy(vec_ref, vec_all.at[s], load_sem.at[15])
    own_vec.start()
    rest[FRONT : FRONT + EXTRA, :] = projection_ref[...].astype(BF)
    greet(layers)

    def features(section):
        size = slices_ref.shape[1]
        return tokens.at[pl.ds(pl.multiple_of(section * size, 16), size), :]

    def feature_copy(i, which, section, to):
        return pltpu.make_async_remote_copy(
            src_ref=slices_ref.at[which],
            dst_ref=features(section),
            send_sem=in_send.at[i],
            recv_sem=in_recv.at[i],
            device_id=(to, b),
            device_id_type=MESH,
        )

    def to_twin(i, src, dst):
        return pltpu.make_async_remote_copy(
            src_ref=src,
            dst_ref=dst,
            send_sem=in_send.at[i],
            recv_sem=in_recv.at[i],
            device_id=(s, twin),
            device_id_type=MESH,
        )

    def quarter_to_twin(i, f):
        return to_twin(i, features(f), features(f))

    swap_ints = to_twin(7, ints_ref, ints_other)
    own_quarter = pltpu.make_async_copy(slices_ref.at[micro], features(s), load_sem.at[14])
    swap_ints.start()

    @pl.when(mine)
    def _():
        own_quarter.start()
        feature_copy(1, 1 - micro, s, y).start()

    @pl.when(jnp.logical_not(mine))
    def _():
        feature_copy(0, micro, s, x).start()
        feature_copy(2, 1 - micro, s, xy).start()

    loads[0].wait()

    @pl.loop(0, D // 96)
    def _(i):
        rows = pl.ds(pl.multiple_of(i * 96, 16), 96)
        to = pl.ds(pl.multiple_of(HALF + i * 96, 16), 96)
        rest[to, :] = down_stage[rows, :].astype(BF)

    quarter = D // 4
    firsts = [(first, first_all, i * quarter, quarter, i < 2) for i in range(4)]
    seconds = [(rest, rest_all, i * 192, 192, i == 0) for i in range(2)]
    small = [
        (rest, rest_all, FRONT, EXTRA, True),
        (vec_ref, vec_all, 0, 8, False),
    ]
    if spread:
        share = D // layers
        at = pl.multiple_of(HALF + z * share, 16)
        half = share // 2
        slices = [
            (rest, rest_all, at, half, True),
            (rest, rest_all, pl.multiple_of(at + half, 16), share - half, False),
        ]
    else:
        slices = []
        seconds += [(rest, rest_all, HALF + i * 192, 192, i % 2 == 0) for i in range(4)]
    pieces = slices + firsts + seconds + small

    def part(n, ref):
        unused, unused, row, rows, unused = pieces[n]
        return ref.at[pl.ds(row, rows), :]

    def remote(n, kind, src, dst, to):
        return pltpu.make_async_remote_copy(
            src_ref=src,
            dst_ref=dst,
            send_sem=send_sem.at[kind, n],
            recv_sem=recv_sem.at[kind, n],
            device_id=(to, b),
            device_id_type=MESH,
        )

    def direct(n, kind):
        mine, every = pieces[n][:2]
        return remote(n, kind, part(n, mine), part(n, every.at[s]), y if kind else x)

    def arrived(n, kind):
        every = pieces[n][1]
        owner = (x, y, xy)[kind]
        here = part(n, every.at[owner])
        remote(n, kind, here, here, x).wait_recv()

    def relay(n):
        every, by_x = pieces[n][1], pieces[n][4]
        source = part(n, every.at[x if by_x else y])
        return remote(n, 2, source, source, y if by_x else x)

    def pass_on(n):
        arrived(n, 0 if pieces[n][4] else 1)
        relay(n).start()

    count = len(pieces)
    front = list(range(len(slices), len(slices) + 4))
    behind = list(range(len(slices) + 4, count))

    def along_x(n):
        direct(n, 0).start()

    def along_y(n):
        direct(n, 1).start()

    z_width = D // layers if spread else 0

    def z_part(section, owner_z):
        at = pl.multiple_of(HALF + owner_z * z_width, 16)
        return rest_all.at[section, pl.ds(at, z_width), :]

    def z_copy(way, step, k, owner_z, to_b):
        source = z_part((x, y, xy)[k], owner_z)
        return pltpu.make_async_remote_copy(
            src_ref=source,
            dst_ref=source,
            send_sem=z_send.at[way, step, k],
            recv_sem=z_recv.at[way, step, k],
            device_id=(s, to_b),
            device_id_type=MESH,
        )

    def z_first(k):
        @pl.when(z < layers - 1)
        def _():
            z_copy(0, 0, k, z, b + 2).start()

        @pl.when(z > 0)
        def _():
            z_copy(1, 0, k, z, b - 2).start()

    def z_step(step):
        @pl.when(z >= step)
        def _():
            for k in range(3):
                z_copy(0, step - 1, k, z - step, b).wait_recv()

                @pl.when(z < layers - 1)
                def _():
                    z_copy(0, step, k, z - step, b + 2).start()

        @pl.when(z < layers - step)
        def _():
            for k in range(3):
                z_copy(1, step - 1, k, z + step, b).wait_recv()

                @pl.when(z > 0)
                def _():
                    z_copy(1, step, k, z + step, b - 2).start()

    def z_drain():
        for step in range(layers - 1):

            @pl.when((z < layers - 1) & (z >= step))
            def _():
                for k in range(3):
                    z_copy(0, step, k, z - step, b + 2).wait_send()

            @pl.when((z > 0) & (z + step < layers))
            def _():
                for k in range(3):
                    z_copy(1, step, k, z + step, b - 2).wait_send()

    for n in range(len(slices)):
        along_x(n)
        along_y(n)
    @pl.when(s % 2 == 0)
    def _():
        for copy in even:
            copy.wait()

        @pl.loop(0, HALF // 96)
        def _(i):
            rows = pl.ds(pl.multiple_of(i * 96, 16), 96)
            rest[rows, :] = out_stage[rows, :].astype(BF)

    @pl.when(s % 2 == 1)
    def _():
        for copy in odd:
            copy.wait()
        for i in range(3):
            for j in range(6):
                block = wide[j * 128 : (j + 1) * 128, FRONT + i * 128 : FRONT + (i + 1) * 128]
                rest[i * 128 : (i + 1) * 128, j * 128 : (j + 1) * 128] = block.T.astype(BF)

    @pl.loop(0, D // 96)
    def _(i):
        rows = pl.ds(pl.multiple_of(i * 96, 16), 96)
        first[rows, :] = wide[rows, 0:FRONT].astype(BF)


    along_x(front[0])
    along_y(front[2])

    @pl.when(mine)
    def _():
        own_quarter.wait()
        quarter_to_twin(3, s).start()
        for i, owner in enumerate((x, y, xy)):
            feature_copy(i, 0, owner, x).wait_recv()
            quarter_to_twin(4 + i, owner).start()

    if spread:
        pass_on(0)
        pass_on(1)
    along_x(front[1])
    along_y(front[3])
    if spread:
        arrived(0, 1)
        arrived(1, 0)
        z_first(0)
        z_first(1)
    pass_on(front[0])
    pass_on(front[2])
    along_x(front[2])
    along_y(front[0])
    if spread:
        arrived(0, 2)
        arrived(1, 2)
        z_first(2)
    pass_on(front[1])
    pass_on(front[3])
    along_x(front[3])
    along_y(front[1])
    z_at = 1
    if spread and z_at < layers - 1:
        z_step(z_at)
        z_at += 1
    for n in behind:
        if pieces[n][4]:
            along_x(n)
        else:
            along_y(n)
    for n in behind:
        if pieces[n][4]:
            along_y(n)
        else:
            along_x(n)
    for n in front:
        arrived(n, 1 if pieces[n][4] else 0)
    while spread and z_at < layers - 1:
        z_step(z_at)
        z_at += 1
    for n in front:
        arrived(n, 2)
    swap_ints.wait()
    own_vec.wait()

    @pl.when(jnp.logical_not(mine))
    def _():
        for i, owner in enumerate((s, x, y, xy)):
            quarter_to_twin(3 + i, owner).wait_recv()

    lane = lax.broadcasted_iota(jnp.int32, (1, 128), 1)

    def entry(first_row, i):
        row = pl.ds(first_row + micro, 1)
        values = jnp.where(mine, ints_ref[row, :].astype(F32), ints_other[row, :].astype(F32))
        return jnp.sum(jnp.where(lane == i, values, 0.0), axis=1, keepdims=True)

    sizes = [entry(0, i) for i in range(PASSAGE_COUNT)]
    is_long = [
        (sizes[0] == float(PLEN)).astype(F32),
        (sizes[1] == float(PLEN)).astype(F32),
        (sizes[2] == float(PLEN)).astype(F32),
    ]
    bound = is_long[0] * sizes[1] + is_long[1] * sizes[2] + is_long[2] * sizes[0]
    long_index = is_long[1] + 2.0 * is_long[2]
    begins = is_long[1] * sizes[0] + is_long[2] * (sizes[0] + sizes[1])

    saves = []

    def save(src, dst):
        copy = pltpu.make_async_copy(src, dst, save_sem.at[len(saves)])
        copy.start()
        saves.append(copy)

    save(first_all, first_out)

    def swap_copy(t, i):
        rows = pl.ds(i * 256, 256)
        return pltpu.make_async_remote_copy(
            src_ref=part_out.at[rows, :],
            dst_ref=part_in.at[t % 2, rows, :],
            send_sem=part_send.at[t, i],
            recv_sem=part_recv.at[t, i],
            device_id=(s, twin),
            device_id_type=MESH,
        )

    hs[0, 0:QROWS, :] = mm(unit_matrix(QROWS), tokens[:, 0:QROWS], ((1,), (1,))).astype(BF)
    for i in range(PASSAGE_TOKENS // 128):
        rows = slice(QROWS + i * 128, QROWS + (i + 1) * 128)
        hs[0, rows, :] = mm(rotation(i, begins), tokens[:, QROWS:], ((1,), (1,))).astype(BF)
    save(hs.at[0], h_out.at[0])

    def norm_rows(t, i):
        bias, gain, shift = vec_all[t, 0:1, :], vec_all[t, 1:2, :], vec_all[t, 2:3, :]
        swap_copy(t, i).wait_recv()

        def body(j, unused):
            rows = pl.ds(pl.multiple_of(j * 128, 128), 128)
            u = (
                hs[t, rows, :].astype(F32)
                + part_out[rows, :].astype(F32)
                + part_in[t % 2, rows, :].astype(F32)
                + bias
            )
            centered = u - jnp.mean(u, -1, keepdims=True)
            scale = lax.rsqrt(jnp.mean(centered * centered, -1, keepdims=True) + NORM_EPSILON)
            xhat = centered * scale
            xhats[t, rows, :] = xhat.astype(BF)
            scales[t, rows, :] = jnp.broadcast_to(scale, (128, 128))
            hs[t + 1, rows, :] = (xhat * gain + shift).astype(BF)
            return unused

        lax.fori_loop(2 * i, 2 * i + 2, body, 0)

    def save_norm(t):
        save(xhats.at[t], xhat_out.at[t])
        save(scales.at[t], scale_out.at[t])
        if t < 3:
            save(hs.at[t + 1], h_out.at[t + 1])

    def attention_pair(l):
        def pair(i, unused):
            base = pl.multiple_of(i * 384, 128)
            q_at = pl.ds(base, 128)
            k_at = pl.ds(pl.multiple_of(base + 128, 128), 128)
            v_at = pl.ds(pl.multiple_of(base + 256, 128), 128)
            c_at = pl.ds(pl.multiple_of(i * 128, 128), 128)
            for which, (begin, size) in enumerate(BLOCKS):
                chunk = size
                span = slice(begin, begin + size)
                k = qkvs[l, span, k_at]
                v = qkvs[l, span, v_at]
                for at in range(begin, begin + size, chunk):
                    rows = slice(at, at + chunk)
                    q = qkvs[l, rows, q_at]
                    total = None
                    for head in range(2):
                        own = (lane < 64) if head == 0 else (lane >= 64)
                        qm = jnp.where(own, q, jnp.zeros_like(q)) * BF(0.125)
                        vm = jnp.where(own, v, jnp.zeros_like(v))
                        score = mm(k, qm, ((1,), (1,)))
                        if which != 1:
                            score = jnp.where(block_mask(which, bound, size), score, MASKED)
                        top = jnp.max(score, axis=0, keepdims=True)
                        e = jnp.exp(score - top)
                        weight = jnp.sum(e, axis=0, keepdims=True)
                        part = mm(vm, e.astype(BF), ((0,), (0,))) * (1.0 / weight)
                        total = part if total is None else total + part
                        lses[l, i, head : head + 1, rows] = top + jnp.log(weight)
                    ctxs[l, rows, c_at] = total.T.astype(BF)
            return unused

        lax.fori_loop(0, PAIRS, pair, 0)

    def attention_layer(l):
        t = 2 * l
        for i in range(3):
            rows = slice(i * 256, (i + 1) * 256)
            if t > 0:
                norm_rows(t - 1, i)
            qkvs[l, rows, :] = mm(hs[t, rows, :], first_all[t]).astype(BF)
        if t > 0:
            save_norm(t - 1)
        save(qkvs.at[l], qkv_out.at[l])
        if l == 0:
            for n in behind:
                pass_on(n)
        attention_pair(l)
        if l == 0:
            for n in behind:
                arrived(n, 1 if pieces[n][4] else 0)
                arrived(n, 2)
        save(ctxs.at[l], ctx_out.at[l])
        save(lses.at[l], lse_out.at[l])
        for i in range(3):
            rows = slice(i * 256, (i + 1) * 256)
            if t > 0:
                swap_copy(t - 1, i).wait_send()
            part_out[rows, :] = mm(ctxs[l, rows, :], rest_all[t, 0:HALF, :]).astype(BF)
            swap_copy(t, i).start()

    def ffn_layer(l):
        t = 2 * l + 1
        for i in range(3):
            rows = slice(i * 256, (i + 1) * 256)
            norm_rows(t - 1, i)
            x_rows = hs[t, rows, :]
            for j in range(4):
                columns = slice(j * HALF, (j + 1) * HALF)
                if j < 3:
                    value = mm(x_rows, first_all[t, :, columns])
                else:
                    value = mm(x_rows, rest_all[t, 0:HALF, :], ((1,), (1,)))
                act, slope = gelu_and_slope(value)
                acts[l, rows, columns] = act
                slopes[l, rows, columns] = slope
            swap_copy(t - 1, i).wait_send()
            part = mm(acts[l, rows, 0:D], rest_all[2 * l, HALF:FRONT, :])
            part = part + mm(acts[l, rows, D:], rest_all[2 * l + 1, HALF:FRONT, :])
            part_out[rows, :] = part.astype(BF)
            swap_copy(t, i).start()
        save_norm(t - 1)
        save(acts.at[l], act_out.at[l])
        save(slopes.at[l], slope_out.at[l])

    attention_layer(0)
    if spread:
        z_step(layers - 1)
    save(vec_all, vec_out)
    save(rest_all, rest_out)
    ffn_layer(0)
    attention_layer(1)
    ffn_layer(1)

    for t in range(4):
        proj[t * EXTRA : (t + 1) * EXTRA, :] = rest_all[t, FRONT : FRONT + EXTRA, :]
    for i in range(3):
        rows = slice(i * 256, (i + 1) * 256)
        norm_rows(3, i)
        w = mm(hs[4, rows, :], proj[...], ((1,), (1,)))
        r = lax.rsqrt(jnp.sum(w * w, -1, keepdims=True) + NORM_EPSILON)
        unit[rows, :] = w * r
        length[rows, :] = jnp.broadcast_to(r, (256, 128))
        embedded[rows, :] = (w * r).astype(BF)
    save_norm(3)
    queries, passages = embedded[0:QROWS, :], embedded[QROWS:, :]
    logits = mm(queries, passages, ((1,), (1,))) * (1.0 / SOFTMAX_DIVISOR)
    column = lax.broadcasted_iota(jnp.int32, (1, REST), 1).astype(F32)
    token = lax.broadcasted_iota(jnp.int32, (QROWS, 1), 0)
    before = column < bound
    softs, shares = [], []
    for p in range(3):
        if p == 0:
            score = logits[:, 0:PLEN]
            top = jnp.max(score, -1, keepdims=True)
            e = jnp.exp(score - top)
        else:
            score = logits[:, PLEN:]
            inside = before if p == 1 else jnp.logical_not(before)
            score = jnp.where(inside, score, MASKED)
            top = jnp.max(score, -1, keepdims=True)
            e = jnp.where(inside, jnp.exp(score - top), 0.0)
        weight = jnp.sum(e, -1, keepdims=True)
        softs.append(SOFTMAX_DIVISOR * (top + jnp.log(weight)))
        shares.append(e * (1.0 / weight))
    loss = jnp.zeros((1, 1), F32)
    grad_softs = [jnp.zeros((QROWS, 1), F32) for p in range(3)]
    for q in range(QUERY_COUNT):
        mine_rows = (token // QUERY_LENGTH) == q
        scores = [
            SIMILARITY_SCALE * jnp.sum(jnp.where(mine_rows, soft, 0.0), 0, keepdims=True)
            for soft in softs
        ]
        top = jnp.maximum(jnp.maximum(scores[0], scores[1]), scores[2])
        es = [jnp.exp(score - top) for score in scores]
        weight = es[0] + es[1] + es[2]
        wanted = entry(8, q) - long_index
        wanted = jnp.where(wanted < 0.0, wanted + 3.0, wanted)
        chosen = [(wanted == float(p)).astype(F32) for p in range(3)]
        picked = chosen[0] * scores[0] + chosen[1] * scores[1] + chosen[2] * scores[2]
        loss = loss + top + jnp.log(weight) - picked
        for p in range(3):
            grad = (es[p] / weight - chosen[p]) * (SIMILARITY_SCALE / queries_all)
            grad_softs[p] = jnp.where(mine_rows, grad, grad_softs[p])
    grad_logits = jnp.concatenate(
        [grad_softs[0] * shares[0], grad_softs[1] * shares[1] + grad_softs[2] * shares[2]], axis=1
    ).astype(BF)
    grad_unit[0:QROWS, :] = mm(grad_logits, passages)
    grad_unit[QROWS:, :] = mm(grad_logits, queries, ((0,), (0,)))
    for i in range(3):
        rows = slice(i * 256, (i + 1) * 256)
        n, dn = unit[rows, :], grad_unit[rows, :]
        inner = jnp.sum(n * dn, -1, keepdims=True)
        grad_low[rows, :] = (length[rows, :] * (dn - n * inner)).astype(BF)
    save(grad_low, dw_out)
    grad_proj = mm(grad_low[...], hs[4], ((0,), (0,)))
    feature = lax.broadcasted_iota(jnp.int32, (16, D), 1)
    line = lax.broadcasted_iota(jnp.int32, (16, D), 0)
    head_rows = jnp.zeros((16, D), F32)
    left = loss
    for i, step in enumerate((8.0, 0.5, 2.0**-5, 2.0**-9, 2.0**-13, 2.0**-17)):
        value = jnp.floor(left * (1.0 / step)) * step
        left = left - value
        head_rows = jnp.where((line == 3) & (feature == i), value, head_rows)
    for t in range(4):
        tails[t, 0:16, :] = head_rows.astype(BF)
        tails[t, 16:TAIL, :] = grad_proj[t * EXTRA : (t + 1) * EXTRA, :].astype(BF)
    save(tails, tails_out)
    which_row = lax.broadcasted_iota(jnp.int32, (8, 1), 0)
    unit[0:8, :] = jnp.broadcast_to(jnp.where(which_row == 0, bound, begins), (8, 128))
    save(unit.at[pl.ds(0, 8), :], bound_out)

    for copy in saves:
        copy.wait()
    for i in range(3):
        swap_copy(3, i).wait_send()
    for n in range(count):
        direct(n, 0).wait_send()
        direct(n, 1).wait_send()
        relay(n).wait_send()
    if spread:
        z_drain()

    @pl.when(mine)
    def _():
        feature_copy(1, 1 - micro, s, y).wait_send()
        for i, owner in enumerate((s, x, y, xy)):
            quarter_to_twin(3 + i, owner).wait_send()

    @pl.when(jnp.logical_not(mine))
    def _():
        feature_copy(0, micro, s, x).wait_send()
        feature_copy(2, 1 - micro, s, xy).wait_send()


def forward(w, down, slices, projection, vectors, lengths, positive, layers, queries_all):
    spread = layers > 1 and D % (32 * layers) == 0
    anywhere = pl.BlockSpec(memory_space=pl.ANY)
    inside = pl.BlockSpec(memory_space=pltpu.VMEM)
    pieces = 12 if not spread else 10
    steps = max(layers - 1, 1) if spread else 1
    kept = [
        ((4, D, FRONT), BF),
        ((4, FRONT + EXTRA, D), BF),
        ((4, 8, D), F32),
        ((4, ROWS, D), BF),
        ((4, ROWS, D), BF),
        ((4, ROWS, 128), F32),
        ((2, ROWS, FRONT), BF),
        ((2, ROWS, HALF), BF),
        ((2, PAIRS, 8, ROWS), F32),
        ((2, ROWS, 2 * D), BF),
        ((2, ROWS, 2 * D), BF),
        ((ROWS, DIM), BF),
        ((4, TAIL, D), BF),
        ((8, 128), F32),
    ]
    return pl.pallas_call(
        partial(forward_kernel, layers, spread, queries_all),
        in_specs=[anywhere] * 3 + [inside] * 6,
        out_specs=[anywhere] * len(kept),
        out_shape=[jax.ShapeDtypeStruct(shape, kind) for shape, kind in kept],
        scratch_shapes=[
            pltpu.VMEM((4, D, FRONT), BF),
            pltpu.VMEM((4, FRONT + EXTRA, D), BF),
            pltpu.VMEM((4, 8, D), F32),
            pltpu.VMEM((D, ROWS), BF),
            pltpu.VMEM((16, 128), jnp.int32),
            pltpu.VMEM((16, 128), jnp.int32),
            pltpu.VMEM((8, D), F32),
            pltpu.VMEM((D, 2 * D), F32),
            pltpu.VMEM((HALF, D), F32),
            pltpu.VMEM((D, D), F32),
            pltpu.VMEM((5, ROWS, D), BF),
            pltpu.VMEM((4, ROWS, D), BF),
            pltpu.VMEM((4, ROWS, 128), F32),
            pltpu.VMEM((2, ROWS, FRONT), BF),
            pltpu.VMEM((2, ROWS, HALF), BF),
            pltpu.VMEM((2, PAIRS, 8, ROWS), F32),
            pltpu.VMEM((2, ROWS, 2 * D), BF),
            pltpu.VMEM((2, ROWS, 2 * D), BF),
            pltpu.VMEM((ROWS, D), BF),
            pltpu.VMEM((2, ROWS, D), BF),
            pltpu.VMEM((DIM, D), BF),
            pltpu.VMEM((ROWS, DIM), BF),
            pltpu.VMEM((ROWS, DIM), F32),
            pltpu.VMEM((ROWS, DIM), F32),
            pltpu.VMEM((ROWS, DIM), F32),
            pltpu.VMEM((ROWS, DIM), BF),
            pltpu.VMEM((4, TAIL, D), BF),
            pltpu.SemaphoreType.DMA((16,)),
            pltpu.SemaphoreType.DMA((3, pieces)),
            pltpu.SemaphoreType.DMA((3, pieces)),
            pltpu.SemaphoreType.DMA((2, steps, 3)),
            pltpu.SemaphoreType.DMA((2, steps, 3)),
            pltpu.SemaphoreType.DMA((8,)),
            pltpu.SemaphoreType.DMA((8,)),
            pltpu.SemaphoreType.DMA((4, 3)),
            pltpu.SemaphoreType.DMA((4, 3)),
            pltpu.SemaphoreType.DMA((32,)),
        ],
        compiler_params=pltpu.CompilerParams(
            collective_id=1, has_side_effects=True, vmem_limit_bytes=62 * 1024 * 1024
        ),
    )(w, down, slices, projection, *vectors, lengths, positive)


TAIL = 48
SIDE = HALF + TAIL
STREAMS = ((D, FRONT, 64, True), (SIDE, D, 48, False), (D, D, 64, True))
CHUNKS = tuple(rows // step for rows, unused, step, unused2 in STREAMS)
OFFSETS = (CHUNKS[2], CHUNKS[2] + CHUNKS[0], 0)
ONE_LOW, ONE_HIGH, TWO, INWARD, BACK, TWIN = 0, 3, 6, 9, 12, 15


def backward_kernel(layers, lags, *refs):
    first_all, rest_all, hs, xhats, scales, qkvs, ctxs, lses, acts, slopes, tails = refs[0:11]
    bound_ref, vec_ref, dw_ref = refs[11:14]
    outs, out_back = refs[14:17], refs[17]
    sums, ones, twos, ins, backs = refs[18:21], refs[21:24], refs[24:27], refs[27:30], refs[30:33]
    (
        h_f,
        xhat_f,
        scale_f,
        slope,
        up_first,
        up_second,
        act_ring,
        down_ring,
        h_a,
        xhat_a,
        scale_a,
        qkv,
        ctx,
        lse,
        att_first,
        att_second,
        proj,
        dy,
        dc,
        part_out,
        part_in,
        shares,
        load_sem,
        ring_sem,
        part_send,
        part_recv,
        send_sem,
        recv_sem,
        keep_sem,
        in_send,
        in_recv,
    ) = refs[33:]
    s, b, x, y, xy = neighbours()
    z, core = b // 2, b % 2
    half = s // 2
    parity = s % 2
    mine = core == parity
    twin = b + 1 - 2 * core
    middle = max(layers // 2 - 1, 0)
    upper = z // max(layers // 2, 1)
    depth = z + upper * (layers - 1 - 2 * z)
    toward = b + 2 - 4 * upper
    outward = b - 2 + 4 * upper
    lag_z, lag_step = lags

    def load(src, dst, i):
        return pltpu.make_async_copy(src, dst, load_sem.at[i])

    def loads_ffn(l):
        t = 2 * l + 1
        return [
            load(hs.at[t], h_f, 0),
            load(xhats.at[t], xhat_f, 1),
            load(scales.at[t], scale_f, 2),
            load(slopes.at[l], slope, 3),
            load(first_all.at[t], up_first, 4),
            load(rest_all.at[t, pl.ds(0, HALF), :], up_second, 5),
        ]

    def loads_attention(l):
        t = 2 * l
        return [
            load(hs.at[t], h_a, 6),
            load(xhats.at[t], xhat_a, 7),
            load(scales.at[t], scale_a, 8),
            load(qkvs.at[l], qkv, 9),
            load(ctxs.at[l], ctx, 10),
            load(lses.at[l], lse, 11),
            load(first_all.at[t], att_first, 12),
            load(rest_all.at[t, pl.ds(0, HALF), :], att_second, 13),
        ]

    def ring(l, j):
        slot = j % 2
        rows = pl.ds(HALF + (j % 2) * HALF, HALF)
        return (
            pltpu.make_async_copy(
                acts.at[l, :, pl.ds(j * HALF, HALF)], act_ring.at[slot], ring_sem.at[0, slot]
            ),
            pltpu.make_async_copy(
                rest_all.at[2 * l + j // 2, rows, :], down_ring.at[slot], ring_sem.at[1, slot]
            ),
        )

    def start(copies):
        for copy in copies:
            copy.start()

    def wait(copies):
        for copy in copies:
            copy.wait()

    start_loads = [
        load(rest_all.at[t, pl.ds(FRONT, EXTRA), :], proj.at[pl.ds(t * EXTRA, EXTRA), :], 14 + t)
        for t in range(4)
    ] + [load(tails.at[t], sums[1].at[t, pl.ds(HALF, TAIL), :], 18 + t) for t in range(4)]
    start(start_loads)
    start(loads_ffn(1))
    start(ring(1, 0))
    start(ring(1, 1))
    start(loads_attention(1))
    greet(layers)
    wait(start_loads)

    def remote(kind, chunk, src, dst, to):
        return pltpu.make_async_remote_copy(
            src_ref=src,
            dst_ref=dst,
            send_sem=send_sem.at[kind, chunk],
            recv_sem=recv_sem.at[kind, chunk],
            device_id=to,
            device_id_type=MESH,
        )

    def rows_of(which, chunk):
        size = STREAMS[which][2]
        return pl.ds(pl.multiple_of(chunk * size, 16), size)

    def one(which, chunk, l):
        rows = rows_of(which, chunk)
        kind = (ONE_HIGH if l else ONE_LOW) + which
        if STREAMS[which][3]:
            src = sums[which].at[2 * l + 1 - parity, rows, :]
            return remote(kind, chunk, src, ones[which].at[l, rows, :], (x, b))
        src = sums[which].at[2 * (1 - half) + l, rows, :]
        return remote(kind, chunk, src, ones[which].at[l, rows, :], (y, b))

    def forwarded(which):
        return 2 * (1 - half) + parity if STREAMS[which][3] else 2 * half + 1 - parity

    def two(which, chunk):
        rows = rows_of(which, chunk)
        src = sums[which].at[forwarded(which), rows, :]
        to = y if STREAMS[which][3] else x
        return remote(TWO + which, chunk, src, twos[which].at[rows, :], (to, b))

    def inward(which, chunk, swap):
        rows = rows_of(which, chunk)
        src = sums[which].at[s, rows, :]
        if swap:
            return remote(BACK + which, chunk, src, backs[which].at[rows, :], (s, toward))
        return remote(INWARD + which, chunk, src, ins[which].at[rows, :], (s, toward))

    def final(which, at_middle):
        return sums[which].at[s] if at_middle else backs[which]

    def outward_copy(which, chunk, at_middle):
        rows = rows_of(which, chunk)
        src = final(which, at_middle).at[rows, :]
        return remote(BACK + which, chunk, src, backs[which].at[rows, :], (s, outward))

    def twin_copy(which, chunk, at_middle):
        rows = rows_of(which, chunk)
        src = final(which, at_middle).at[rows, :]
        return remote(TWIN + which, chunk, src, outs[which].at[core, rows, :], (s, twin))

    def keep_copy(which, chunk, at_middle):
        rows = rows_of(which, chunk)
        src = final(which, at_middle).at[rows, :]
        return pltpu.make_async_copy(
            src, outs[which].at[core, rows, :], keep_sem.at[which, chunk]
        )

    def plus(*values):
        total = values[0].astype(F32)
        for value in values[1:]:
            total = total + value.astype(F32)
        return total

    def send_block(which, t, start_row, rows):
        size = STREAMS[which][2]
        by_x = STREAMS[which][3]

        @pl.when(parity != t % 2 if by_x else half != t // 2)
        def _():
            def body(c, unused):
                one(which, c, t // 2 if by_x else t % 2).start()
                return unused

            lax.fori_loop(start_row // size, (start_row + rows) // size, body, 0)

    def swap_copy(t, i):
        rows = pl.ds(i * 256, 256)
        return pltpu.make_async_remote_copy(
            src_ref=part_out.at[rows, :],
            dst_ref=part_in.at[t % 2, rows, :],
            send_sem=part_send.at[t, i],
            recv_sem=part_recv.at[t, i],
            device_id=(s, twin),
            device_id_type=MESH,
        )

    def norm_back(t, grad_of, xhat, scale):
        gain = vec_ref[t, 1:2, :]

        def body(i, carry):
            rows = pl.ds(pl.multiple_of(i * 128, 128), 128)
            grad = grad_of(rows)
            xh = xhat[rows, :].astype(F32)
            weighted = grad * gain
            mean_1 = jnp.mean(weighted, -1, keepdims=True)
            mean_2 = jnp.mean(weighted * xh, -1, keepdims=True)
            du = scale[rows, 0:1] * (weighted - mean_1 - xh * mean_2)
            dy[rows, :] = du.astype(BF)
            return (
                carry[0] + jnp.sum(du, 0, keepdims=True),
                carry[1] + jnp.sum(grad * xh, 0, keepdims=True),
                carry[2] + jnp.sum(grad, 0, keepdims=True),
            )

        zero = jnp.zeros((1, D), F32)
        carry = (zero, zero, zero)
        for i in range(3):
            if t < 3:
                swap_copy(t + 1, i).wait_recv()
            carry = lax.fori_loop(2 * i, 2 * i + 2, body, carry)
        row = lax.broadcasted_iota(jnp.int32, (16, 1), 0)
        block = sums[1][t, HALF : HALF + 16, :].astype(F32)
        for i in range(3):
            block = jnp.where(row == i, carry[i], block)
        sums[1][t, HALF : HALF + 16, :] = block.astype(BF)

    def grad_from_head(rows):
        return mm(dw_ref[rows, :], proj[...])

    def grad_from(t):
        def grad_of(rows):
            total = plus(dy[rows, :], part_out[rows, :], part_in[t % 2, rows, :])
            return total.astype(BF).astype(F32)

        return grad_of

    def ffn_back(l):
        t = 2 * l + 1
        for j in range(4):
            wait(ring(l, j))
            slot = j % 2
            columns = slice(j * HALF, (j + 1) * HALF)
            low = dy[...]
            to = (j % 2) * HALF
            sums[2][2 * l + j // 2, to : to + HALF, :] = mm(
                act_ring[slot], low, ((0,), (0,))
            ).astype(BF)
            send_block(2, 2 * l + j // 2, to, HALF)
            for i in range(3):
                rows = slice(i * 256, (i + 1) * 256)
                grad = mm(dy[rows, :], down_ring[slot], ((1,), (1,)))
                slope[rows, columns] = (grad * slope[rows, columns].astype(F32)).astype(BF)
            if j < 2:
                start(ring(l, j + 2))
        for i in range(3):
            rows = slice(i * 256, (i + 1) * 256)
            if t < 3:
                swap_copy(t + 1, i).wait_send()
            part = mm(slope[rows, 0:FRONT], up_first[...], ((1,), (1,)))
            part = part + mm(slope[rows, FRONT:], up_second[...])
            part_out[rows, :] = part.astype(BF)
            swap_copy(t, i).start()
        for i in range(3):
            rows = slice(i * 256, (i + 1) * 256)
            sums[0][t, rows, :] = mm(h_f[:, rows], slope[:, 0:FRONT], ((0,), (0,))).astype(BF)
        sums[1][t, 0:HALF, :] = mm(slope[:, FRONT:], h_f[...], ((0,), (0,))).astype(BF)

    def attention_pair(i, unused):
        lane = lax.broadcasted_iota(jnp.int32, (1, 128), 1)
        base = pl.multiple_of(i * 384, 128)
        q_at, k_at, v_at = (
            pl.ds(base, 128),
            pl.ds(pl.multiple_of(base + 128, 128), 128),
            pl.ds(pl.multiple_of(base + 256, 128), 128),
        )
        c_at = pl.ds(pl.multiple_of(i * 128, 128), 128)
        for which, (begin, size) in enumerate(BLOCKS):
            chunk = size
            span = slice(begin, begin + size)
            k = qkv[span, k_at]
            v = qkv[span, v_at]
            dk = jnp.zeros((size, 128), F32)
            dv = jnp.zeros((size, 128), F32)
            for at in range(begin, begin + size, chunk):
                rows = slice(at, at + chunk)
                q = qkv[rows, q_at]
                dcs = dc[rows, c_at]
                dq = None
                for head in range(2):
                    own = (lane < 64) if head == 0 else (lane >= 64)
                    qm = jnp.where(own, q, jnp.zeros_like(q)) * BF(0.125)
                    dcm = jnp.where(own, dcs, jnp.zeros_like(dcs))
                    km = jnp.where(own, k, jnp.zeros_like(k))
                    score = mm(k, qm, ((1,), (1,)))
                    if which != 1:
                        score = jnp.where(block_mask(which, bound_ref[0:1, 0:1], size), score, MASKED)
                    p = jnp.exp(score - lse[i, head : head + 1, rows])
                    dp = mm(v, dcm, ((1,), (1,)))
                    inner = jnp.sum(p * dp, axis=0, keepdims=True)
                    ds = (p * (dp - inner)).astype(BF)
                    dv = dv + mm(p.astype(BF), dcm)
                    dk = dk + mm(ds, qm)
                    part = mm(km, ds, ((0,), (0,)))
                    dq = part if dq is None else dq + part
                qkv[rows, q_at] = (dq.T * 0.125).astype(BF)
            qkv[span, k_at] = dk.astype(BF)
            qkv[span, v_at] = dv.astype(BF)
        return unused

    def attention_grads(l):
        t = 2 * l
        sums[1][t, 0:HALF, :] = mm(ctx[...], dy[...], ((0,), (0,))).astype(BF)
        send_block(1, t, 0, SIDE)
        for i in range(3):
            rows = slice(i * 256, (i + 1) * 256)
            dc[rows, :] = mm(dy[rows, :], att_second[...], ((1,), (1,))).astype(BF)
        lax.fori_loop(0, PAIRS, attention_pair, 0)
        for i in range(3):
            rows = slice(i * 256, (i + 1) * 256)
            swap_copy(t + 1, i).wait_send()
            part_out[rows, :] = mm(qkv[rows, :], att_first[...], ((1,), (1,))).astype(BF)
            swap_copy(t, i).start()
        for i in range(3):
            rows = slice(i * 256, (i + 1) * 256)
            sums[0][t, rows, :] = mm(h_a[:, rows], qkv[...], ((0,), (0,))).astype(BF)

    def send_sections(t):
        if t % 2 == 1:
            send_block(1, t, 0, SIDE)
        send_block(0, t, 0, D)

    def came_one(which, chunk, l):
        one(which, chunk, l).wait_recv()

    def start_two(which, chunk):
        rows = rows_of(which, chunk)
        t = forwarded(which)
        if STREAMS[which][3]:
            came_one(which, chunk, 0)
            came_one(which, chunk, 1)
            got = ones[which][1 - half, rows, :]
        else:
            came_one(which, chunk, 0)
            came_one(which, chunk, 1)
            got = ones[which][1 - parity, rows, :]
        sums[which][t, rows, :] = plus(sums[which][t, rows, :], got).astype(BF)
        two(which, chunk).start()

    wait(loads_ffn(1))
    norm_back(3, grad_from_head, xhat_f, scale_f)
    ffn_back(1)
    send_sections(3)
    start(loads_ffn(0))
    start(ring(0, 0))
    start(ring(0, 1))
    wait(loads_attention(1))
    norm_back(2, grad_from(3), xhat_a, scale_a)
    attention_grads(1)
    send_sections(2)
    start(loads_attention(0))
    wait(loads_ffn(0))
    norm_back(1, grad_from(2), xhat_f, scale_f)
    ffn_back(0)
    send_sections(1)
    wait(loads_attention(0))
    norm_back(0, grad_from(1), xhat_a, scale_a)

    attention_grads(0)
    send_sections(0)

    for i in range(3):
        swap_copy(0, i).wait_recv()

        def body(j, unused):
            rows = pl.ds(pl.multiple_of(j * 64, 64), 64)
            dy[rows, :] = plus(dy[rows, :], part_out[rows, :], part_in[0, rows, :]).astype(BF)
            return unused

        lax.fori_loop(4 * i, 4 * i + 4, body, 0)
    back = -bound_ref[1:2, 0:1]
    for i in range(6):
        rows = slice(i * 128, (i + 1) * 128)
        if i == 0:
            total = dy[rows, :].astype(F32)
        else:
            total = mm(rotation(i - 1, back), dy[QROWS:, :])
        shares[:, rows] = total.T.astype(BF)

    def features(section):
        size = out_back.shape[1]
        return shares.at[pl.ds(pl.multiple_of(section * size, 16), size), :]

    def back_to(i, to):
        return pltpu.make_async_remote_copy(
            src_ref=features(to),
            dst_ref=out_back.at[i],
            send_sem=in_send.at[i],
            recv_sem=in_recv.at[i],
            device_id=(to, b),
            device_id_type=MESH,
        )

    own_share = pltpu.make_async_copy(features(s), out_back.at[3], in_send.at[3])
    own_share.start()

    @pl.when(mine)
    def _():
        for i, to in enumerate((x, y, xy)):
            back_to(i, to).start()

    def start_z(which, chunk):
        rows = rows_of(which, chunk)
        two(which, chunk).wait_recv()
        got = ones[which][half if STREAMS[which][3] else parity, rows, :]
        total = plus(sums[which][s, rows, :], got, twos[which][rows, :])
        if layers == 1:
            sums[which][s, rows, :] = total.astype(BF)
            twin_copy(which, chunk, True).start()
            keep_copy(which, chunk, True).start()
            return
        if middle > 0:

            @pl.when(depth > 0)
            def _():
                inward(which, chunk, False).wait_recv()
                sums[which][s, rows, :] = plus(total, ins[which][rows, :]).astype(BF)

            @pl.when(depth == 0)
            def _():
                sums[which][s, rows, :] = total.astype(BF)

            @pl.when(depth < middle)
            def _():
                inward(which, chunk, False).start()

        else:
            sums[which][s, rows, :] = total.astype(BF)

        @pl.when(depth == middle)
        def _():
            inward(which, chunk, True).start()

    def finish(which, chunk):
        rows = rows_of(which, chunk)
        inward(which, chunk, True).wait_recv()

        @pl.when(depth == middle)
        def _():
            inward(which, chunk, True).wait_send()
            sums[which][s, rows, :] = plus(
                sums[which][s, rows, :], backs[which][rows, :]
            ).astype(BF)
            if middle > 0:
                outward_copy(which, chunk, True).start()
            twin_copy(which, chunk, True).start()
            keep_copy(which, chunk, True).start()

        if middle > 0:

            @pl.when(depth < middle)
            def _():
                @pl.when(depth > 0)
                def _():
                    outward_copy(which, chunk, False).start()

                twin_copy(which, chunk, False).start()
                keep_copy(which, chunk, False).start()

    lag3 = lag_z + lag_step * depth
    lag5 = lag_z + lag_step * (middle + 1) + lag_step * (middle - depth)
    slots = sum(CHUNKS) + lag_z + (lag_step * (2 * middle + 1) if layers > 1 else 0)

    def guarded(position, step):
        for which, count in enumerate(CHUNKS):
            chunk = position - OFFSETS[which]

            @pl.when((chunk >= 0) & (chunk < count))
            def _():
                step(which, chunk)

    def slot(k, unused):
        guarded(k, start_two)
        guarded(k - lag3, start_z)
        if layers > 1:
            guarded(k - lag5, finish)
        return unused

    lax.fori_loop(0, slots, slot, 0)

    def drain(which, chunk):
        twin_copy(which, chunk, True).wait_recv()
        twin_copy(which, chunk, True).wait_send()
        keep_copy(which, chunk, True).wait()
        if STREAMS[which][3]:
            one(which, chunk, 0).wait_send()
            one(which, chunk, 1).wait_send()
        else:
            one(which, chunk, 0).wait_send()
            one(which, chunk, 1).wait_send()
        two(which, chunk).wait_send()
        if layers > 1 and middle > 0:

            @pl.when(depth < middle)
            def _():
                inward(which, chunk, False).wait_send()

            @pl.when(depth > 0)
            def _():
                outward_copy(which, chunk, True).wait_send()

    def last(k, unused):
        guarded(k, drain)
        return unused

    lax.fori_loop(0, sum(CHUNKS), last, 0)
    for i in range(3):
        swap_copy(0, i).wait_send()
    own_share.wait()

    @pl.when(mine)
    def _():
        for i, to in enumerate((x, y, xy)):
            back_to(i, to).wait_send()
        back_to(1, y).wait_recv()

    @pl.when(jnp.logical_not(mine))
    def _():
        back_to(0, x).wait_recv()
        back_to(2, xy).wait_recv()


def backward(first_all, rest_all, vec, kept, dw, tails, bound, width, layers, lags=(2, 2)):
    anywhere = pl.BlockSpec(memory_space=pl.ANY)
    inside = pl.BlockSpec(memory_space=pltpu.VMEM)
    shapes = [(rows, columns) for rows, columns, unused, unused2 in STREAMS]
    most = max(CHUNKS)
    return pl.pallas_call(
        partial(backward_kernel, layers, lags),
        in_specs=[anywhere] * 11 + [inside] * 3,
        out_specs=[anywhere] * 4,
        out_shape=[jax.ShapeDtypeStruct((2,) + shape, BF) for shape in shapes]
        + [jax.ShapeDtypeStruct((4, width, ROWS), BF)],
        scratch_shapes=[pltpu.VMEM((4,) + shape, BF) for shape in shapes]
        + [pltpu.VMEM((2,) + shape, BF) for shape in shapes]
        + [pltpu.VMEM(shape, BF) for shape in shapes] * 3
        + [
            pltpu.VMEM((ROWS, D), BF),
            pltpu.VMEM((ROWS, D), BF),
            pltpu.VMEM((ROWS, 128), F32),
            pltpu.VMEM((ROWS, 2 * D), BF),
            pltpu.VMEM((D, FRONT), BF),
            pltpu.VMEM((HALF, D), BF),
            pltpu.VMEM((2, ROWS, HALF), BF),
            pltpu.VMEM((2, HALF, D), BF),
            pltpu.VMEM((ROWS, D), BF),
            pltpu.VMEM((ROWS, D), BF),
            pltpu.VMEM((ROWS, 128), F32),
            pltpu.VMEM((ROWS, FRONT), BF),
            pltpu.VMEM((ROWS, HALF), BF),
            pltpu.VMEM((PAIRS, 8, ROWS), F32),
            pltpu.VMEM((D, FRONT), BF),
            pltpu.VMEM((HALF, D), BF),
            pltpu.VMEM((4 * EXTRA, D), BF),
            pltpu.VMEM((ROWS, D), BF),
            pltpu.VMEM((ROWS, HALF), BF),
            pltpu.VMEM((ROWS, D), BF),
            pltpu.VMEM((2, ROWS, D), BF),
            pltpu.VMEM((D, ROWS), BF),
            pltpu.SemaphoreType.DMA((22,)),
            pltpu.SemaphoreType.DMA((2, 2)),
            pltpu.SemaphoreType.DMA((4, 3)),
            pltpu.SemaphoreType.DMA((4, 3)),
            pltpu.SemaphoreType.DMA((18, most)),
            pltpu.SemaphoreType.DMA((18, most)),
            pltpu.SemaphoreType.DMA((3, most)),
            pltpu.SemaphoreType.DMA((4,)),
            pltpu.SemaphoreType.DMA((4,)),
        ],
        compiler_params=pltpu.CompilerParams(
            collective_id=2, has_side_effects=True, vmem_limit_bytes=62 * 1024 * 1024
        ),
    )(first_all, rest_all, *kept, tails, bound, vec, dw)


def assemble_kernel(
    queries_all,
    first_ref,
    side_ref,
    down_ref,
    back_ref,
    out_ref,
    down_out,
    input_out,
    bias_out,
    gain_out,
    shift_out,
    projection_out,
    loss_out,
):
    s, b = lax.axis_index("section"), lax.axis_index("batch")
    row = pl.program_id(0)

    @pl.when(s % 2 == 0)
    def _():
        for core in range(2):
            for i in range(PAIRS):
                for t in range(3):
                    to = t * D + core * HALF + i * 128
                    at = (3 * i + t) * 128
                    out_ref[:, to : to + 128] = first_ref[core, :, at : at + 128].astype(F32)
        from_core = row // 3
        at = pl.multiple_of((row % 3) * 128, 128)
        out_ref[:, 3 * D :] = side_ref[from_core, pl.ds(at, 128), :].astype(F32)

    @pl.when(s % 2 == 1)
    def _():
        lanes = pl.ds(pl.multiple_of(row * 128, 128), 128)
        for core in range(2):
            out_ref[:, core * D : (core + 1) * D] = first_ref[core, :, 0:D].astype(F32)
            at = 2 * D + core * D
            out_ref[:, at : at + HALF] = first_ref[core, :, D:].astype(F32)
            out_ref[:, at + HALF : at + D] = side_ref[core, 0:HALF, lanes].astype(F32).T

    down_out[...] = down_ref[...].astype(F32)
    mine = b % 2 == s % 2
    same = jnp.where(mine, back_ref[3].astype(F32), back_ref[0].astype(F32))
    other = jnp.where(mine, back_ref[1].astype(F32), back_ref[2].astype(F32))
    for m in range(2):
        input_out[m] = jnp.where(s // 2 == m, same, other)

    @pl.when(row == 0)
    def _():
        vectors = side_ref[0, HALF : HALF + 16, :].astype(F32)
        bias_out[...] = vectors[0:1]
        gain_out[...] = vectors[1:2]
        shift_out[...] = vectors[2:3]
        loss_out[...] = jnp.sum(vectors[3:4], axis=1, keepdims=True) * (1.0 / queries_all)
        projection_out[...] = side_ref[0, HALF + 16 :, :].astype(F32)


def assemble(first_sum, side_sum, down_sum, back, queries_all):
    width = back.shape[1]
    steps = D // 128

    def whole(shape):
        return pl.BlockSpec(shape, lambda i: (0,) * len(shape))

    return pl.pallas_call(
        partial(assemble_kernel, queries_all),
        grid=(steps,),
        in_specs=[
            pl.BlockSpec((2, 128, FRONT), lambda i: (0, i, 0)),
            whole((2, SIDE, D)),
            pl.BlockSpec((256, D), lambda i: (i, 0)),
            pl.BlockSpec((4, width, 128), lambda i: (0, 0, i)),
        ],
        out_specs=[
            pl.BlockSpec((128, 4 * D), lambda i: (i, 0)),
            pl.BlockSpec((256, D), lambda i: (i, 0)),
            pl.BlockSpec((2, width, 128), lambda i: (0, 0, i)),
            whole((1, D)),
            whole((1, D)),
            whole((1, D)),
            whole((EXTRA, D)),
            whole((1, 1)),
        ],
        out_shape=[
            jax.ShapeDtypeStruct(shape, F32)
            for shape in (
                (D, 4 * D),
                (2 * D, D),
                (2, width, ROWS),
                (1, D),
                (1, D),
                (1, D),
                (EXTRA, D),
                (1, 1),
            )
        ],
        compiler_params=pltpu.CompilerParams(vmem_limit_bytes=60 * 1024 * 1024),
    )(first_sum, side_sum, down_sum.reshape(2 * D, D), back)


def gelu_and_slope(z):
    upper = 0.5 * (1.0 + lax.erf(z * 0.7071067811865476))
    density = jnp.exp(-0.5 * z * z) * 0.3989422804014327
    return (z * upper).astype(BF), (upper + z * density).astype(BF)


def on_device(
    inputs,
    in_weight,
    down_weight,
    out_bias,
    norm_gains,
    norm_shifts,
    projection,
    passage_lengths,
    positive,
):
    batches = lax.axis_size("batch")
    layers = batches // 2
    queries_all = inputs.shape[0] * batches * QUERY_COUNT
    first_all, rest_all, vectors, *kept, dw, tails, bound = forward(
        in_weight[0],
        down_weight,
        inputs.transpose(0, 2, 1),
        projection.T,
        (out_bias, norm_gains, norm_shifts),
        passage_lengths[:, 0],
        positive,
        layers,
        queries_all,
    )
    first_sum, side_sum, down_sum, back = backward(
        first_all, rest_all, vectors, kept, dw, tails, bound, inputs.shape[2], layers
    )
    in_grad, down_grad, input_grad, bias_grad, gain_grad, shift_grad, projection_grad, loss = (
        assemble(first_sum, side_sum, down_sum, back, queries_all)
    )
    return (
        loss[0, 0],
        input_grad.transpose(0, 2, 1),
        in_grad[None],
        down_grad,
        bias_grad,
        gain_grad,
        shift_grad,
        projection_grad.T,
    )


def solution(mesh):
    in_specs = (
        P(None, "batch", "section"),
        P("section", None, None),
        P("section", None),
        P("section", None),
        P("section", None),
        P("section", None),
        P(None, "section"),
        P(None, "batch", None),
        P(None, "batch"),
    )
    out_specs = (
        P(),
        P(None, "batch", "section"),
        P("section", None, None),
        P("section", None),
        P("section", None),
        P("section", None),
        P("section", None),
        P(None, "section"),
    )
    return jax.shard_map(
        on_device, mesh=mesh, in_specs=in_specs, out_specs=out_specs, check_vma=False
    )
```

```python
from functools import partial

import jax
import jax.numpy as jnp
from jax import lax
from jax.experimental import pallas as pl
from jax.experimental.pallas import tpu as pltpu
from jax.sharding import PartitionSpec as P

D = 768
HEADS = 12
FF = 3072
DIM = 128
QUERY_LENGTH = 32
QUERY_COUNT = 4
PASSAGE_COUNT = 3
PASSAGE_TOKENS = 640
PLEN = 512
QROWS = QUERY_LENGTH * QUERY_COUNT
ROWS = QROWS + PASSAGE_TOKENS
REST = PASSAGE_TOKENS - PLEN
SOFTMAX_DIVISOR = 0.1
SIMILARITY_SCALE = 0.25
NORM_EPSILON = 1e-06
MASKED = -1000000000.0
BF = jnp.bfloat16
F32 = jnp.float32
BLOCKS = ((0, QROWS), (QROWS, PLEN), (QROWS + PLEN, REST))
PAIRS = HEADS // 4
HALF = D // 2


def mm(a, b, dims=((1,), (0,))):
    return lax.dot_general(a, b, (dims, ((), ())), preferred_element_type=F32)


def block_mask(which, bound, rows):
    t = lax.broadcasted_iota(jnp.int32, (rows, rows), 0)
    r = lax.broadcasted_iota(jnp.int32, (rows, rows), 1)
    if which == 0:
        return (t // QUERY_LENGTH) == (r // QUERY_LENGTH)
    return ((t.astype(F32) < bound).astype(F32) - (r.astype(F32) < bound).astype(F32)) == 0.0


def unit_matrix(n):
    r = lax.broadcasted_iota(jnp.int32, (n, n), 0)
    c = lax.broadcasted_iota(jnp.int32, (n, n), 1)
    return (r == c).astype(F32).astype(BF)


def rotation(i, begins):
    r = lax.broadcasted_iota(jnp.int32, (128, PASSAGE_TOKENS), 0).astype(F32) + float(i * 128)
    c = lax.broadcasted_iota(jnp.int32, (128, PASSAGE_TOKENS), 1).astype(F32)
    ahead = c - r - begins
    total = float(PASSAGE_TOKENS)
    return ((ahead == 0.0) | (ahead == -total) | (ahead == total)).astype(F32).astype(BF)


MESH = pl.DeviceIdType.MESH
EXTRA = 32
FRONT = 1152
SPREAD = 960


def neighbours():
    s, b = lax.axis_index("section"), lax.axis_index("batch")
    x = s + 1 - 2 * (s % 2)
    y = s + 2 - 4 * (s // 2)
    xy = 3 - s
    return s, b, x, y, xy


def greet(layers):
    s, b, x, y, xy = neighbours()
    z, core = b // 2, b % 2
    barrier = pltpu.get_barrier_semaphore()

    def signal(to):
        pl.semaphore_signal(barrier, inc=1, device_id=to, device_id_type=MESH)

    signal((x, b))
    signal((y, b))
    signal((xy, b))
    signal((s, b + 1 - 2 * core))
    if layers > 1:

        @pl.when(z > 0)
        def _():
            signal((s, b - 2))

        @pl.when(z < layers - 1)
        def _():
            signal((s, b + 2))

        ends = (layers - 1 - z) // (layers - 1) + z // (layers - 1)
        pl.semaphore_wait(barrier, 6 - ends)
    else:
        pl.semaphore_wait(barrier, 4)


def forward_kernel(layers, spread, queries_all, *refs):
    w_ref, down_ref, slices_ref, projection_ref = refs[0:4]
    bias_ref, gain_ref, shift_ref, lengths_ref, positive_ref = refs[4:9]
    first_out, rest_out, vec_out, h_out, xhat_out, scale_out, qkv_out, ctx_out = refs[9:17]
    lse_out, act_out, slope_out, dw_out, tails_out, bound_out = refs[17:23]
    (
        first_all,
        rest_all,
        vec_all,
        tokens,
        ints_ref,
        ints_other,
        vec_ref,
        wide,
        out_stage,
        down_stage,
        hs,
        xhats,
        scales,
        qkvs,
        ctxs,
        lses,
        acts,
        slopes,
        part_out,
        part_in,
        proj,
        embedded,
        unit,
        length,
        grad_unit,
        grad_low,
        tails,
        load_sem,
        send_sem,
        recv_sem,
        z_send,
        z_recv,
        in_send,
        in_recv,
        part_send,
        part_recv,
        save_sem,
    ) = refs[23:]
    s, b, x, y, xy = neighbours()
    z, core = b // 2, b % 2
    micro = s // 2
    mine = core == s % 2
    twin = b + 1 - 2 * core

    def load(src, dst, i):
        return pltpu.make_async_copy(src, dst, load_sem.at[i])

    loads = [load(down_ref.at[pl.ds(core * D, D), :], down_stage, 0)]
    even, odd = [], []
    for i in range(PAIRS):
        for t in range(3):
            at = pl.multiple_of(t * D + core * HALF + i * 128, 128)
            to = (3 * i + t) * 128
            even.append(
                load(w_ref.at[:, pl.ds(at, 128)], wide.at[:, pl.ds(to, 128)], 1 + 3 * i + t)
            )
    even.append(load(w_ref.at[pl.ds(core * HALF, HALF), pl.ds(3 * D, D)], out_stage, 10))
    for i in range(2):
        at = pl.multiple_of(i * 2 * D + core * D, 128)
        odd.append(load(w_ref.at[:, pl.ds(at, D)], wide.at[:, pl.ds(i * D, D)], 11 + i))
    loads[0].start()

    @pl.when(s % 2 == 0)
    def _():
        for copy in even:
            copy.start()

    @pl.when(s % 2 == 1)
    def _():
        for copy in odd:
            copy.start()

    first, rest = first_all.at[s], rest_all.at[s]
    ints_ref[...] = jnp.zeros_like(ints_ref)
    ints_ref[0:2, 0:PASSAGE_COUNT] = lengths_ref[...]
    ints_ref[8:10, 0:QUERY_COUNT] = positive_ref[...]
    vec_ref[0:1, :] = bias_ref[...]
    vec_ref[1:2, :] = gain_ref[...]
    vec_ref[2:3, :] = shift_ref[...]
    vec_ref[3:8, :] = jnp.zeros((5, D), F32)
    own_vec = pltpu.make_async_copy(vec_ref, vec_all.at[s], load_sem.at[15])
    own_vec.start()
    rest[FRONT : FRONT + EXTRA, :] = projection_ref[...].astype(BF)
    greet(layers)

    def features(section):
        size = slices_ref.shape[1]
        return tokens.at[pl.ds(pl.multiple_of(section * size, 16), size), :]

    def feature_copy(i, which, section, to):
        return pltpu.make_async_remote_copy(
            src_ref=slices_ref.at[which],
            dst_ref=features(section),
            send_sem=in_send.at[i],
            recv_sem=in_recv.at[i],
            device_id=(to, b),
            device_id_type=MESH,
        )

    def to_twin(i, src, dst):
        return pltpu.make_async_remote_copy(
            src_ref=src,
            dst_ref=dst,
            send_sem=in_send.at[i],
            recv_sem=in_recv.at[i],
            device_id=(s, twin),
            device_id_type=MESH,
        )

    def quarter_to_twin(i, f):
        return to_twin(i, features(f), features(f))

    swap_ints = to_twin(7, ints_ref, ints_other)
    own_quarter = pltpu.make_async_copy(slices_ref.at[micro], features(s), load_sem.at[14])
    swap_ints.start()

    def send_features():
        @pl.when(mine)
        def _():
            own_quarter.start()
            feature_copy(1, 1 - micro, s, y).start()

        @pl.when(jnp.logical_not(mine))
        def _():
            feature_copy(0, micro, s, x).start()
            feature_copy(2, 1 - micro, s, xy).start()

    loads[0].wait()

    @pl.loop(0, D // 96)
    def _(i):
        rows = pl.ds(pl.multiple_of(i * 96, 16), 96)
        to = pl.ds(pl.multiple_of(HALF + i * 96, 16), 96)
        rest[to, :] = down_stage[rows, :].astype(BF)

    @pl.when(s % 2 == 0)
    def _():
        for copy in even:
            copy.wait()

        @pl.loop(0, HALF // 96)
        def _(i):
            rows = pl.ds(pl.multiple_of(i * 96, 16), 96)
            rest[rows, :] = out_stage[rows, :].astype(BF)

    @pl.when(s % 2 == 1)
    def _():
        for copy in odd:
            copy.wait()
        for i in range(3):
            for j in range(6):
                block = wide[j * 128 : (j + 1) * 128, FRONT + i * 128 : FRONT + (i + 1) * 128]
                rest[i * 128 : (i + 1) * 128, j * 128 : (j + 1) * 128] = block.T.astype(BF)

    quarter = D // 4
    firsts = [(first, first_all, i * quarter, quarter, i < 2) for i in range(4)]
    seconds = [(rest, rest_all, i * 96, 96, i == 0) for i in range(2)]
    small = [
        (rest, rest_all, FRONT, EXTRA, True),
        (vec_ref, vec_all, 0, 8, False),
    ]
    if spread:
        share = SPREAD // layers
        at = pl.multiple_of(FRONT - SPREAD + z * share, 16)
        half = share // 32 * 16
        slices = [
            (rest, rest_all, at, half, True),
            (rest, rest_all, pl.multiple_of(at + half, 16), share - half, False),
        ]
    else:
        slices = []
        seconds = [(rest, rest_all, i * 192, 192, i % 2 == 0) for i in range(6)]
    pieces = slices + firsts + seconds + small

    def part(n, ref):
        unused, unused, row, rows, unused = pieces[n]
        return ref.at[pl.ds(row, rows), :]

    def remote(n, kind, src, dst, to):
        return pltpu.make_async_remote_copy(
            src_ref=src,
            dst_ref=dst,
            send_sem=send_sem.at[kind, n],
            recv_sem=recv_sem.at[kind, n],
            device_id=(to, b),
            device_id_type=MESH,
        )

    def direct(n, kind):
        mine, every = pieces[n][:2]
        return remote(n, kind, part(n, mine), part(n, every.at[s]), y if kind else x)

    def arrived(n, kind):
        every = pieces[n][1]
        owner = (x, y, xy)[kind]
        here = part(n, every.at[owner])
        remote(n, kind, here, here, x).wait_recv()

    def relay(n):
        every, by_x = pieces[n][1], pieces[n][4]
        source = part(n, every.at[x if by_x else y])
        return remote(n, 2, source, source, y if by_x else x)

    def pass_on(n):
        arrived(n, 0 if pieces[n][4] else 1)
        relay(n).start()

    count = len(pieces)
    front = list(range(len(slices), len(slices) + 4))
    behind = list(range(len(slices) + 4, count))

    def along_x(n):
        direct(n, 0).start()

    def along_y(n):
        direct(n, 1).start()

    z_width = SPREAD // layers if spread else 0

    def z_part(section, owner_z):
        at = pl.multiple_of(FRONT - SPREAD + owner_z * z_width, 16)
        return rest_all.at[section, pl.ds(at, z_width), :]

    def z_copy(way, step, k, owner_z, to_b):
        source = z_part((x, y, xy)[k], owner_z)
        return pltpu.make_async_remote_copy(
            src_ref=source,
            dst_ref=source,
            send_sem=z_send.at[way, step, k],
            recv_sem=z_recv.at[way, step, k],
            device_id=(s, to_b),
            device_id_type=MESH,
        )

    def z_first(k):
        @pl.when(z < layers - 1)
        def _():
            z_copy(0, 0, k, z, b + 2).start()

        @pl.when(z > 0)
        def _():
            z_copy(1, 0, k, z, b - 2).start()

    def z_step(step):
        @pl.when(z >= step)
        def _():
            for k in range(3):
                z_copy(0, step - 1, k, z - step, b).wait_recv()

                @pl.when(z < layers - 1)
                def _():
                    z_copy(0, step, k, z - step, b + 2).start()

        @pl.when(z < layers - step)
        def _():
            for k in range(3):
                z_copy(1, step - 1, k, z + step, b).wait_recv()

                @pl.when(z > 0)
                def _():
                    z_copy(1, step, k, z + step, b - 2).start()

    def z_drain():
        for step in range(layers - 1):

            @pl.when((z < layers - 1) & (z >= step))
            def _():
                for k in range(3):
                    z_copy(0, step, k, z - step, b + 2).wait_send()

            @pl.when((z > 0) & (z + step < layers))
            def _():
                for k in range(3):
                    z_copy(1, step, k, z + step, b - 2).wait_send()

    for n in range(len(slices)):
        along_x(n)
        along_y(n)
    send_features()
    @pl.loop(0, D // 96)
    def _(i):
        rows = pl.ds(pl.multiple_of(i * 96, 16), 96)
        first[rows, :] = wide[rows, 0:FRONT].astype(BF)


    along_x(front[0])
    along_y(front[2])

    if spread:
        pass_on(0)
        pass_on(1)
    along_x(front[1])
    along_y(front[3])
    if spread:
        arrived(0, 1)
        arrived(1, 0)
        z_first(0)
        z_first(1)
    @pl.when(mine)
    def _():
        own_quarter.wait()
        quarter_to_twin(3, s).start()
        for i, owner in enumerate((x, y, xy)):
            feature_copy(i, 0, owner, x).wait_recv()
            quarter_to_twin(4 + i, owner).start()

    pass_on(front[0])
    pass_on(front[2])
    along_x(front[2])
    along_y(front[0])
    if spread:
        arrived(0, 2)
        arrived(1, 2)
        z_first(2)
    pass_on(front[1])
    pass_on(front[3])
    along_x(front[3])
    along_y(front[1])
    z_at = 1
    if spread and z_at < layers - 1:
        z_step(z_at)
        z_at += 1
    for n in behind:
        if pieces[n][4]:
            along_x(n)
        else:
            along_y(n)
    for n in behind:
        if pieces[n][4]:
            along_y(n)
        else:
            along_x(n)
    arrived(front[0], 1)
    arrived(front[2], 0)
    while spread and z_at < layers - 1:
        z_step(z_at)
        z_at += 1
    arrived(front[1], 1)
    arrived(front[3], 0)
    for n in front:
        arrived(n, 2)
    swap_ints.wait()
    own_vec.wait()

    @pl.when(jnp.logical_not(mine))
    def _():
        for i, owner in enumerate((s, x, y, xy)):
            quarter_to_twin(3 + i, owner).wait_recv()

    lane = lax.broadcasted_iota(jnp.int32, (1, 128), 1)

    def entry(first_row, i):
        row = pl.ds(first_row + micro, 1)
        values = jnp.where(mine, ints_ref[row, :].astype(F32), ints_other[row, :].astype(F32))
        return jnp.sum(jnp.where(lane == i, values, 0.0), axis=1, keepdims=True)

    sizes = [entry(0, i) for i in range(PASSAGE_COUNT)]
    is_long = [
        (sizes[0] == float(PLEN)).astype(F32),
        (sizes[1] == float(PLEN)).astype(F32),
        (sizes[2] == float(PLEN)).astype(F32),
    ]
    bound = is_long[0] * sizes[1] + is_long[1] * sizes[2] + is_long[2] * sizes[0]
    long_index = is_long[1] + 2.0 * is_long[2]
    begins = is_long[1] * sizes[0] + is_long[2] * (sizes[0] + sizes[1])

    saves = []

    def save(src, dst):
        copy = pltpu.make_async_copy(src, dst, save_sem.at[len(saves)])
        copy.start()
        saves.append(copy)

    save(first_all, first_out)

    def swap_copy(t, i):
        rows = pl.ds(i * 256, 256)
        return pltpu.make_async_remote_copy(
            src_ref=part_out.at[rows, :],
            dst_ref=part_in.at[t % 2, rows, :],
            send_sem=part_send.at[t, i],
            recv_sem=part_recv.at[t, i],
            device_id=(s, twin),
            device_id_type=MESH,
        )

    hs[0, 0:QROWS, :] = mm(unit_matrix(QROWS), tokens[:, 0:QROWS], ((1,), (1,))).astype(BF)
    for i in range(PASSAGE_TOKENS // 128):
        rows = slice(QROWS + i * 128, QROWS + (i + 1) * 128)
        hs[0, rows, :] = mm(rotation(i, begins), tokens[:, QROWS:], ((1,), (1,))).astype(BF)
    save(hs.at[0], h_out.at[0])

    def norm_rows(t, i):
        bias, gain, shift = vec_all[t, 0:1, :], vec_all[t, 1:2, :], vec_all[t, 2:3, :]
        swap_copy(t, i).wait_recv()

        def body(j, unused):
            rows = pl.ds(pl.multiple_of(j * 128, 128), 128)
            u = (
                hs[t, rows, :].astype(F32)
                + part_out[rows, :].astype(F32)
                + part_in[t % 2, rows, :].astype(F32)
                + bias
            )
            centered = u - jnp.mean(u, -1, keepdims=True)
            scale = lax.rsqrt(jnp.mean(centered * centered, -1, keepdims=True) + NORM_EPSILON)
            xhat = centered * scale
            xhats[t, rows, :] = xhat.astype(BF)
            scales[t, rows, :] = jnp.broadcast_to(scale, (128, 128))
            hs[t + 1, rows, :] = (xhat * gain + shift).astype(BF)
            return unused

        lax.fori_loop(2 * i, 2 * i + 2, body, 0)

    def save_norm(t):
        save(xhats.at[t], xhat_out.at[t])
        save(scales.at[t], scale_out.at[t])
        if t < 3:
            save(hs.at[t + 1], h_out.at[t + 1])

    def attention_pair(l):
        def pair(i, unused):
            base = pl.multiple_of(i * 384, 128)
            q_at = pl.ds(base, 128)
            k_at = pl.ds(pl.multiple_of(base + 128, 128), 128)
            v_at = pl.ds(pl.multiple_of(base + 256, 128), 128)
            c_at = pl.ds(pl.multiple_of(i * 128, 128), 128)
            for which, (begin, size) in enumerate(BLOCKS):
                chunk = size
                span = slice(begin, begin + size)
                k = qkvs[l, span, k_at]
                v = qkvs[l, span, v_at]
                for at in range(begin, begin + size, chunk):
                    rows = slice(at, at + chunk)
                    q = qkvs[l, rows, q_at]
                    total = None
                    for head in range(2):
                        own = (lane < 64) if head == 0 else (lane >= 64)
                        qm = jnp.where(own, q, jnp.zeros_like(q)) * BF(0.125)
                        vm = jnp.where(own, v, jnp.zeros_like(v))
                        score = mm(k, qm, ((1,), (1,)))
                        if which != 1:
                            score = jnp.where(block_mask(which, bound, size), score, MASKED)
                        top = jnp.max(score, axis=0, keepdims=True)
                        e = jnp.exp(score - top)
                        weight = jnp.sum(e, axis=0, keepdims=True)
                        part = mm(vm, e.astype(BF), ((0,), (0,))) * (1.0 / weight)
                        total = part if total is None else total + part
                        lses[l, i, head : head + 1, rows] = top + jnp.log(weight)
                    ctxs[l, rows, c_at] = total.T.astype(BF)
            return unused

        lax.fori_loop(0, PAIRS, pair, 0)

    def attention_layer(l):
        t = 2 * l
        for i in range(3):
            rows = slice(i * 256, (i + 1) * 256)
            if t > 0:
                norm_rows(t - 1, i)
            qkvs[l, rows, :] = mm(hs[t, rows, :], first_all[t]).astype(BF)
        if t > 0:
            save_norm(t - 1)
        save(qkvs.at[l], qkv_out.at[l])
        if l == 0:
            for n in behind:
                pass_on(n)
        attention_pair(l)
        if l == 0:
            for n in behind:
                arrived(n, 1 if pieces[n][4] else 0)
                arrived(n, 2)
            if spread:
                z_step(layers - 1)
        save(ctxs.at[l], ctx_out.at[l])
        save(lses.at[l], lse_out.at[l])
        for i in range(3):
            rows = slice(i * 256, (i + 1) * 256)
            if t > 0:
                swap_copy(t - 1, i).wait_send()
            part_out[rows, :] = mm(ctxs[l, rows, :], rest_all[t, 0:HALF, :]).astype(BF)
            swap_copy(t, i).start()

    def ffn_layer(l):
        t = 2 * l + 1
        for i in range(3):
            rows = slice(i * 256, (i + 1) * 256)
            norm_rows(t - 1, i)
            x_rows = hs[t, rows, :]
            for j in range(4):
                columns = slice(j * HALF, (j + 1) * HALF)
                if j < 3:
                    value = mm(x_rows, first_all[t, :, columns])
                else:
                    value = mm(x_rows, rest_all[t, 0:HALF, :], ((1,), (1,)))
                act, slope = gelu_and_slope(value)
                acts[l, rows, columns] = act
                slopes[l, rows, columns] = slope
            swap_copy(t - 1, i).wait_send()
            part = mm(acts[l, rows, 0:D], rest_all[2 * l, HALF:FRONT, :])
            part = part + mm(acts[l, rows, D:], rest_all[2 * l + 1, HALF:FRONT, :])
            part_out[rows, :] = part.astype(BF)
            swap_copy(t, i).start()
        save_norm(t - 1)
        save(acts.at[l], act_out.at[l])
        save(slopes.at[l], slope_out.at[l])

    attention_layer(0)
    save(vec_all, vec_out)
    save(rest_all, rest_out)
    ffn_layer(0)
    attention_layer(1)
    ffn_layer(1)

    for t in range(4):
        proj[t * EXTRA : (t + 1) * EXTRA, :] = rest_all[t, FRONT : FRONT + EXTRA, :]
    for i in range(3):
        rows = slice(i * 256, (i + 1) * 256)
        norm_rows(3, i)
        w = mm(hs[4, rows, :], proj[...], ((1,), (1,)))
        r = lax.rsqrt(jnp.sum(w * w, -1, keepdims=True) + NORM_EPSILON)
        unit[rows, :] = w * r
        length[rows, :] = jnp.broadcast_to(r, (256, 128))
        embedded[rows, :] = (w * r).astype(BF)
    save_norm(3)
    queries, passages = embedded[0:QROWS, :], embedded[QROWS:, :]
    logits = mm(queries, passages, ((1,), (1,))) * (1.0 / SOFTMAX_DIVISOR)
    column = lax.broadcasted_iota(jnp.int32, (1, REST), 1).astype(F32)
    token = lax.broadcasted_iota(jnp.int32, (QROWS, 1), 0)
    before = column < bound
    softs, shares = [], []
    for p in range(3):
        if p == 0:
            score = logits[:, 0:PLEN]
            top = jnp.max(score, -1, keepdims=True)
            e = jnp.exp(score - top)
        else:
            score = logits[:, PLEN:]
            inside = before if p == 1 else jnp.logical_not(before)
            score = jnp.where(inside, score, MASKED)
            top = jnp.max(score, -1, keepdims=True)
            e = jnp.where(inside, jnp.exp(score - top), 0.0)
        weight = jnp.sum(e, -1, keepdims=True)
        softs.append(SOFTMAX_DIVISOR * (top + jnp.log(weight)))
        shares.append(e * (1.0 / weight))
    loss = jnp.zeros((1, 1), F32)
    grad_softs = [jnp.zeros((QROWS, 1), F32) for p in range(3)]
    for q in range(QUERY_COUNT):
        mine_rows = (token // QUERY_LENGTH) == q
        scores = [
            SIMILARITY_SCALE * jnp.sum(jnp.where(mine_rows, soft, 0.0), 0, keepdims=True)
            for soft in softs
        ]
        top = jnp.maximum(jnp.maximum(scores[0], scores[1]), scores[2])
        es = [jnp.exp(score - top) for score in scores]
        weight = es[0] + es[1] + es[2]
        wanted = entry(8, q) - long_index
        wanted = jnp.where(wanted < 0.0, wanted + 3.0, wanted)
        chosen = [(wanted == float(p)).astype(F32) for p in range(3)]
        picked = chosen[0] * scores[0] + chosen[1] * scores[1] + chosen[2] * scores[2]
        loss = loss + top + jnp.log(weight) - picked
        for p in range(3):
            grad = (es[p] / weight - chosen[p]) * (SIMILARITY_SCALE / queries_all)
            grad_softs[p] = jnp.where(mine_rows, grad, grad_softs[p])
    grad_logits = jnp.concatenate(
        [grad_softs[0] * shares[0], grad_softs[1] * shares[1] + grad_softs[2] * shares[2]], axis=1
    ).astype(BF)
    grad_unit[0:QROWS, :] = mm(grad_logits, passages)
    grad_unit[QROWS:, :] = mm(grad_logits, queries, ((0,), (0,)))
    for i in range(3):
        rows = slice(i * 256, (i + 1) * 256)
        n, dn = unit[rows, :], grad_unit[rows, :]
        inner = jnp.sum(n * dn, -1, keepdims=True)
        grad_low[rows, :] = (length[rows, :] * (dn - n * inner)).astype(BF)
    save(grad_low, dw_out)
    grad_proj = mm(grad_low[...], hs[4], ((0,), (0,)))
    feature = lax.broadcasted_iota(jnp.int32, (16, D), 1)
    line = lax.broadcasted_iota(jnp.int32, (16, D), 0)
    head_rows = jnp.zeros((16, D), F32)
    left = loss
    for i, step in enumerate((8.0, 0.5, 2.0**-5, 2.0**-9, 2.0**-13, 2.0**-17)):
        value = jnp.floor(left * (1.0 / step)) * step
        left = left - value
        head_rows = jnp.where((line == 3) & (feature == i), value, head_rows)
    for t in range(4):
        tails[t, 0:16, :] = head_rows.astype(BF)
        tails[t, 16:TAIL, :] = grad_proj[t * EXTRA : (t + 1) * EXTRA, :].astype(BF)
    save(tails, tails_out)
    which_row = lax.broadcasted_iota(jnp.int32, (8, 1), 0)
    unit[0:8, :] = jnp.broadcast_to(jnp.where(which_row == 0, bound, begins), (8, 128))
    save(unit.at[pl.ds(0, 8), :], bound_out)

    for copy in saves:
        copy.wait()
    for i in range(3):
        swap_copy(3, i).wait_send()
    for n in range(count):
        direct(n, 0).wait_send()
        direct(n, 1).wait_send()
        relay(n).wait_send()
    if spread:
        z_drain()

    @pl.when(mine)
    def _():
        feature_copy(1, 1 - micro, s, y).wait_send()
        for i, owner in enumerate((s, x, y, xy)):
            quarter_to_twin(3 + i, owner).wait_send()

    @pl.when(jnp.logical_not(mine))
    def _():
        feature_copy(0, micro, s, x).wait_send()
        feature_copy(2, 1 - micro, s, xy).wait_send()


def forward(w, down, slices, projection, vectors, lengths, positive, layers, queries_all):
    spread = layers > 1 and SPREAD % (16 * layers) == 0 and SPREAD >= 32 * layers
    anywhere = pl.BlockSpec(memory_space=pl.ANY)
    inside = pl.BlockSpec(memory_space=pltpu.VMEM)
    pieces = 12 if not spread else 10
    steps = max(layers - 1, 1) if spread else 1
    kept = [
        ((4, D, FRONT), BF),
        ((4, FRONT + EXTRA, D), BF),
        ((4, 8, D), F32),
        ((4, ROWS, D), BF),
        ((4, ROWS, D), BF),
        ((4, ROWS, 128), F32),
        ((2, ROWS, FRONT), BF),
        ((2, ROWS, HALF), BF),
        ((2, PAIRS, 8, ROWS), F32),
        ((2, ROWS, 2 * D), BF),
        ((2, ROWS, 2 * D), BF),
        ((ROWS, DIM), BF),
        ((4, TAIL, D), BF),
        ((8, 128), F32),
    ]
    return pl.pallas_call(
        partial(forward_kernel, layers, spread, queries_all),
        in_specs=[anywhere] * 3 + [inside] * 6,
        out_specs=[anywhere] * len(kept),
        out_shape=[jax.ShapeDtypeStruct(shape, kind) for shape, kind in kept],
        scratch_shapes=[
            pltpu.VMEM((4, D, FRONT), BF),
            pltpu.VMEM((4, FRONT + EXTRA, D), BF),
            pltpu.VMEM((4, 8, D), F32),
            pltpu.VMEM((D, ROWS), BF),
            pltpu.VMEM((16, 128), jnp.int32),
            pltpu.VMEM((16, 128), jnp.int32),
            pltpu.VMEM((8, D), F32),
            pltpu.VMEM((D, 2 * D), F32),
            pltpu.VMEM((HALF, D), F32),
            pltpu.VMEM((D, D), F32),
            pltpu.VMEM((5, ROWS, D), BF),
            pltpu.VMEM((4, ROWS, D), BF),
            pltpu.VMEM((4, ROWS, 128), F32),
            pltpu.VMEM((2, ROWS, FRONT), BF),
            pltpu.VMEM((2, ROWS, HALF), BF),
            pltpu.VMEM((2, PAIRS, 8, ROWS), F32),
            pltpu.VMEM((2, ROWS, 2 * D), BF),
            pltpu.VMEM((2, ROWS, 2 * D), BF),
            pltpu.VMEM((ROWS, D), BF),
            pltpu.VMEM((2, ROWS, D), BF),
            pltpu.VMEM((DIM, D), BF),
            pltpu.VMEM((ROWS, DIM), BF),
            pltpu.VMEM((ROWS, DIM), F32),
            pltpu.VMEM((ROWS, DIM), F32),
            pltpu.VMEM((ROWS, DIM), F32),
            pltpu.VMEM((ROWS, DIM), BF),
            pltpu.VMEM((4, TAIL, D), BF),
            pltpu.SemaphoreType.DMA((16,)),
            pltpu.SemaphoreType.DMA((3, pieces)),
            pltpu.SemaphoreType.DMA((3, pieces)),
            pltpu.SemaphoreType.DMA((2, steps, 3)),
            pltpu.SemaphoreType.DMA((2, steps, 3)),
            pltpu.SemaphoreType.DMA((8,)),
            pltpu.SemaphoreType.DMA((8,)),
            pltpu.SemaphoreType.DMA((4, 3)),
            pltpu.SemaphoreType.DMA((4, 3)),
            pltpu.SemaphoreType.DMA((32,)),
        ],
        compiler_params=pltpu.CompilerParams(
            collective_id=1, has_side_effects=True, vmem_limit_bytes=62 * 1024 * 1024
        ),
    )(w, down, slices, projection, *vectors, lengths, positive)


TAIL = 48
SIDE = HALF + TAIL
STREAMS = ((D, FRONT, 64, True), (SIDE, D, 48, False), (D, D, 64, True))
CHUNKS = tuple(rows // step for rows, unused, step, unused2 in STREAMS)
OFFSETS = (CHUNKS[2], CHUNKS[2] + CHUNKS[0], 0)
ONE_LOW, ONE_HIGH, TWO, INWARD, BACK, TWIN = 0, 3, 6, 9, 12, 15


def backward_kernel(layers, lags, *refs):
    first_all, rest_all, hs, xhats, scales, qkvs, ctxs, lses, acts, slopes, tails = refs[0:11]
    bound_ref, vec_ref, dw_ref = refs[11:14]
    outs, out_back = refs[14:17], refs[17]
    sums, ones, twos, ins, backs = refs[18:21], refs[21:24], refs[24:27], refs[27:30], refs[30:33]
    (
        h_f,
        xhat_f,
        scale_f,
        slope,
        up_first,
        up_second,
        act_ring,
        down_ring,
        h_a,
        xhat_a,
        scale_a,
        qkv,
        ctx,
        lse,
        att_first,
        att_second,
        proj,
        dy,
        dc,
        part_out,
        part_in,
        shares,
        load_sem,
        ring_sem,
        part_send,
        part_recv,
        send_sem,
        recv_sem,
        keep_sem,
        in_send,
        in_recv,
    ) = refs[33:]
    s, b, x, y, xy = neighbours()
    z, core = b // 2, b % 2
    half = s // 2
    parity = s % 2
    mine = core == parity
    twin = b + 1 - 2 * core
    middle = max(layers // 2 - 1, 0)
    upper = z // max(layers // 2, 1)
    depth = z + upper * (layers - 1 - 2 * z)
    toward = b + 2 - 4 * upper
    outward = b - 2 + 4 * upper
    lag_z, lag_step = lags

    def load(src, dst, i):
        return pltpu.make_async_copy(src, dst, load_sem.at[i])

    def loads_ffn(l, begin=0, end=6):
        t = 2 * l + 1
        copies = [
            (xhats.at[t], xhat_f, 1),
            (scales.at[t], scale_f, 2),
            (slopes.at[l], slope, 3),
            (first_all.at[t], up_first, 4),
            (rest_all.at[t, pl.ds(0, HALF), :], up_second, 5),
            (hs.at[t], h_f, 0),
        ]
        return [load(*copy) for copy in copies[begin:end]]

    def loads_attention(l, begin=0, end=8):
        t = 2 * l
        copies = [
            (xhats.at[t], xhat_a, 7),
            (scales.at[t], scale_a, 8),
            (ctxs.at[l], ctx, 10),
            (qkvs.at[l], qkv, 9),
            (lses.at[l], lse, 11),
            (rest_all.at[t, pl.ds(0, HALF), :], att_second, 13),
            (first_all.at[t], att_first, 12),
            (hs.at[t], h_a, 6),
        ]
        return [load(*copy) for copy in copies[begin:end]]

    def ring(l, j):
        slot = j % 2
        rows = pl.ds(HALF + (j % 2) * HALF, HALF)
        return (
            pltpu.make_async_copy(
                acts.at[l, :, pl.ds(j * HALF, HALF)], act_ring.at[slot], ring_sem.at[0, slot]
            ),
            pltpu.make_async_copy(
                rest_all.at[2 * l + j // 2, rows, :], down_ring.at[slot], ring_sem.at[1, slot]
            ),
        )

    def start(copies):
        for copy in copies:
            copy.start()

    def wait(copies):
        for copy in copies:
            copy.wait()

    start_loads = [
        load(rest_all.at[t, pl.ds(FRONT, EXTRA), :], proj.at[pl.ds(t * EXTRA, EXTRA), :], 14 + t)
        for t in range(4)
    ] + [load(tails.at[t], sums[1].at[t, pl.ds(HALF, TAIL), :], 18 + t) for t in range(4)]
    start(start_loads)
    start(loads_ffn(1, 0, 2))
    start(ring(1, 0))
    start(loads_ffn(1, 2, 3))
    start(ring(1, 1))
    start(loads_ffn(1, 3))
    start(loads_attention(1))
    greet(layers)
    wait(start_loads)

    def remote(kind, chunk, src, dst, to):
        return pltpu.make_async_remote_copy(
            src_ref=src,
            dst_ref=dst,
            send_sem=send_sem.at[kind, chunk],
            recv_sem=recv_sem.at[kind, chunk],
            device_id=to,
            device_id_type=MESH,
        )

    def rows_of(which, chunk):
        size = STREAMS[which][2]
        return pl.ds(pl.multiple_of(chunk * size, 16), size)

    def one(which, chunk, l):
        rows = rows_of(which, chunk)
        kind = (ONE_HIGH if l else ONE_LOW) + which
        if STREAMS[which][3]:
            src = sums[which].at[2 * l + 1 - parity, rows, :]
            return remote(kind, chunk, src, ones[which].at[l, rows, :], (x, b))
        src = sums[which].at[2 * (1 - half) + l, rows, :]
        return remote(kind, chunk, src, ones[which].at[l, rows, :], (y, b))

    def forwarded(which):
        return 2 * (1 - half) + parity if STREAMS[which][3] else 2 * half + 1 - parity

    def two(which, chunk):
        rows = rows_of(which, chunk)
        src = sums[which].at[forwarded(which), rows, :]
        to = y if STREAMS[which][3] else x
        return remote(TWO + which, chunk, src, twos[which].at[rows, :], (to, b))

    def inward(which, chunk, swap):
        rows = rows_of(which, chunk)
        src = sums[which].at[s, rows, :]
        if swap:
            return remote(BACK + which, chunk, src, backs[which].at[rows, :], (s, toward))
        return remote(INWARD + which, chunk, src, ins[which].at[rows, :], (s, toward))

    def final(which, at_middle):
        return sums[which].at[s] if at_middle else backs[which]

    def outward_copy(which, chunk, at_middle):
        rows = rows_of(which, chunk)
        src = final(which, at_middle).at[rows, :]
        return remote(BACK + which, chunk, src, backs[which].at[rows, :], (s, outward))

    def twin_copy(which, chunk, at_middle):
        rows = rows_of(which, chunk)
        src = final(which, at_middle).at[rows, :]
        return remote(TWIN + which, chunk, src, outs[which].at[core, rows, :], (s, twin))

    def keep_copy(which, chunk, at_middle):
        rows = rows_of(which, chunk)
        src = final(which, at_middle).at[rows, :]
        return pltpu.make_async_copy(
            src, outs[which].at[core, rows, :], keep_sem.at[which, chunk]
        )

    def plus(*values):
        total = values[0].astype(F32)
        for value in values[1:]:
            total = total + value.astype(F32)
        return total

    def send_block(which, t, start_row, rows):
        size = STREAMS[which][2]
        by_x = STREAMS[which][3]

        @pl.when(parity != t % 2 if by_x else half != t // 2)
        def _():
            def body(c, unused):
                one(which, c, t // 2 if by_x else t % 2).start()
                return unused

            lax.fori_loop(start_row // size, (start_row + rows) // size, body, 0)

    def swap_copy(t, i):
        rows = pl.ds(i * 256, 256)
        return pltpu.make_async_remote_copy(
            src_ref=part_out.at[rows, :],
            dst_ref=part_in.at[t % 2, rows, :],
            send_sem=part_send.at[t, i],
            recv_sem=part_recv.at[t, i],
            device_id=(s, twin),
            device_id_type=MESH,
        )

    def norm_back(t, grad_of, xhat, scale):
        gain = vec_ref[t, 1:2, :]

        def body(i, carry):
            rows = pl.ds(pl.multiple_of(i * 128, 128), 128)
            grad = grad_of(rows)
            xh = xhat[rows, :].astype(F32)
            weighted = grad * gain
            mean_1 = jnp.mean(weighted, -1, keepdims=True)
            mean_2 = jnp.mean(weighted * xh, -1, keepdims=True)
            du = scale[rows, 0:1] * (weighted - mean_1 - xh * mean_2)
            dy[rows, :] = du.astype(BF)
            return (
                carry[0] + jnp.sum(du, 0, keepdims=True),
                carry[1] + jnp.sum(grad * xh, 0, keepdims=True),
                carry[2] + jnp.sum(grad, 0, keepdims=True),
            )

        zero = jnp.zeros((1, D), F32)
        carry = (zero, zero, zero)
        for i in range(3):
            if t < 3:
                swap_copy(t + 1, i).wait_recv()
            carry = lax.fori_loop(2 * i, 2 * i + 2, body, carry)
        row = lax.broadcasted_iota(jnp.int32, (16, 1), 0)
        block = sums[1][t, HALF : HALF + 16, :].astype(F32)
        for i in range(3):
            block = jnp.where(row == i, carry[i], block)
        sums[1][t, HALF : HALF + 16, :] = block.astype(BF)

    def grad_from_head(rows):
        return mm(dw_ref[rows, :], proj[...])

    def grad_from(t):
        def grad_of(rows):
            total = plus(dy[rows, :], part_out[rows, :], part_in[t % 2, rows, :])
            return total.astype(BF).astype(F32)

        return grad_of

    def ffn_back(l):
        t = 2 * l + 1
        for j in range(4):
            wait(ring(l, j))
            slot = j % 2
            columns = slice(j * HALF, (j + 1) * HALF)
            low = dy[...]
            to = (j % 2) * HALF
            sums[2][2 * l + j // 2, to : to + HALF, :] = mm(
                act_ring[slot], low, ((0,), (0,))
            ).astype(BF)
            send_block(2, 2 * l + j // 2, to, HALF)
            if j == 0:
                wait(loads_ffn(l, 2, 3))
            for i in range(3):
                rows = slice(i * 256, (i + 1) * 256)
                grad = mm(dy[rows, :], down_ring[slot], ((1,), (1,)))
                slope[rows, columns] = (grad * slope[rows, columns].astype(F32)).astype(BF)
            if j < 2:
                start(ring(l, j + 2))
        wait(loads_ffn(l, 3))
        for i in range(3):
            rows = slice(i * 256, (i + 1) * 256)
            if t < 3:
                swap_copy(t + 1, i).wait_send()
            part = mm(slope[rows, 0:FRONT], up_first[...], ((1,), (1,)))
            part = part + mm(slope[rows, FRONT:], up_second[...])
            part_out[rows, :] = part.astype(BF)
            swap_copy(t, i).start()
        for i in range(3):
            rows = slice(i * 256, (i + 1) * 256)
            sums[0][t, rows, :] = mm(h_f[:, rows], slope[:, 0:FRONT], ((0,), (0,))).astype(BF)
        sums[1][t, 0:HALF, :] = mm(slope[:, FRONT:], h_f[...], ((0,), (0,))).astype(BF)

    def attention_pair(i, unused):
        lane = lax.broadcasted_iota(jnp.int32, (1, 128), 1)
        base = pl.multiple_of(i * 384, 128)
        q_at, k_at, v_at = (
            pl.ds(base, 128),
            pl.ds(pl.multiple_of(base + 128, 128), 128),
            pl.ds(pl.multiple_of(base + 256, 128), 128),
        )
        c_at = pl.ds(pl.multiple_of(i * 128, 128), 128)
        for which, (begin, size) in enumerate(BLOCKS):
            chunk = size
            span = slice(begin, begin + size)
            k = qkv[span, k_at]
            v = qkv[span, v_at]
            dk = jnp.zeros((size, 128), F32)
            dv = jnp.zeros((size, 128), F32)
            for at in range(begin, begin + size, chunk):
                rows = slice(at, at + chunk)
                q = qkv[rows, q_at]
                dcs = dc[rows, c_at]
                dq = None
                for head in range(2):
                    own = (lane < 64) if head == 0 else (lane >= 64)
                    qm = jnp.where(own, q, jnp.zeros_like(q)) * BF(0.125)
                    dcm = jnp.where(own, dcs, jnp.zeros_like(dcs))
                    km = jnp.where(own, k, jnp.zeros_like(k))
                    score = mm(k, qm, ((1,), (1,)))
                    if which != 1:
                        score = jnp.where(block_mask(which, bound_ref[0:1, 0:1], size), score, MASKED)
                    p = jnp.exp(score - lse[i, head : head + 1, rows])
                    dp = mm(v, dcm, ((1,), (1,)))
                    inner = jnp.sum(p * dp, axis=0, keepdims=True)
                    ds = (p * (dp - inner)).astype(BF)
                    dv = dv + mm(p.astype(BF), dcm)
                    dk = dk + mm(ds, qm)
                    part = mm(km, ds, ((0,), (0,)))
                    dq = part if dq is None else dq + part
                qkv[rows, q_at] = (dq.T * 0.125).astype(BF)
            qkv[span, k_at] = dk.astype(BF)
            qkv[span, v_at] = dv.astype(BF)
        return unused

    def attention_grads(l):
        t = 2 * l
        sums[1][t, 0:HALF, :] = mm(ctx[...], dy[...], ((0,), (0,))).astype(BF)
        send_block(1, t, 0, SIDE)
        for i in range(3):
            rows = slice(i * 256, (i + 1) * 256)
            dc[rows, :] = mm(dy[rows, :], att_second[...], ((1,), (1,))).astype(BF)
        lax.fori_loop(0, PAIRS, attention_pair, 0)
        for i in range(3):
            rows = slice(i * 256, (i + 1) * 256)
            swap_copy(t + 1, i).wait_send()
            part_out[rows, :] = mm(qkv[rows, :], att_first[...], ((1,), (1,))).astype(BF)
            swap_copy(t, i).start()
        for i in range(3):
            rows = slice(i * 256, (i + 1) * 256)
            sums[0][t, rows, :] = mm(h_a[:, rows], qkv[...], ((0,), (0,))).astype(BF)

    def send_sections(t):
        if t % 2 == 1:
            send_block(1, t, 0, SIDE)
        send_block(0, t, 0, D)

    def came_one(which, chunk, l):
        one(which, chunk, l).wait_recv()

    def start_two(which, chunk):
        rows = rows_of(which, chunk)
        t = forwarded(which)
        if STREAMS[which][3]:
            came_one(which, chunk, 0)
            came_one(which, chunk, 1)
            got = ones[which][1 - half, rows, :]
        else:
            came_one(which, chunk, 0)
            came_one(which, chunk, 1)
            got = ones[which][1 - parity, rows, :]
        sums[which][t, rows, :] = plus(sums[which][t, rows, :], got).astype(BF)
        two(which, chunk).start()

    wait(loads_ffn(1, 0, 2))
    norm_back(3, grad_from_head, xhat_f, scale_f)
    ffn_back(1)
    send_sections(3)
    start(loads_ffn(0))
    start(ring(0, 0))
    start(ring(0, 1))
    wait(loads_attention(1))
    norm_back(2, grad_from(3), xhat_a, scale_a)
    attention_grads(1)
    send_sections(2)
    start(loads_attention(0))
    wait(loads_ffn(0, 0, 2))
    norm_back(1, grad_from(2), xhat_f, scale_f)
    ffn_back(0)
    send_sections(1)
    wait(loads_attention(0))
    norm_back(0, grad_from(1), xhat_a, scale_a)

    attention_grads(0)
    send_sections(0)

    for i in range(3):
        swap_copy(0, i).wait_recv()

        def body(j, unused):
            rows = pl.ds(pl.multiple_of(j * 64, 64), 64)
            dy[rows, :] = plus(dy[rows, :], part_out[rows, :], part_in[0, rows, :]).astype(BF)
            return unused

        lax.fori_loop(4 * i, 4 * i + 4, body, 0)
    back = -bound_ref[1:2, 0:1]
    for i in range(6):
        rows = slice(i * 128, (i + 1) * 128)
        if i == 0:
            total = dy[rows, :].astype(F32)
        else:
            total = mm(rotation(i - 1, back), dy[QROWS:, :])
        shares[:, rows] = total.T.astype(BF)

    def features(section):
        size = out_back.shape[1]
        return shares.at[pl.ds(pl.multiple_of(section * size, 16), size), :]

    def back_to(i, to):
        return pltpu.make_async_remote_copy(
            src_ref=features(to),
            dst_ref=out_back.at[i],
            send_sem=in_send.at[i],
            recv_sem=in_recv.at[i],
            device_id=(to, b),
            device_id_type=MESH,
        )

    own_share = pltpu.make_async_copy(features(s), out_back.at[3], in_send.at[3])
    own_share.start()

    @pl.when(mine)
    def _():
        for i, to in enumerate((x, y, xy)):
            back_to(i, to).start()

    def start_z(which, chunk):
        rows = rows_of(which, chunk)
        two(which, chunk).wait_recv()
        got = ones[which][half if STREAMS[which][3] else parity, rows, :]
        total = plus(sums[which][s, rows, :], got, twos[which][rows, :])
        if layers == 1:
            sums[which][s, rows, :] = total.astype(BF)
            twin_copy(which, chunk, True).start()
            keep_copy(which, chunk, True).start()
            return
        if middle > 0:

            @pl.when(depth > 0)
            def _():
                inward(which, chunk, False).wait_recv()
                sums[which][s, rows, :] = plus(total, ins[which][rows, :]).astype(BF)

            @pl.when(depth == 0)
            def _():
                sums[which][s, rows, :] = total.astype(BF)

            @pl.when(depth < middle)
            def _():
                inward(which, chunk, False).start()

        else:
            sums[which][s, rows, :] = total.astype(BF)

        @pl.when(depth == middle)
        def _():
            inward(which, chunk, True).start()

    def finish(which, chunk):
        rows = rows_of(which, chunk)
        inward(which, chunk, True).wait_recv()

        @pl.when(depth == middle)
        def _():
            inward(which, chunk, True).wait_send()
            sums[which][s, rows, :] = plus(
                sums[which][s, rows, :], backs[which][rows, :]
            ).astype(BF)
            if middle > 0:
                outward_copy(which, chunk, True).start()
            twin_copy(which, chunk, True).start()
            keep_copy(which, chunk, True).start()

        if middle > 0:

            @pl.when(depth < middle)
            def _():
                @pl.when(depth > 0)
                def _():
                    outward_copy(which, chunk, False).start()

                twin_copy(which, chunk, False).start()
                keep_copy(which, chunk, False).start()

    lag3 = lag_z + lag_step * depth
    lag5 = lag_z + lag_step * (middle + 1) + lag_step * (middle - depth)
    slots = sum(CHUNKS) + lag_z + (lag_step * (2 * middle + 1) if layers > 1 else 0)

    def guarded(position, step):
        for which, count in enumerate(CHUNKS):
            chunk = position - OFFSETS[which]

            @pl.when((chunk >= 0) & (chunk < count))
            def _():
                step(which, chunk)

    def slot(k, unused):
        guarded(k, start_two)
        guarded(k - lag3, start_z)
        if layers > 1:
            guarded(k - lag5, finish)
        return unused

    lax.fori_loop(0, slots, slot, 0)

    def drain(which, chunk):
        twin_copy(which, chunk, True).wait_recv()
        twin_copy(which, chunk, True).wait_send()
        keep_copy(which, chunk, True).wait()
        if STREAMS[which][3]:
            one(which, chunk, 0).wait_send()
            one(which, chunk, 1).wait_send()
        else:
            one(which, chunk, 0).wait_send()
            one(which, chunk, 1).wait_send()
        two(which, chunk).wait_send()
        if layers > 1 and middle > 0:

            @pl.when(depth < middle)
            def _():
                inward(which, chunk, False).wait_send()

            @pl.when(depth > 0)
            def _():
                outward_copy(which, chunk, True).wait_send()

    def last(k, unused):
        guarded(k, drain)
        return unused

    lax.fori_loop(0, sum(CHUNKS), last, 0)
    for i in range(3):
        swap_copy(0, i).wait_send()
    own_share.wait()

    @pl.when(mine)
    def _():
        for i, to in enumerate((x, y, xy)):
            back_to(i, to).wait_send()
        back_to(1, y).wait_recv()

    @pl.when(jnp.logical_not(mine))
    def _():
        back_to(0, x).wait_recv()
        back_to(2, xy).wait_recv()


def backward(first_all, rest_all, vec, kept, dw, tails, bound, width, layers, lags=(2, 2)):
    anywhere = pl.BlockSpec(memory_space=pl.ANY)
    inside = pl.BlockSpec(memory_space=pltpu.VMEM)
    shapes = [(rows, columns) for rows, columns, unused, unused2 in STREAMS]
    most = max(CHUNKS)
    return pl.pallas_call(
        partial(backward_kernel, layers, lags),
        in_specs=[anywhere] * 11 + [inside] * 3,
        out_specs=[anywhere] * 4,
        out_shape=[jax.ShapeDtypeStruct((2,) + shape, BF) for shape in shapes]
        + [jax.ShapeDtypeStruct((4, width, ROWS), BF)],
        scratch_shapes=[pltpu.VMEM((4,) + shape, BF) for shape in shapes]
        + [pltpu.VMEM((2,) + shape, BF) for shape in shapes]
        + [pltpu.VMEM(shape, BF) for shape in shapes] * 3
        + [
            pltpu.VMEM((ROWS, D), BF),
            pltpu.VMEM((ROWS, D), BF),
            pltpu.VMEM((ROWS, 128), F32),
            pltpu.VMEM((ROWS, 2 * D), BF),
            pltpu.VMEM((D, FRONT), BF),
            pltpu.VMEM((HALF, D), BF),
            pltpu.VMEM((2, ROWS, HALF), BF),
            pltpu.VMEM((2, HALF, D), BF),
            pltpu.VMEM((ROWS, D), BF),
            pltpu.VMEM((ROWS, D), BF),
            pltpu.VMEM((ROWS, 128), F32),
            pltpu.VMEM((ROWS, FRONT), BF),
            pltpu.VMEM((ROWS, HALF), BF),
            pltpu.VMEM((PAIRS, 8, ROWS), F32),
            pltpu.VMEM((D, FRONT), BF),
            pltpu.VMEM((HALF, D), BF),
            pltpu.VMEM((4 * EXTRA, D), BF),
            pltpu.VMEM((ROWS, D), BF),
            pltpu.VMEM((ROWS, HALF), BF),
            pltpu.VMEM((ROWS, D), BF),
            pltpu.VMEM((2, ROWS, D), BF),
            pltpu.VMEM((D, ROWS), BF),
            pltpu.SemaphoreType.DMA((22,)),
            pltpu.SemaphoreType.DMA((2, 2)),
            pltpu.SemaphoreType.DMA((4, 3)),
            pltpu.SemaphoreType.DMA((4, 3)),
            pltpu.SemaphoreType.DMA((18, most)),
            pltpu.SemaphoreType.DMA((18, most)),
            pltpu.SemaphoreType.DMA((3, most)),
            pltpu.SemaphoreType.DMA((4,)),
            pltpu.SemaphoreType.DMA((4,)),
        ],
        compiler_params=pltpu.CompilerParams(
            collective_id=2, has_side_effects=True, vmem_limit_bytes=62 * 1024 * 1024
        ),
    )(first_all, rest_all, *kept, tails, bound, vec, dw)


def assemble_kernel(
    queries_all,
    first_ref,
    side_ref,
    down_ref,
    back_ref,
    out_ref,
    down_out,
    input_out,
    bias_out,
    gain_out,
    shift_out,
    projection_out,
    loss_out,
):
    s, b = lax.axis_index("section"), lax.axis_index("batch")
    row = pl.program_id(0)

    @pl.when(s % 2 == 0)
    def _():
        for core in range(2):
            for i in range(PAIRS):
                for t in range(3):
                    to = t * D + core * HALF + i * 128
                    at = (3 * i + t) * 128
                    out_ref[:, to : to + 128] = first_ref[core, :, at : at + 128].astype(F32)
        from_core = row // 3
        at = pl.multiple_of((row % 3) * 128, 128)
        out_ref[:, 3 * D :] = side_ref[from_core, pl.ds(at, 128), :].astype(F32)

    @pl.when(s % 2 == 1)
    def _():
        lanes = pl.ds(pl.multiple_of(row * 128, 128), 128)
        for core in range(2):
            out_ref[:, core * D : (core + 1) * D] = first_ref[core, :, 0:D].astype(F32)
            at = 2 * D + core * D
            out_ref[:, at : at + HALF] = first_ref[core, :, D:].astype(F32)
            out_ref[:, at + HALF : at + D] = side_ref[core, 0:HALF, lanes].astype(F32).T

    down_out[...] = down_ref[...].astype(F32)
    mine = b % 2 == s % 2
    same = jnp.where(mine, back_ref[3].astype(F32), back_ref[0].astype(F32))
    other = jnp.where(mine, back_ref[1].astype(F32), back_ref[2].astype(F32))
    for m in range(2):
        input_out[m] = jnp.where(s // 2 == m, same, other)

    @pl.when(row == 0)
    def _():
        vectors = side_ref[0, HALF : HALF + 16, :].astype(F32)
        bias_out[...] = vectors[0:1]
        gain_out[...] = vectors[1:2]
        shift_out[...] = vectors[2:3]
        loss_out[...] = jnp.sum(vectors[3:4], axis=1, keepdims=True) * (1.0 / queries_all)
        projection_out[...] = side_ref[0, HALF + 16 :, :].astype(F32)


def assemble(first_sum, side_sum, down_sum, back, queries_all):
    width = back.shape[1]
    steps = D // 128

    def whole(shape):
        return pl.BlockSpec(shape, lambda i: (0,) * len(shape))

    return pl.pallas_call(
        partial(assemble_kernel, queries_all),
        grid=(steps,),
        in_specs=[
            pl.BlockSpec((2, 128, FRONT), lambda i: (0, i, 0)),
            whole((2, SIDE, D)),
            pl.BlockSpec((256, D), lambda i: (i, 0)),
            pl.BlockSpec((4, width, 128), lambda i: (0, 0, i)),
        ],
        out_specs=[
            pl.BlockSpec((128, 4 * D), lambda i: (i, 0)),
            pl.BlockSpec((256, D), lambda i: (i, 0)),
            pl.BlockSpec((2, width, 128), lambda i: (0, 0, i)),
            whole((1, D)),
            whole((1, D)),
            whole((1, D)),
            whole((EXTRA, D)),
            whole((1, 1)),
        ],
        out_shape=[
            jax.ShapeDtypeStruct(shape, F32)
            for shape in (
                (D, 4 * D),
                (2 * D, D),
                (2, width, ROWS),
                (1, D),
                (1, D),
                (1, D),
                (EXTRA, D),
                (1, 1),
            )
        ],
        compiler_params=pltpu.CompilerParams(vmem_limit_bytes=60 * 1024 * 1024),
    )(first_sum, side_sum, down_sum.reshape(2 * D, D), back)


def gelu_and_slope(z):
    upper = 0.5 * (1.0 + lax.erf(z * 0.7071067811865476))
    density = jnp.exp(-0.5 * z * z) * 0.3989422804014327
    return (z * upper).astype(BF), (upper + z * density).astype(BF)


def on_device(
    inputs,
    in_weight,
    down_weight,
    out_bias,
    norm_gains,
    norm_shifts,
    projection,
    passage_lengths,
    positive,
):
    batches = lax.axis_size("batch")
    layers = batches // 2
    queries_all = inputs.shape[0] * batches * QUERY_COUNT
    first_all, rest_all, vectors, *kept, dw, tails, bound = forward(
        in_weight[0],
        down_weight,
        inputs.transpose(0, 2, 1),
        projection.T,
        (out_bias, norm_gains, norm_shifts),
        passage_lengths[:, 0],
        positive,
        layers,
        queries_all,
    )
    first_sum, side_sum, down_sum, back = backward(
        first_all, rest_all, vectors, kept, dw, tails, bound, inputs.shape[2], layers
    )
    in_grad, down_grad, input_grad, bias_grad, gain_grad, shift_grad, projection_grad, loss = (
        assemble(first_sum, side_sum, down_sum, back, queries_all)
    )
    return (
        loss[0, 0],
        input_grad.transpose(0, 2, 1),
        in_grad[None],
        down_grad,
        bias_grad,
        gain_grad,
        shift_grad,
        projection_grad.T,
    )


def solution(mesh):
    in_specs = (
        P(None, "batch", "section"),
        P("section", None, None),
        P("section", None),
        P("section", None),
        P("section", None),
        P("section", None),
        P(None, "section"),
        P(None, "batch", None),
        P(None, "batch"),
    )
    out_specs = (
        P(),
        P(None, "batch", "section"),
        P("section", None, None),
        P("section", None),
        P("section", None),
        P("section", None),
        P("section", None),
        P(None, "section"),
    )
    return jax.shard_map(
        on_device, mesh=mesh, in_specs=in_specs, out_specs=out_specs, check_vma=False
    )
```

```python
from functools import partial

import jax
import jax.numpy as jnp
from jax import lax
from jax.experimental import pallas as pl
from jax.experimental.pallas import tpu as pltpu
from jax.sharding import PartitionSpec as P

D = 768
HEADS = 12
FF = 3072
DIM = 128
QUERY_LENGTH = 32
QUERY_COUNT = 4
PASSAGE_COUNT = 3
PASSAGE_TOKENS = 640
PLEN = 512
QROWS = QUERY_LENGTH * QUERY_COUNT
ROWS = QROWS + PASSAGE_TOKENS
REST = PASSAGE_TOKENS - PLEN
SOFTMAX_DIVISOR = 0.1
SIMILARITY_SCALE = 0.25
NORM_EPSILON = 1e-06
MASKED = -1000000000.0
BF = jnp.bfloat16
F32 = jnp.float32
BLOCKS = ((0, QROWS), (QROWS, PLEN), (QROWS + PLEN, REST))
PAIRS = HEADS // 4
HALF = D // 2


def mm(a, b, dims=((1,), (0,))):
    return lax.dot_general(a, b, (dims, ((), ())), preferred_element_type=F32)


def block_mask(which, bound, rows):
    t = lax.broadcasted_iota(jnp.int32, (rows, rows), 0)
    r = lax.broadcasted_iota(jnp.int32, (rows, rows), 1)
    if which == 0:
        return (t // QUERY_LENGTH) == (r // QUERY_LENGTH)
    return ((t.astype(F32) < bound).astype(F32) - (r.astype(F32) < bound).astype(F32)) == 0.0


def unit_matrix(n):
    r = lax.broadcasted_iota(jnp.int32, (n, n), 0)
    c = lax.broadcasted_iota(jnp.int32, (n, n), 1)
    return (r == c).astype(F32).astype(BF)


def rotation(i, begins):
    r = lax.broadcasted_iota(jnp.int32, (128, PASSAGE_TOKENS), 0).astype(F32) + float(i * 128)
    c = lax.broadcasted_iota(jnp.int32, (128, PASSAGE_TOKENS), 1).astype(F32)
    ahead = c - r - begins
    total = float(PASSAGE_TOKENS)
    return ((ahead == 0.0) | (ahead == -total) | (ahead == total)).astype(F32).astype(BF)


MESH = pl.DeviceIdType.MESH
EXTRA = 32
FRONT = 1152
SPREAD = 960


def neighbours():
    s, b = lax.axis_index("section"), lax.axis_index("batch")
    x = s + 1 - 2 * (s % 2)
    y = s + 2 - 4 * (s // 2)
    xy = 3 - s
    return s, b, x, y, xy


def greet(layers):
    s, b, x, y, xy = neighbours()
    z, core = b // 2, b % 2
    barrier = pltpu.get_barrier_semaphore()

    def signal(to):
        pl.semaphore_signal(barrier, inc=1, device_id=to, device_id_type=MESH)

    signal((x, b))
    signal((y, b))
    signal((xy, b))
    signal((s, b + 1 - 2 * core))
    if layers > 1:

        @pl.when(z > 0)
        def _():
            signal((s, b - 2))

        @pl.when(z < layers - 1)
        def _():
            signal((s, b + 2))

        ends = (layers - 1 - z) // (layers - 1) + z // (layers - 1)
        pl.semaphore_wait(barrier, 6 - ends)
    else:
        pl.semaphore_wait(barrier, 4)


def forward_kernel(layers, spread, queries_all, *refs):
    w_ref, down_ref, slices_ref, projection_ref = refs[0:4]
    bias_ref, gain_ref, shift_ref, lengths_ref, positive_ref = refs[4:9]
    first_out, rest_out, vec_out, h_out, xhat_out, scale_out, qkv_out, ctx_out = refs[9:17]
    lse_out, act_out, slope_out, dw_out, tails_out, bound_out = refs[17:23]
    (
        first_all,
        rest_all,
        vec_all,
        tokens,
        ints_ref,
        ints_other,
        vec_ref,
        wide,
        out_stage,
        down_stage,
        hs,
        xhats,
        scales,
        qkvs,
        ctxs,
        lses,
        acts,
        slopes,
        part_out,
        part_in,
        proj,
        embedded,
        unit,
        length,
        grad_unit,
        grad_low,
        tails,
        load_sem,
        send_sem,
        recv_sem,
        z_send,
        z_recv,
        in_send,
        in_recv,
        part_send,
        part_recv,
        save_sem,
    ) = refs[23:]
    s, b, x, y, xy = neighbours()
    z, core = b // 2, b % 2
    micro = s // 2
    mine = core == s % 2
    twin = b + 1 - 2 * core

    def load(src, dst, i):
        return pltpu.make_async_copy(src, dst, load_sem.at[i])

    loads = [load(down_ref.at[pl.ds(core * D, D), :], down_stage, 0)]
    even, odd = [], []
    for i in range(PAIRS):
        for t in range(3):
            at = pl.multiple_of(t * D + core * HALF + i * 128, 128)
            to = (3 * i + t) * 128
            even.append(
                load(w_ref.at[:, pl.ds(at, 128)], wide.at[:, pl.ds(to, 128)], 1 + 3 * i + t)
            )
    even.append(load(w_ref.at[pl.ds(core * HALF, HALF), pl.ds(3 * D, D)], out_stage, 10))
    for i in range(2):
        at = pl.multiple_of(i * 2 * D + core * D, 128)
        odd.append(load(w_ref.at[:, pl.ds(at, D)], wide.at[:, pl.ds(i * D, D)], 11 + i))
    loads[0].start()

    @pl.when(s % 2 == 0)
    def _():
        for copy in even:
            copy.start()

    @pl.when(s % 2 == 1)
    def _():
        for copy in odd:
            copy.start()

    first, rest = first_all.at[s], rest_all.at[s]
    ints_ref[...] = jnp.zeros_like(ints_ref)
    ints_ref[0:2, 0:PASSAGE_COUNT] = lengths_ref[...]
    ints_ref[8:10, 0:QUERY_COUNT] = positive_ref[...]
    vec_ref[0:1, :] = bias_ref[...]
    vec_ref[1:2, :] = gain_ref[...]
    vec_ref[2:3, :] = shift_ref[...]
    vec_ref[3:8, :] = jnp.zeros((5, D), F32)
    own_vec = pltpu.make_async_copy(vec_ref, vec_all.at[s], load_sem.at[15])
    own_vec.start()
    rest[FRONT : FRONT + EXTRA, :] = projection_ref[...].astype(BF)
    greet(layers)

    def features(section):
        size = slices_ref.shape[1]
        return tokens.at[pl.ds(pl.multiple_of(section * size, 16), size), :]

    def feature_copy(i, which, section, to):
        return pltpu.make_async_remote_copy(
            src_ref=slices_ref.at[which],
            dst_ref=features(section),
            send_sem=in_send.at[i],
            recv_sem=in_recv.at[i],
            device_id=(to, b),
            device_id_type=MESH,
        )

    def to_twin(i, src, dst):
        return pltpu.make_async_remote_copy(
            src_ref=src,
            dst_ref=dst,
            send_sem=in_send.at[i],
            recv_sem=in_recv.at[i],
            device_id=(s, twin),
            device_id_type=MESH,
        )

    def quarter_to_twin(i, f):
        return to_twin(i, features(f), features(f))

    swap_ints = to_twin(7, ints_ref, ints_other)
    own_quarter = pltpu.make_async_copy(slices_ref.at[micro], features(s), load_sem.at[14])
    swap_ints.start()

    def send_features():
        @pl.when(mine)
        def _():
            own_quarter.start()
            feature_copy(1, 1 - micro, s, y).start()

        @pl.when(jnp.logical_not(mine))
        def _():
            feature_copy(0, micro, s, x).start()
            feature_copy(2, 1 - micro, s, xy).start()

    loads[0].wait()

    @pl.loop(0, D // 96)
    def _(i):
        rows = pl.ds(pl.multiple_of(i * 96, 16), 96)
        to = pl.ds(pl.multiple_of(HALF + i * 96, 16), 96)
        rest[to, :] = down_stage[rows, :].astype(BF)

    @pl.when(s % 2 == 0)
    def _():
        for copy in even:
            copy.wait()

        @pl.loop(0, HALF // 96)
        def _(i):
            rows = pl.ds(pl.multiple_of(i * 96, 16), 96)
            rest[rows, :] = out_stage[rows, :].astype(BF)

    @pl.when(s % 2 == 1)
    def _():
        for copy in odd:
            copy.wait()
        for i in range(3):
            for j in range(6):
                block = wide[j * 128 : (j + 1) * 128, FRONT + i * 128 : FRONT + (i + 1) * 128]
                rest[i * 128 : (i + 1) * 128, j * 128 : (j + 1) * 128] = block.T.astype(BF)

    quarter = D // 4
    firsts = [(first, first_all, i * quarter, quarter, i < 2) for i in range(4)]
    seconds = [(rest, rest_all, i * 96, 96, i == 0) for i in range(2)]
    small = [
        (rest, rest_all, FRONT, EXTRA, True),
        (vec_ref, vec_all, 0, 8, False),
    ]
    if spread:
        share = SPREAD // layers
        at = pl.multiple_of(FRONT - SPREAD + z * share, 16)
        half = share // 32 * 16
        slices = [
            (rest, rest_all, at, half, True),
            (rest, rest_all, pl.multiple_of(at + half, 16), share - half, False),
        ]
    else:
        slices = []
        seconds = [(rest, rest_all, i * 192, 192, i % 2 == 0) for i in range(6)]
    pieces = slices + firsts + seconds + small

    def part(n, ref):
        unused, unused, row, rows, unused = pieces[n]
        return ref.at[pl.ds(row, rows), :]

    def remote(n, kind, src, dst, to):
        return pltpu.make_async_remote_copy(
            src_ref=src,
            dst_ref=dst,
            send_sem=send_sem.at[kind, n],
            recv_sem=recv_sem.at[kind, n],
            device_id=(to, b),
            device_id_type=MESH,
        )

    def direct(n, kind):
        mine, every = pieces[n][:2]
        return remote(n, kind, part(n, mine), part(n, every.at[s]), y if kind else x)

    def arrived(n, kind):
        every = pieces[n][1]
        owner = (x, y, xy)[kind]
        here = part(n, every.at[owner])
        remote(n, kind, here, here, x).wait_recv()

    def relay(n):
        every, by_x = pieces[n][1], pieces[n][4]
        source = part(n, every.at[x if by_x else y])
        return remote(n, 2, source, source, y if by_x else x)

    def pass_on(n):
        arrived(n, 0 if pieces[n][4] else 1)
        relay(n).start()

    count = len(pieces)
    front = list(range(len(slices), len(slices) + 4))
    behind = list(range(len(slices) + 4, count))

    def along_x(n):
        direct(n, 0).start()

    def along_y(n):
        direct(n, 1).start()

    z_width = SPREAD // layers if spread else 0

    def z_part(section, owner_z):
        at = pl.multiple_of(FRONT - SPREAD + owner_z * z_width, 16)
        return rest_all.at[section, pl.ds(at, z_width), :]

    def z_copy(way, step, k, owner_z, to_b):
        source = z_part((x, y, xy)[k], owner_z)
        return pltpu.make_async_remote_copy(
            src_ref=source,
            dst_ref=source,
            send_sem=z_send.at[way, step, k],
            recv_sem=z_recv.at[way, step, k],
            device_id=(s, to_b),
            device_id_type=MESH,
        )

    def z_first(k):
        @pl.when(z < layers - 1)
        def _():
            z_copy(0, 0, k, z, b + 2).start()

        @pl.when(z > 0)
        def _():
            z_copy(1, 0, k, z, b - 2).start()

    def z_step(step):
        @pl.when(z >= step)
        def _():
            for k in range(3):
                z_copy(0, step - 1, k, z - step, b).wait_recv()

                @pl.when(z < layers - 1)
                def _():
                    z_copy(0, step, k, z - step, b + 2).start()

        @pl.when(z < layers - step)
        def _():
            for k in range(3):
                z_copy(1, step - 1, k, z + step, b).wait_recv()

                @pl.when(z > 0)
                def _():
                    z_copy(1, step, k, z + step, b - 2).start()

    def z_drain():
        for step in range(layers - 1):

            @pl.when((z < layers - 1) & (z >= step))
            def _():
                for k in range(3):
                    z_copy(0, step, k, z - step, b + 2).wait_send()

            @pl.when((z > 0) & (z + step < layers))
            def _():
                for k in range(3):
                    z_copy(1, step, k, z + step, b - 2).wait_send()

    for n in range(len(slices)):
        along_x(n)
        along_y(n)
    send_features()
    @pl.loop(0, D // 96)
    def _(i):
        rows = pl.ds(pl.multiple_of(i * 96, 16), 96)
        first[rows, :] = wide[rows, 0:FRONT].astype(BF)


    along_x(front[0])
    along_y(front[2])

    if spread:
        pass_on(0)
        pass_on(1)
    along_x(front[1])
    along_y(front[3])
    if spread:
        arrived(0, 1)
        arrived(1, 0)
        z_first(0)
        z_first(1)
    @pl.when(mine)
    def _():
        own_quarter.wait()
        quarter_to_twin(3, s).start()
        for i, owner in enumerate((x, y, xy)):
            feature_copy(i, 0, owner, x).wait_recv()
            quarter_to_twin(4 + i, owner).start()

    pass_on(front[0])
    pass_on(front[2])
    along_x(front[2])
    along_y(front[0])
    if spread:
        arrived(0, 2)
        arrived(1, 2)
        z_first(2)
    pass_on(front[1])
    pass_on(front[3])
    along_x(front[3])
    along_y(front[1])
    z_at = 1
    if spread and z_at < layers - 1:
        z_step(z_at)
        z_at += 1
    for n in behind:
        if pieces[n][4]:
            along_x(n)
        else:
            along_y(n)
    for n in behind:
        if pieces[n][4]:
            along_y(n)
        else:
            along_x(n)
    arrived(front[0], 1)
    arrived(front[2], 0)
    while spread and z_at < layers - 1:
        z_step(z_at)
        z_at += 1
    arrived(front[1], 1)
    arrived(front[3], 0)
    for n in front:
        arrived(n, 2)
    swap_ints.wait()
    own_vec.wait()

    @pl.when(jnp.logical_not(mine))
    def _():
        for i, owner in enumerate((s, x, y, xy)):
            quarter_to_twin(3 + i, owner).wait_recv()

    lane = lax.broadcasted_iota(jnp.int32, (1, 128), 1)

    def entry(first_row, i):
        row = pl.ds(first_row + micro, 1)
        values = jnp.where(mine, ints_ref[row, :].astype(F32), ints_other[row, :].astype(F32))
        return jnp.sum(jnp.where(lane == i, values, 0.0), axis=1, keepdims=True)

    sizes = [entry(0, i) for i in range(PASSAGE_COUNT)]
    is_long = [
        (sizes[0] == float(PLEN)).astype(F32),
        (sizes[1] == float(PLEN)).astype(F32),
        (sizes[2] == float(PLEN)).astype(F32),
    ]
    bound = is_long[0] * sizes[1] + is_long[1] * sizes[2] + is_long[2] * sizes[0]
    long_index = is_long[1] + 2.0 * is_long[2]
    begins = is_long[1] * sizes[0] + is_long[2] * (sizes[0] + sizes[1])

    saves = []

    def save(src, dst):
        copy = pltpu.make_async_copy(src, dst, save_sem.at[len(saves)])
        copy.start()
        saves.append(copy)

    save(first_all, first_out)

    def swap_copy(t, i):
        rows = pl.ds(i * 256, 256)
        return pltpu.make_async_remote_copy(
            src_ref=part_out.at[rows, :],
            dst_ref=part_in.at[t % 2, rows, :],
            send_sem=part_send.at[t, i],
            recv_sem=part_recv.at[t, i],
            device_id=(s, twin),
            device_id_type=MESH,
        )

    hs[0, 0:QROWS, :] = mm(unit_matrix(QROWS), tokens[:, 0:QROWS], ((1,), (1,))).astype(BF)
    for i in range(PASSAGE_TOKENS // 128):
        rows = slice(QROWS + i * 128, QROWS + (i + 1) * 128)
        hs[0, rows, :] = mm(rotation(i, begins), tokens[:, QROWS:], ((1,), (1,))).astype(BF)
    save(hs.at[0], h_out.at[0])

    def norm_rows(t, i):
        bias, gain, shift = vec_all[t, 0:1, :], vec_all[t, 1:2, :], vec_all[t, 2:3, :]
        swap_copy(t, i).wait_recv()

        def body(j, unused):
            rows = pl.ds(pl.multiple_of(j * 128, 128), 128)
            u = (
                hs[t, rows, :].astype(F32)
                + part_out[rows, :].astype(F32)
                + part_in[t % 2, rows, :].astype(F32)
                + bias
            )
            centered = u - jnp.mean(u, -1, keepdims=True)
            scale = lax.rsqrt(jnp.mean(centered * centered, -1, keepdims=True) + NORM_EPSILON)
            xhat = centered * scale
            xhats[t, rows, :] = xhat.astype(BF)
            scales[t, rows, :] = jnp.broadcast_to(scale, (128, 128))
            hs[t + 1, rows, :] = (xhat * gain + shift).astype(BF)
            return unused

        lax.fori_loop(2 * i, 2 * i + 2, body, 0)

    def save_norm(t):
        save(xhats.at[t], xhat_out.at[t])
        save(scales.at[t], scale_out.at[t])
        if t < 3:
            save(hs.at[t + 1], h_out.at[t + 1])

    def attention_pair(l):
        def pair(i, unused):
            base = pl.multiple_of(i * 384, 128)
            q_at = pl.ds(base, 128)
            k_at = pl.ds(pl.multiple_of(base + 128, 128), 128)
            v_at = pl.ds(pl.multiple_of(base + 256, 128), 128)
            c_at = pl.ds(pl.multiple_of(i * 128, 128), 128)
            for which, (begin, size) in enumerate(BLOCKS):
                chunk = size
                span = slice(begin, begin + size)
                k = qkvs[l, span, k_at]
                v = qkvs[l, span, v_at]
                for at in range(begin, begin + size, chunk):
                    rows = slice(at, at + chunk)
                    q = qkvs[l, rows, q_at]
                    total = None
                    for head in range(2):
                        own = (lane < 64) if head == 0 else (lane >= 64)
                        qm = jnp.where(own, q, jnp.zeros_like(q)) * BF(0.125)
                        vm = jnp.where(own, v, jnp.zeros_like(v))
                        score = mm(k, qm, ((1,), (1,)))
                        if which != 1:
                            score = jnp.where(block_mask(which, bound, size), score, MASKED)
                        top = jnp.max(score, axis=0, keepdims=True)
                        e = jnp.exp(score - top)
                        weight = jnp.sum(e, axis=0, keepdims=True)
                        part = mm(vm, e.astype(BF), ((0,), (0,))) * (1.0 / weight)
                        total = part if total is None else total + part
                        lses[l, i, head : head + 1, rows] = top + jnp.log(weight)
                    ctxs[l, rows, c_at] = total.T.astype(BF)
            return unused

        lax.fori_loop(0, PAIRS, pair, 0)

    def attention_layer(l):
        t = 2 * l
        for i in range(3):
            rows = slice(i * 256, (i + 1) * 256)
            if t > 0:
                norm_rows(t - 1, i)
            qkvs[l, rows, :] = mm(hs[t, rows, :], first_all[t]).astype(BF)
        if t > 0:
            save_norm(t - 1)
        save(qkvs.at[l], qkv_out.at[l])
        if l == 0:
            for n in behind:
                pass_on(n)
        attention_pair(l)
        if l == 0:
            for n in behind:
                arrived(n, 1 if pieces[n][4] else 0)
                arrived(n, 2)
            if spread:
                z_step(layers - 1)
        save(ctxs.at[l], ctx_out.at[l])
        save(lses.at[l], lse_out.at[l])
        for i in range(3):
            rows = slice(i * 256, (i + 1) * 256)
            if t > 0:
                swap_copy(t - 1, i).wait_send()
            part_out[rows, :] = mm(ctxs[l, rows, :], rest_all[t, 0:HALF, :]).astype(BF)
            swap_copy(t, i).start()

    def ffn_layer(l):
        t = 2 * l + 1
        for i in range(3):
            rows = slice(i * 256, (i + 1) * 256)
            norm_rows(t - 1, i)
            x_rows = hs[t, rows, :]
            for j in range(4):
                columns = slice(j * HALF, (j + 1) * HALF)
                if j < 3:
                    value = mm(x_rows, first_all[t, :, columns])
                else:
                    value = mm(x_rows, rest_all[t, 0:HALF, :], ((1,), (1,)))
                act, slope = gelu_and_slope(value)
                acts[l, rows, columns] = act
                slopes[l, rows, columns] = slope
            swap_copy(t - 1, i).wait_send()
            part = mm(acts[l, rows, 0:D], rest_all[2 * l, HALF:FRONT, :])
            part = part + mm(acts[l, rows, D:], rest_all[2 * l + 1, HALF:FRONT, :])
            part_out[rows, :] = part.astype(BF)
            swap_copy(t, i).start()
        save_norm(t - 1)
        save(acts.at[l], act_out.at[l])
        save(slopes.at[l], slope_out.at[l])

    attention_layer(0)
    save(vec_all, vec_out)
    save(rest_all, rest_out)
    ffn_layer(0)
    attention_layer(1)
    ffn_layer(1)

    for t in range(4):
        proj[t * EXTRA : (t + 1) * EXTRA, :] = rest_all[t, FRONT : FRONT + EXTRA, :]
    for i in range(3):
        rows = slice(i * 256, (i + 1) * 256)
        norm_rows(3, i)
        w = mm(hs[4, rows, :], proj[...], ((1,), (1,)))
        r = lax.rsqrt(jnp.sum(w * w, -1, keepdims=True) + NORM_EPSILON)
        unit[rows, :] = w * r
        length[rows, :] = jnp.broadcast_to(r, (256, 128))
        embedded[rows, :] = (w * r).astype(BF)
    save_norm(3)
    queries, passages = embedded[0:QROWS, :], embedded[QROWS:, :]
    logits = mm(queries, passages, ((1,), (1,))) * (1.0 / SOFTMAX_DIVISOR)
    column = lax.broadcasted_iota(jnp.int32, (1, REST), 1).astype(F32)
    token = lax.broadcasted_iota(jnp.int32, (QROWS, 1), 0)
    before = column < bound
    softs, shares = [], []
    for p in range(3):
        if p == 0:
            score = logits[:, 0:PLEN]
            top = jnp.max(score, -1, keepdims=True)
            e = jnp.exp(score - top)
        else:
            score = logits[:, PLEN:]
            inside = before if p == 1 else jnp.logical_not(before)
            score = jnp.where(inside, score, MASKED)
            top = jnp.max(score, -1, keepdims=True)
            e = jnp.where(inside, jnp.exp(score - top), 0.0)
        weight = jnp.sum(e, -1, keepdims=True)
        softs.append(SOFTMAX_DIVISOR * (top + jnp.log(weight)))
        shares.append(e * (1.0 / weight))
    loss = jnp.zeros((1, 1), F32)
    grad_softs = [jnp.zeros((QROWS, 1), F32) for p in range(3)]
    for q in range(QUERY_COUNT):
        mine_rows = (token // QUERY_LENGTH) == q
        scores = [
            SIMILARITY_SCALE * jnp.sum(jnp.where(mine_rows, soft, 0.0), 0, keepdims=True)
            for soft in softs
        ]
        top = jnp.maximum(jnp.maximum(scores[0], scores[1]), scores[2])
        es = [jnp.exp(score - top) for score in scores]
        weight = es[0] + es[1] + es[2]
        wanted = entry(8, q) - long_index
        wanted = jnp.where(wanted < 0.0, wanted + 3.0, wanted)
        chosen = [(wanted == float(p)).astype(F32) for p in range(3)]
        picked = chosen[0] * scores[0] + chosen[1] * scores[1] + chosen[2] * scores[2]
        loss = loss + top + jnp.log(weight) - picked
        for p in range(3):
            grad = (es[p] / weight - chosen[p]) * (SIMILARITY_SCALE / queries_all)
            grad_softs[p] = jnp.where(mine_rows, grad, grad_softs[p])
    grad_logits = jnp.concatenate(
        [grad_softs[0] * shares[0], grad_softs[1] * shares[1] + grad_softs[2] * shares[2]], axis=1
    ).astype(BF)
    grad_unit[0:QROWS, :] = mm(grad_logits, passages)
    grad_unit[QROWS:, :] = mm(grad_logits, queries, ((0,), (0,)))
    for i in range(3):
        rows = slice(i * 256, (i + 1) * 256)
        n, dn = unit[rows, :], grad_unit[rows, :]
        inner = jnp.sum(n * dn, -1, keepdims=True)
        grad_low[rows, :] = (length[rows, :] * (dn - n * inner)).astype(BF)
    save(grad_low, dw_out)
    grad_proj = mm(grad_low[...], hs[4], ((0,), (0,)))
    feature = lax.broadcasted_iota(jnp.int32, (16, D), 1)
    line = lax.broadcasted_iota(jnp.int32, (16, D), 0)
    head_rows = jnp.zeros((16, D), F32)
    left = loss
    for i, step in enumerate((8.0, 0.5, 2.0**-5, 2.0**-9, 2.0**-13, 2.0**-17)):
        value = jnp.floor(left * (1.0 / step)) * step
        left = left - value
        head_rows = jnp.where((line == 3) & (feature == i), value, head_rows)
    for t in range(4):
        tails[t, 0:16, :] = head_rows.astype(BF)
        tails[t, 16:TAIL, :] = grad_proj[t * EXTRA : (t + 1) * EXTRA, :].astype(BF)
    save(tails, tails_out)
    which_row = lax.broadcasted_iota(jnp.int32, (8, 1), 0)
    unit[0:8, :] = jnp.broadcast_to(jnp.where(which_row == 0, bound, begins), (8, 128))
    save(unit.at[pl.ds(0, 8), :], bound_out)

    for copy in saves:
        copy.wait()
    for i in range(3):
        swap_copy(3, i).wait_send()
    for n in range(count):
        direct(n, 0).wait_send()
        direct(n, 1).wait_send()
        relay(n).wait_send()
    if spread:
        z_drain()

    @pl.when(mine)
    def _():
        feature_copy(1, 1 - micro, s, y).wait_send()
        for i, owner in enumerate((s, x, y, xy)):
            quarter_to_twin(3 + i, owner).wait_send()

    @pl.when(jnp.logical_not(mine))
    def _():
        feature_copy(0, micro, s, x).wait_send()
        feature_copy(2, 1 - micro, s, xy).wait_send()


def forward(w, down, slices, projection, vectors, lengths, positive, layers, queries_all):
    spread = layers > 1 and SPREAD % (16 * layers) == 0 and SPREAD >= 32 * layers
    anywhere = pl.BlockSpec(memory_space=pl.ANY)
    inside = pl.BlockSpec(memory_space=pltpu.VMEM)
    pieces = 12 if not spread else 10
    steps = max(layers - 1, 1) if spread else 1
    kept = [
        ((4, D, FRONT), BF),
        ((4, FRONT + EXTRA, D), BF),
        ((4, 8, D), F32),
        ((4, ROWS, D), BF),
        ((4, ROWS, D), BF),
        ((4, ROWS, 128), F32),
        ((2, ROWS, FRONT), BF),
        ((2, ROWS, HALF), BF),
        ((2, PAIRS, 8, ROWS), F32),
        ((2, ROWS, 2 * D), BF),
        ((2, ROWS, 2 * D), BF),
        ((ROWS, DIM), BF),
        ((4, TAIL, D), BF),
        ((8, 128), F32),
    ]
    return pl.pallas_call(
        partial(forward_kernel, layers, spread, queries_all),
        in_specs=[anywhere] * 3 + [inside] * 6,
        out_specs=[anywhere] * len(kept),
        out_shape=[jax.ShapeDtypeStruct(shape, kind) for shape, kind in kept],
        scratch_shapes=[
            pltpu.VMEM((4, D, FRONT), BF),
            pltpu.VMEM((4, FRONT + EXTRA, D), BF),
            pltpu.VMEM((4, 8, D), F32),
            pltpu.VMEM((D, ROWS), BF),
            pltpu.VMEM((16, 128), jnp.int32),
            pltpu.VMEM((16, 128), jnp.int32),
            pltpu.VMEM((8, D), F32),
            pltpu.VMEM((D, 2 * D), F32),
            pltpu.VMEM((HALF, D), F32),
            pltpu.VMEM((D, D), F32),
            pltpu.VMEM((5, ROWS, D), BF),
            pltpu.VMEM((4, ROWS, D), BF),
            pltpu.VMEM((4, ROWS, 128), F32),
            pltpu.VMEM((2, ROWS, FRONT), BF),
            pltpu.VMEM((2, ROWS, HALF), BF),
            pltpu.VMEM((2, PAIRS, 8, ROWS), F32),
            pltpu.VMEM((2, ROWS, 2 * D), BF),
            pltpu.VMEM((2, ROWS, 2 * D), BF),
            pltpu.VMEM((ROWS, D), BF),
            pltpu.VMEM((2, ROWS, D), BF),
            pltpu.VMEM((DIM, D), BF),
            pltpu.VMEM((ROWS, DIM), BF),
            pltpu.VMEM((ROWS, DIM), F32),
            pltpu.VMEM((ROWS, DIM), F32),
            pltpu.VMEM((ROWS, DIM), F32),
            pltpu.VMEM((ROWS, DIM), BF),
            pltpu.VMEM((4, TAIL, D), BF),
            pltpu.SemaphoreType.DMA((16,)),
            pltpu.SemaphoreType.DMA((3, pieces)),
            pltpu.SemaphoreType.DMA((3, pieces)),
            pltpu.SemaphoreType.DMA((2, steps, 3)),
            pltpu.SemaphoreType.DMA((2, steps, 3)),
            pltpu.SemaphoreType.DMA((8,)),
            pltpu.SemaphoreType.DMA((8,)),
            pltpu.SemaphoreType.DMA((4, 3)),
            pltpu.SemaphoreType.DMA((4, 3)),
            pltpu.SemaphoreType.DMA((32,)),
        ],
        compiler_params=pltpu.CompilerParams(
            collective_id=1, has_side_effects=True, vmem_limit_bytes=62 * 1024 * 1024
        ),
    )(w, down, slices, projection, *vectors, lengths, positive)


TAIL = 48
SIDE = HALF + TAIL
STREAMS = ((D, FRONT, 64, True), (SIDE, D, 48, False), (D, D, 64, True))
CHUNKS = tuple(rows // step for rows, unused, step, unused2 in STREAMS)
OFFSETS = (CHUNKS[2], CHUNKS[2] + CHUNKS[0], 0)
TWO_OFFSETS = (CHUNKS[2], 0, 0)
ONE_LOW, ONE_HIGH, TWO, INWARD, BACK, TWIN = 0, 3, 6, 9, 12, 15


def backward_kernel(layers, lags, *refs):
    first_all, rest_all, hs, xhats, scales, qkvs, ctxs, lses, acts, slopes, tails = refs[0:11]
    bound_ref, vec_ref, dw_ref = refs[11:14]
    outs, out_back = refs[14:17], refs[17]
    sums, ones, twos, ins, backs = refs[18:21], refs[21:24], refs[24:27], refs[27:30], refs[30:33]
    (
        h_f,
        xhat_f,
        scale_f,
        slope,
        up_first,
        up_second,
        act_ring,
        down_ring,
        h_a,
        xhat_a,
        scale_a,
        qkv,
        ctx,
        lse,
        att_first,
        att_second,
        proj,
        dy,
        dc,
        part_out,
        part_in,
        shares,
        load_sem,
        ring_sem,
        part_send,
        part_recv,
        send_sem,
        recv_sem,
        keep_sem,
        in_send,
        in_recv,
    ) = refs[33:]
    s, b, x, y, xy = neighbours()
    z, core = b // 2, b % 2
    half = s // 2
    parity = s % 2
    mine = core == parity
    twin = b + 1 - 2 * core
    middle = max(layers // 2 - 1, 0)
    upper = z // max(layers // 2, 1)
    depth = z + upper * (layers - 1 - 2 * z)
    toward = b + 2 - 4 * upper
    outward = b - 2 + 4 * upper
    lag_z, lag_step = lags

    def load(src, dst, i):
        return pltpu.make_async_copy(src, dst, load_sem.at[i])

    def loads_ffn(l, begin=0, end=6):
        t = 2 * l + 1
        copies = [
            (xhats.at[t], xhat_f, 1),
            (scales.at[t], scale_f, 2),
            (slopes.at[l], slope, 3),
            (first_all.at[t], up_first, 4),
            (rest_all.at[t, pl.ds(0, HALF), :], up_second, 5),
            (hs.at[t], h_f, 0),
        ]
        return [load(*copy) for copy in copies[begin:end]]

    def loads_attention(l, begin=0, end=8):
        t = 2 * l
        copies = [
            (xhats.at[t], xhat_a, 7),
            (scales.at[t], scale_a, 8),
            (ctxs.at[l], ctx, 10),
            (qkvs.at[l], qkv, 9),
            (lses.at[l], lse, 11),
            (rest_all.at[t, pl.ds(0, HALF), :], att_second, 13),
            (first_all.at[t], att_first, 12),
            (hs.at[t], h_a, 6),
        ]
        return [load(*copy) for copy in copies[begin:end]]

    def ring(l, j):
        slot = j % 2
        rows = pl.ds(HALF + (j % 2) * HALF, HALF)
        return (
            pltpu.make_async_copy(
                acts.at[l, :, pl.ds(j * HALF, HALF)], act_ring.at[slot], ring_sem.at[0, slot]
            ),
            pltpu.make_async_copy(
                rest_all.at[2 * l + j // 2, rows, :], down_ring.at[slot], ring_sem.at[1, slot]
            ),
        )

    def start(copies):
        for copy in copies:
            copy.start()

    def wait(copies):
        for copy in copies:
            copy.wait()

    start_loads = [
        load(rest_all.at[t, pl.ds(FRONT, EXTRA), :], proj.at[pl.ds(t * EXTRA, EXTRA), :], 14 + t)
        for t in range(4)
    ] + [load(tails.at[t], sums[1].at[t, pl.ds(HALF, TAIL), :], 18 + t) for t in range(4)]
    start(start_loads)
    start(loads_ffn(1, 0, 2))
    start(ring(1, 0))
    start(loads_ffn(1, 2, 3))
    start(ring(1, 1))
    start(loads_ffn(1, 3))
    start(loads_attention(1))
    greet(layers)
    wait(start_loads)

    def remote(kind, chunk, src, dst, to):
        return pltpu.make_async_remote_copy(
            src_ref=src,
            dst_ref=dst,
            send_sem=send_sem.at[kind, chunk],
            recv_sem=recv_sem.at[kind, chunk],
            device_id=to,
            device_id_type=MESH,
        )

    def rows_of(which, chunk):
        size = STREAMS[which][2]
        return pl.ds(pl.multiple_of(chunk * size, 16), size)

    def one(which, chunk, l):
        rows = rows_of(which, chunk)
        kind = (ONE_HIGH if l else ONE_LOW) + which
        if STREAMS[which][3]:
            src = sums[which].at[2 * l + 1 - parity, rows, :]
            return remote(kind, chunk, src, ones[which].at[l, rows, :], (x, b))
        src = sums[which].at[2 * (1 - half) + l, rows, :]
        return remote(kind, chunk, src, ones[which].at[l, rows, :], (y, b))

    def forwarded(which):
        return 2 * (1 - half) + parity if STREAMS[which][3] else 2 * half + 1 - parity

    def two(which, chunk):
        rows = rows_of(which, chunk)
        src = sums[which].at[forwarded(which), rows, :]
        to = y if STREAMS[which][3] else x
        return remote(TWO + which, chunk, src, twos[which].at[rows, :], (to, b))

    def inward(which, chunk, swap):
        rows = rows_of(which, chunk)
        src = sums[which].at[s, rows, :]
        if swap:
            return remote(BACK + which, chunk, src, backs[which].at[rows, :], (s, toward))
        return remote(INWARD + which, chunk, src, ins[which].at[rows, :], (s, toward))

    def final(which, at_middle):
        return sums[which].at[s] if at_middle else backs[which]

    def outward_copy(which, chunk, at_middle):
        rows = rows_of(which, chunk)
        src = final(which, at_middle).at[rows, :]
        return remote(BACK + which, chunk, src, backs[which].at[rows, :], (s, outward))

    def twin_copy(which, chunk, at_middle):
        rows = rows_of(which, chunk)
        src = final(which, at_middle).at[rows, :]
        return remote(TWIN + which, chunk, src, outs[which].at[core, rows, :], (s, twin))

    def keep_copy(which, chunk, at_middle):
        rows = rows_of(which, chunk)
        src = final(which, at_middle).at[rows, :]
        return pltpu.make_async_copy(
            src, outs[which].at[core, rows, :], keep_sem.at[which, chunk]
        )

    def plus(*values):
        total = values[0].astype(F32)
        for value in values[1:]:
            total = total + value.astype(F32)
        return total

    def send_block(which, t, start_row, rows):
        size = STREAMS[which][2]
        by_x = STREAMS[which][3]

        @pl.when(parity != t % 2 if by_x else half != t // 2)
        def _():
            def body(c, unused):
                one(which, c, t // 2 if by_x else t % 2).start()
                return unused

            lax.fori_loop(start_row // size, (start_row + rows) // size, body, 0)

    def swap_copy(t, i):
        rows = pl.ds(i * 256, 256)
        return pltpu.make_async_remote_copy(
            src_ref=part_out.at[rows, :],
            dst_ref=part_in.at[t % 2, rows, :],
            send_sem=part_send.at[t, i],
            recv_sem=part_recv.at[t, i],
            device_id=(s, twin),
            device_id_type=MESH,
        )

    def norm_back(t, grad_of, xhat, scale):
        gain = vec_ref[t, 1:2, :]

        def body(i, carry):
            rows = pl.ds(pl.multiple_of(i * 128, 128), 128)
            grad = grad_of(rows)
            xh = xhat[rows, :].astype(F32)
            weighted = grad * gain
            mean_1 = jnp.mean(weighted, -1, keepdims=True)
            mean_2 = jnp.mean(weighted * xh, -1, keepdims=True)
            du = scale[rows, 0:1] * (weighted - mean_1 - xh * mean_2)
            dy[rows, :] = du.astype(BF)
            return (
                carry[0] + jnp.sum(du, 0, keepdims=True),
                carry[1] + jnp.sum(grad * xh, 0, keepdims=True),
                carry[2] + jnp.sum(grad, 0, keepdims=True),
            )

        zero = jnp.zeros((1, D), F32)
        carry = (zero, zero, zero)
        for i in range(3):
            if t < 3:
                swap_copy(t + 1, i).wait_recv()
            carry = lax.fori_loop(2 * i, 2 * i + 2, body, carry)
        row = lax.broadcasted_iota(jnp.int32, (16, 1), 0)
        block = sums[1][t, HALF : HALF + 16, :].astype(F32)
        for i in range(3):
            block = jnp.where(row == i, carry[i], block)
        sums[1][t, HALF : HALF + 16, :] = block.astype(BF)

    def grad_from_head(rows):
        return mm(dw_ref[rows, :], proj[...])

    def grad_from(t):
        def grad_of(rows):
            total = plus(dy[rows, :], part_out[rows, :], part_in[t % 2, rows, :])
            return total.astype(BF).astype(F32)

        return grad_of

    def ffn_back(l):
        t = 2 * l + 1
        for j in range(4):
            wait(ring(l, j))
            slot = j % 2
            columns = slice(j * HALF, (j + 1) * HALF)
            low = dy[...]
            to = (j % 2) * HALF
            sums[2][2 * l + j // 2, to : to + HALF, :] = mm(
                act_ring[slot], low, ((0,), (0,))
            ).astype(BF)
            send_block(2, 2 * l + j // 2, to, HALF)
            if j == 0:
                wait(loads_ffn(l, 2, 3))
            for i in range(3):
                rows = slice(i * 256, (i + 1) * 256)
                grad = mm(dy[rows, :], down_ring[slot], ((1,), (1,)))
                slope[rows, columns] = (grad * slope[rows, columns].astype(F32)).astype(BF)
            if j < 2:
                start(ring(l, j + 2))
        wait(loads_ffn(l, 3))
        for i in range(3):
            rows = slice(i * 256, (i + 1) * 256)
            if t < 3:
                swap_copy(t + 1, i).wait_send()
            part = mm(slope[rows, 0:FRONT], up_first[...], ((1,), (1,)))
            part = part + mm(slope[rows, FRONT:], up_second[...])
            part_out[rows, :] = part.astype(BF)
            swap_copy(t, i).start()
        for i in range(3):
            rows = slice(i * 256, (i + 1) * 256)
            sums[0][t, rows, :] = mm(h_f[:, rows], slope[:, 0:FRONT], ((0,), (0,))).astype(BF)
        sums[1][t, 0:HALF, :] = mm(slope[:, FRONT:], h_f[...], ((0,), (0,))).astype(BF)

    def attention_pair(i, unused):
        lane = lax.broadcasted_iota(jnp.int32, (1, 128), 1)
        base = pl.multiple_of(i * 384, 128)
        q_at, k_at, v_at = (
            pl.ds(base, 128),
            pl.ds(pl.multiple_of(base + 128, 128), 128),
            pl.ds(pl.multiple_of(base + 256, 128), 128),
        )
        c_at = pl.ds(pl.multiple_of(i * 128, 128), 128)
        for which, (begin, size) in enumerate(BLOCKS):
            chunk = size
            span = slice(begin, begin + size)
            k = qkv[span, k_at]
            v = qkv[span, v_at]
            dk = jnp.zeros((size, 128), F32)
            dv = jnp.zeros((size, 128), F32)
            for at in range(begin, begin + size, chunk):
                rows = slice(at, at + chunk)
                q = qkv[rows, q_at]
                dcs = dc[rows, c_at]
                dq = None
                for head in range(2):
                    own = (lane < 64) if head == 0 else (lane >= 64)
                    qm = jnp.where(own, q, jnp.zeros_like(q)) * BF(0.125)
                    dcm = jnp.where(own, dcs, jnp.zeros_like(dcs))
                    km = jnp.where(own, k, jnp.zeros_like(k))
                    score = mm(k, qm, ((1,), (1,)))
                    if which != 1:
                        score = jnp.where(block_mask(which, bound_ref[0:1, 0:1], size), score, MASKED)
                    p = jnp.exp(score - lse[i, head : head + 1, rows])
                    dp = mm(v, dcm, ((1,), (1,)))
                    inner = jnp.sum(p * dp, axis=0, keepdims=True)
                    ds = (p * (dp - inner)).astype(BF)
                    dv = dv + mm(p.astype(BF), dcm)
                    dk = dk + mm(ds, qm)
                    part = mm(km, ds, ((0,), (0,)))
                    dq = part if dq is None else dq + part
                qkv[rows, q_at] = (dq.T * 0.125).astype(BF)
            qkv[span, k_at] = dk.astype(BF)
            qkv[span, v_at] = dv.astype(BF)
        return unused

    def attention_grads(l):
        t = 2 * l
        sums[1][t, 0:HALF, :] = mm(ctx[...], dy[...], ((0,), (0,))).astype(BF)
        send_block(1, t, 0, SIDE)
        for i in range(3):
            rows = slice(i * 256, (i + 1) * 256)
            dc[rows, :] = mm(dy[rows, :], att_second[...], ((1,), (1,))).astype(BF)
        lax.fori_loop(0, PAIRS, attention_pair, 0)
        for i in range(3):
            rows = slice(i * 256, (i + 1) * 256)
            swap_copy(t + 1, i).wait_send()
            part_out[rows, :] = mm(qkv[rows, :], att_first[...], ((1,), (1,))).astype(BF)
            swap_copy(t, i).start()
        for i in range(3):
            rows = slice(i * 256, (i + 1) * 256)
            sums[0][t, rows, :] = mm(h_a[:, rows], qkv[...], ((0,), (0,))).astype(BF)

    def send_sections(t):
        if t % 2 == 1:
            send_block(1, t, 0, SIDE)
        send_block(0, t, 0, D)

    def came_one(which, chunk, l):
        one(which, chunk, l).wait_recv()

    def start_two(which, chunk):
        rows = rows_of(which, chunk)
        t = forwarded(which)
        if STREAMS[which][3]:
            came_one(which, chunk, 0)
            came_one(which, chunk, 1)
            got = ones[which][1 - half, rows, :]
        else:
            came_one(which, chunk, 0)
            came_one(which, chunk, 1)
            got = ones[which][1 - parity, rows, :]
        sums[which][t, rows, :] = plus(sums[which][t, rows, :], got).astype(BF)
        two(which, chunk).start()

    wait(loads_ffn(1, 0, 2))
    norm_back(3, grad_from_head, xhat_f, scale_f)
    ffn_back(1)
    send_sections(3)
    start(loads_ffn(0))
    start(ring(0, 0))
    start(ring(0, 1))
    wait(loads_attention(1))
    norm_back(2, grad_from(3), xhat_a, scale_a)
    attention_grads(1)
    send_sections(2)
    start(loads_attention(0))
    wait(loads_ffn(0, 0, 2))
    norm_back(1, grad_from(2), xhat_f, scale_f)
    ffn_back(0)
    send_sections(1)
    wait(loads_attention(0))
    norm_back(0, grad_from(1), xhat_a, scale_a)

    attention_grads(0)
    send_sections(0)

    def start_z(which, chunk):
        rows = rows_of(which, chunk)
        two(which, chunk).wait_recv()
        got = ones[which][half if STREAMS[which][3] else parity, rows, :]
        total = plus(sums[which][s, rows, :], got, twos[which][rows, :])
        if layers == 1:
            sums[which][s, rows, :] = total.astype(BF)
            twin_copy(which, chunk, True).start()
            keep_copy(which, chunk, True).start()
            return
        if middle > 0:

            @pl.when(depth > 0)
            def _():
                inward(which, chunk, False).wait_recv()
                sums[which][s, rows, :] = plus(total, ins[which][rows, :]).astype(BF)

            @pl.when(depth == 0)
            def _():
                sums[which][s, rows, :] = total.astype(BF)

            @pl.when(depth < middle)
            def _():
                inward(which, chunk, False).start()

        else:
            sums[which][s, rows, :] = total.astype(BF)

        @pl.when(depth == middle)
        def _():
            inward(which, chunk, True).start()

    def finish(which, chunk):
        rows = rows_of(which, chunk)
        inward(which, chunk, True).wait_recv()

        @pl.when(depth == middle)
        def _():
            inward(which, chunk, True).wait_send()
            sums[which][s, rows, :] = plus(
                sums[which][s, rows, :], backs[which][rows, :]
            ).astype(BF)
            if middle > 0:
                outward_copy(which, chunk, True).start()
            twin_copy(which, chunk, True).start()
            keep_copy(which, chunk, True).start()

        if middle > 0:

            @pl.when(depth < middle)
            def _():
                @pl.when(depth > 0)
                def _():
                    outward_copy(which, chunk, False).start()

                twin_copy(which, chunk, False).start()
                keep_copy(which, chunk, False).start()

    lag3 = lag_z + lag_step * depth
    lag5 = lag_z + lag_step * (middle + 1) + lag_step * (middle - depth)
    slots = sum(CHUNKS) + lag_z + (lag_step * (2 * middle + 1) if layers > 1 else 0)

    def guarded(position, step, offsets=OFFSETS):
        for which, count in enumerate(CHUNKS):
            chunk = position - offsets[which]

            @pl.when((chunk >= 0) & (chunk < count))
            def _():
                step(which, chunk)

    def slot(k, unused):
        guarded(k, start_two, TWO_OFFSETS)
        guarded(k - lag3, start_z)
        if layers > 1:
            guarded(k - lag5, finish)
        return unused

    lax.fori_loop(0, 24, slot, 0)
    for i in range(3):
        swap_copy(0, i).wait_recv()

        def body(j, unused):
            rows = pl.ds(pl.multiple_of(j * 64, 64), 64)
            dy[rows, :] = plus(dy[rows, :], part_out[rows, :], part_in[0, rows, :]).astype(BF)
            return unused

        lax.fori_loop(4 * i, 4 * i + 4, body, 0)
    back = -bound_ref[1:2, 0:1]
    for i in range(6):
        rows = slice(i * 128, (i + 1) * 128)
        if i == 0:
            total = dy[rows, :].astype(F32)
        else:
            total = mm(rotation(i - 1, back), dy[QROWS:, :])
        shares[:, rows] = total.T.astype(BF)

    def features(section):
        size = out_back.shape[1]
        return shares.at[pl.ds(pl.multiple_of(section * size, 16), size), :]

    def back_to(i, to):
        return pltpu.make_async_remote_copy(
            src_ref=features(to),
            dst_ref=out_back.at[i],
            send_sem=in_send.at[i],
            recv_sem=in_recv.at[i],
            device_id=(to, b),
            device_id_type=MESH,
        )

    own_share = pltpu.make_async_copy(features(s), out_back.at[3], in_send.at[3])
    own_share.start()

    @pl.when(mine)
    def _():
        for i, to in enumerate((x, y, xy)):
            back_to(i, to).start()

    lax.fori_loop(24, slots, slot, 0)

    def drain(which, chunk):
        twin_copy(which, chunk, True).wait_recv()
        twin_copy(which, chunk, True).wait_send()
        keep_copy(which, chunk, True).wait()
        if STREAMS[which][3]:
            one(which, chunk, 0).wait_send()
            one(which, chunk, 1).wait_send()
        else:
            one(which, chunk, 0).wait_send()
            one(which, chunk, 1).wait_send()
        two(which, chunk).wait_send()
        if layers > 1 and middle > 0:

            @pl.when(depth < middle)
            def _():
                inward(which, chunk, False).wait_send()

            @pl.when(depth > 0)
            def _():
                outward_copy(which, chunk, True).wait_send()

    def last(k, unused):
        guarded(k, drain)
        return unused

    lax.fori_loop(0, sum(CHUNKS), last, 0)
    for i in range(3):
        swap_copy(0, i).wait_send()
    own_share.wait()

    @pl.when(mine)
    def _():
        for i, to in enumerate((x, y, xy)):
            back_to(i, to).wait_send()
        back_to(1, y).wait_recv()

    @pl.when(jnp.logical_not(mine))
    def _():
        back_to(0, x).wait_recv()
        back_to(2, xy).wait_recv()


def backward(first_all, rest_all, vec, kept, dw, tails, bound, width, layers, lags=(2, 2)):
    anywhere = pl.BlockSpec(memory_space=pl.ANY)
    inside = pl.BlockSpec(memory_space=pltpu.VMEM)
    shapes = [(rows, columns) for rows, columns, unused, unused2 in STREAMS]
    most = max(CHUNKS)
    return pl.pallas_call(
        partial(backward_kernel, layers, lags),
        in_specs=[anywhere] * 11 + [inside] * 3,
        out_specs=[anywhere] * 4,
        out_shape=[jax.ShapeDtypeStruct((2,) + shape, BF) for shape in shapes]
        + [jax.ShapeDtypeStruct((4, width, ROWS), BF)],
        scratch_shapes=[pltpu.VMEM((4,) + shape, BF) for shape in shapes]
        + [pltpu.VMEM((2,) + shape, BF) for shape in shapes]
        + [pltpu.VMEM(shape, BF) for shape in shapes] * 3
        + [
            pltpu.VMEM((ROWS, D), BF),
            pltpu.VMEM((ROWS, D), BF),
            pltpu.VMEM((ROWS, 128), F32),
            pltpu.VMEM((ROWS, 2 * D), BF),
            pltpu.VMEM((D, FRONT), BF),
            pltpu.VMEM((HALF, D), BF),
            pltpu.VMEM((2, ROWS, HALF), BF),
            pltpu.VMEM((2, HALF, D), BF),
            pltpu.VMEM((ROWS, D), BF),
            pltpu.VMEM((ROWS, D), BF),
            pltpu.VMEM((ROWS, 128), F32),
            pltpu.VMEM((ROWS, FRONT), BF),
            pltpu.VMEM((ROWS, HALF), BF),
            pltpu.VMEM((PAIRS, 8, ROWS), F32),
            pltpu.VMEM((D, FRONT), BF),
            pltpu.VMEM((HALF, D), BF),
            pltpu.VMEM((4 * EXTRA, D), BF),
            pltpu.VMEM((ROWS, D), BF),
            pltpu.VMEM((ROWS, HALF), BF),
            pltpu.VMEM((ROWS, D), BF),
            pltpu.VMEM((2, ROWS, D), BF),
            pltpu.VMEM((D, ROWS), BF),
            pltpu.SemaphoreType.DMA((22,)),
            pltpu.SemaphoreType.DMA((2, 2)),
            pltpu.SemaphoreType.DMA((4, 3)),
            pltpu.SemaphoreType.DMA((4, 3)),
            pltpu.SemaphoreType.DMA((18, most)),
            pltpu.SemaphoreType.DMA((18, most)),
            pltpu.SemaphoreType.DMA((3, most)),
            pltpu.SemaphoreType.DMA((4,)),
            pltpu.SemaphoreType.DMA((4,)),
        ],
        compiler_params=pltpu.CompilerParams(
            collective_id=2, has_side_effects=True, vmem_limit_bytes=62 * 1024 * 1024
        ),
    )(first_all, rest_all, *kept, tails, bound, vec, dw)


def assemble_kernel(
    queries_all,
    first_ref,
    side_ref,
    down_ref,
    back_ref,
    out_ref,
    down_out,
    input_out,
    bias_out,
    gain_out,
    shift_out,
    projection_out,
    loss_out,
):
    s, b = lax.axis_index("section"), lax.axis_index("batch")
    row = pl.program_id(0)

    @pl.when(s % 2 == 0)
    def _():
        for core in range(2):
            for i in range(PAIRS):
                for t in range(3):
                    to = t * D + core * HALF + i * 128
                    at = (3 * i + t) * 128
                    out_ref[:, to : to + 128] = first_ref[core, :, at : at + 128].astype(F32)
        from_core = row // 3
        at = pl.multiple_of((row % 3) * 128, 128)
        out_ref[:, 3 * D :] = side_ref[from_core, pl.ds(at, 128), :].astype(F32)

    @pl.when(s % 2 == 1)
    def _():
        lanes = pl.ds(pl.multiple_of(row * 128, 128), 128)
        for core in range(2):
            out_ref[:, core * D : (core + 1) * D] = first_ref[core, :, 0:D].astype(F32)
            at = 2 * D + core * D
            out_ref[:, at : at + HALF] = first_ref[core, :, D:].astype(F32)
            out_ref[:, at + HALF : at + D] = side_ref[core, 0:HALF, lanes].astype(F32).T

    down_out[...] = down_ref[...].astype(F32)
    mine = b % 2 == s % 2
    same = jnp.where(mine, back_ref[3].astype(F32), back_ref[0].astype(F32))
    other = jnp.where(mine, back_ref[1].astype(F32), back_ref[2].astype(F32))
    for m in range(2):
        input_out[m] = jnp.where(s // 2 == m, same, other)

    @pl.when(row == 0)
    def _():
        vectors = side_ref[0, HALF : HALF + 16, :].astype(F32)
        bias_out[...] = vectors[0:1]
        gain_out[...] = vectors[1:2]
        shift_out[...] = vectors[2:3]
        loss_out[...] = jnp.sum(vectors[3:4], axis=1, keepdims=True) * (1.0 / queries_all)
        projection_out[...] = side_ref[0, HALF + 16 :, :].astype(F32)


def assemble(first_sum, side_sum, down_sum, back, queries_all):
    width = back.shape[1]
    steps = D // 128

    def whole(shape):
        return pl.BlockSpec(shape, lambda i: (0,) * len(shape))

    return pl.pallas_call(
        partial(assemble_kernel, queries_all),
        grid=(steps,),
        in_specs=[
            pl.BlockSpec((2, 128, FRONT), lambda i: (0, i, 0)),
            whole((2, SIDE, D)),
            pl.BlockSpec((256, D), lambda i: (i, 0)),
            pl.BlockSpec((4, width, 128), lambda i: (0, 0, i)),
        ],
        out_specs=[
            pl.BlockSpec((128, 4 * D), lambda i: (i, 0)),
            pl.BlockSpec((256, D), lambda i: (i, 0)),
            pl.BlockSpec((2, width, 128), lambda i: (0, 0, i)),
            whole((1, D)),
            whole((1, D)),
            whole((1, D)),
            whole((EXTRA, D)),
            whole((1, 1)),
        ],
        out_shape=[
            jax.ShapeDtypeStruct(shape, F32)
            for shape in (
                (D, 4 * D),
                (2 * D, D),
                (2, width, ROWS),
                (1, D),
                (1, D),
                (1, D),
                (EXTRA, D),
                (1, 1),
            )
        ],
        compiler_params=pltpu.CompilerParams(vmem_limit_bytes=60 * 1024 * 1024),
    )(first_sum, side_sum, down_sum.reshape(2 * D, D), back)


def gelu_and_slope(z):
    upper = 0.5 * (1.0 + lax.erf(z * 0.7071067811865476))
    density = jnp.exp(-0.5 * z * z) * 0.3989422804014327
    return (z * upper).astype(BF), (upper + z * density).astype(BF)


def on_device(
    inputs,
    in_weight,
    down_weight,
    out_bias,
    norm_gains,
    norm_shifts,
    projection,
    passage_lengths,
    positive,
):
    batches = lax.axis_size("batch")
    layers = batches // 2
    queries_all = inputs.shape[0] * batches * QUERY_COUNT
    first_all, rest_all, vectors, *kept, dw, tails, bound = forward(
        in_weight[0],
        down_weight,
        inputs.transpose(0, 2, 1),
        projection.T,
        (out_bias, norm_gains, norm_shifts),
        passage_lengths[:, 0],
        positive,
        layers,
        queries_all,
    )
    first_sum, side_sum, down_sum, back = backward(
        first_all, rest_all, vectors, kept, dw, tails, bound, inputs.shape[2], layers
    )
    in_grad, down_grad, input_grad, bias_grad, gain_grad, shift_grad, projection_grad, loss = (
        assemble(first_sum, side_sum, down_sum, back, queries_all)
    )
    return (
        loss[0, 0],
        input_grad.transpose(0, 2, 1),
        in_grad[None],
        down_grad,
        bias_grad,
        gain_grad,
        shift_grad,
        projection_grad.T,
    )


def solution(mesh):
    in_specs = (
        P(None, "batch", "section"),
        P("section", None, None),
        P("section", None),
        P("section", None),
        P("section", None),
        P("section", None),
        P(None, "section"),
        P(None, "batch", None),
        P(None, "batch"),
    )
    out_specs = (
        P(),
        P(None, "batch", "section"),
        P("section", None, None),
        P("section", None),
        P("section", None),
        P("section", None),
        P("section", None),
        P(None, "section"),
    )
    return jax.shard_map(
        on_device, mesh=mesh, in_specs=in_specs, out_specs=out_specs, check_vma=False
    )
```

```python
from functools import partial

import jax
import jax.numpy as jnp
from jax import lax
from jax.experimental import pallas as pl
from jax.experimental.pallas import tpu as pltpu
from jax.sharding import PartitionSpec as P

D = 768
HEADS = 12
FF = 3072
DIM = 128
QUERY_LENGTH = 32
QUERY_COUNT = 4
PASSAGE_COUNT = 3
PASSAGE_TOKENS = 640
PLEN = 512
QROWS = QUERY_LENGTH * QUERY_COUNT
ROWS = QROWS + PASSAGE_TOKENS
REST = PASSAGE_TOKENS - PLEN
SOFTMAX_DIVISOR = 0.1
SIMILARITY_SCALE = 0.25
NORM_EPSILON = 1e-06
MASKED = -1000000000.0
BF = jnp.bfloat16
F32 = jnp.float32
BLOCKS = ((0, QROWS), (QROWS, PLEN), (QROWS + PLEN, REST))
PAIRS = HEADS // 4
HALF = D // 2


def mm(a, b, dims=((1,), (0,))):
    return lax.dot_general(a, b, (dims, ((), ())), preferred_element_type=F32)


def block_mask(which, bound, rows):
    t = lax.broadcasted_iota(jnp.int32, (rows, rows), 0)
    r = lax.broadcasted_iota(jnp.int32, (rows, rows), 1)
    if which == 0:
        return (t // QUERY_LENGTH) == (r // QUERY_LENGTH)
    return ((t.astype(F32) < bound).astype(F32) - (r.astype(F32) < bound).astype(F32)) == 0.0


def unit_matrix(n):
    r = lax.broadcasted_iota(jnp.int32, (n, n), 0)
    c = lax.broadcasted_iota(jnp.int32, (n, n), 1)
    return (r == c).astype(F32).astype(BF)


def rotation(i, begins):
    r = lax.broadcasted_iota(jnp.int32, (128, PASSAGE_TOKENS), 0).astype(F32) + float(i * 128)
    c = lax.broadcasted_iota(jnp.int32, (128, PASSAGE_TOKENS), 1).astype(F32)
    ahead = c - r - begins
    total = float(PASSAGE_TOKENS)
    return ((ahead == 0.0) | (ahead == -total) | (ahead == total)).astype(F32).astype(BF)


MESH = pl.DeviceIdType.MESH
EXTRA = 32
FRONT = 1152
SPREAD = 960


def neighbours():
    s, b = lax.axis_index("section"), lax.axis_index("batch")
    x = s + 1 - 2 * (s % 2)
    y = s + 2 - 4 * (s // 2)
    xy = 3 - s
    return s, b, x, y, xy


def greet(layers):
    s, b, x, y, xy = neighbours()
    z, core = b // 2, b % 2
    barrier = pltpu.get_barrier_semaphore()

    def signal(to):
        pl.semaphore_signal(barrier, inc=1, device_id=to, device_id_type=MESH)

    signal((x, b))
    signal((y, b))
    signal((xy, b))
    signal((s, b + 1 - 2 * core))
    if layers > 1:

        @pl.when(z > 0)
        def _():
            signal((s, b - 2))

        @pl.when(z < layers - 1)
        def _():
            signal((s, b + 2))

        ends = (layers - 1 - z) // (layers - 1) + z // (layers - 1)
        pl.semaphore_wait(barrier, 6 - ends)
    else:
        pl.semaphore_wait(barrier, 4)


def forward_kernel(layers, spread, queries_all, *refs):
    w_ref, down_ref, slices_ref, projection_ref = refs[0:4]
    bias_ref, gain_ref, shift_ref, lengths_ref, positive_ref = refs[4:9]
    first_out, rest_out, vec_out, h_out, xhat_out, scale_out, qkv_out, ctx_out = refs[9:17]
    lse_out, act_out, slope_out, dw_out, tails_out, bound_out = refs[17:23]
    (
        first_all,
        rest_all,
        vec_all,
        tokens,
        ints_ref,
        ints_other,
        vec_ref,
        wide,
        out_stage,
        down_stage,
        hs,
        xhats,
        scales,
        qkvs,
        ctxs,
        lses,
        acts,
        slopes,
        part_out,
        part_in,
        proj,
        embedded,
        unit,
        length,
        grad_unit,
        grad_low,
        tails,
        load_sem,
        send_sem,
        recv_sem,
        z_send,
        z_recv,
        in_send,
        in_recv,
        part_send,
        part_recv,
        save_sem,
    ) = refs[23:]
    s, b, x, y, xy = neighbours()
    z, core = b // 2, b % 2
    micro = s // 2
    mine = core == s % 2
    twin = b + 1 - 2 * core

    def load(src, dst, i):
        return pltpu.make_async_copy(src, dst, load_sem.at[i])

    loads = [load(down_ref.at[pl.ds(core * D, D), :], down_stage, 0)]
    even, odd = [], []
    for i in range(PAIRS):
        for t in range(3):
            at = pl.multiple_of(t * D + core * HALF + i * 128, 128)
            to = (3 * i + t) * 128
            even.append(
                load(w_ref.at[:, pl.ds(at, 128)], wide.at[:, pl.ds(to, 128)], 1 + 3 * i + t)
            )
    even.append(load(w_ref.at[pl.ds(core * HALF, HALF), pl.ds(3 * D, D)], out_stage, 10))
    for i in range(2):
        at = pl.multiple_of(i * 2 * D + core * D, 128)
        odd.append(load(w_ref.at[:, pl.ds(at, D)], wide.at[:, pl.ds(i * D, D)], 11 + i))
    loads[0].start()

    @pl.when(s % 2 == 0)
    def _():
        for copy in even:
            copy.start()

    @pl.when(s % 2 == 1)
    def _():
        for copy in odd:
            copy.start()

    first, rest = first_all.at[s], rest_all.at[s]
    ints_ref[...] = jnp.zeros_like(ints_ref)
    ints_ref[0:2, 0:PASSAGE_COUNT] = lengths_ref[...]
    ints_ref[8:10, 0:QUERY_COUNT] = positive_ref[...]
    vec_ref[0:1, :] = bias_ref[...]
    vec_ref[1:2, :] = gain_ref[...]
    vec_ref[2:3, :] = shift_ref[...]
    vec_ref[3:8, :] = jnp.zeros((5, D), F32)
    own_vec = pltpu.make_async_copy(vec_ref, vec_all.at[s], load_sem.at[15])
    own_vec.start()
    rest[FRONT : FRONT + EXTRA, :] = projection_ref[...].astype(BF)
    greet(layers)

    def features(section):
        size = slices_ref.shape[1]
        return tokens.at[pl.ds(pl.multiple_of(section * size, 16), size), :]

    def feature_copy(i, which, section, to):
        return pltpu.make_async_remote_copy(
            src_ref=slices_ref.at[which],
            dst_ref=features(section),
            send_sem=in_send.at[i],
            recv_sem=in_recv.at[i],
            device_id=(to, b),
            device_id_type=MESH,
        )

    def to_twin(i, src, dst):
        return pltpu.make_async_remote_copy(
            src_ref=src,
            dst_ref=dst,
            send_sem=in_send.at[i],
            recv_sem=in_recv.at[i],
            device_id=(s, twin),
            device_id_type=MESH,
        )

    def quarter_to_twin(i, f):
        return to_twin(i, features(f), features(f))

    swap_ints = to_twin(7, ints_ref, ints_other)
    own_quarter = pltpu.make_async_copy(slices_ref.at[micro], features(s), load_sem.at[14])
    swap_ints.start()

    def send_features():
        @pl.when(mine)
        def _():
            own_quarter.start()
            feature_copy(1, 1 - micro, s, y).start()

        @pl.when(jnp.logical_not(mine))
        def _():
            feature_copy(0, micro, s, x).start()
            feature_copy(2, 1 - micro, s, xy).start()

    loads[0].wait()

    @pl.loop(0, D // 96)
    def _(i):
        rows = pl.ds(pl.multiple_of(i * 96, 16), 96)
        to = pl.ds(pl.multiple_of(HALF + i * 96, 16), 96)
        rest[to, :] = down_stage[rows, :].astype(BF)

    @pl.when(s % 2 == 0)
    def _():
        for copy in even:
            copy.wait()

        @pl.loop(0, HALF // 96)
        def _(i):
            rows = pl.ds(pl.multiple_of(i * 96, 16), 96)
            rest[rows, :] = out_stage[rows, :].astype(BF)

    @pl.when(s % 2 == 1)
    def _():
        for copy in odd:
            copy.wait()
        for i in range(3):
            for j in range(6):
                block = wide[j * 128 : (j + 1) * 128, FRONT + i * 128 : FRONT + (i + 1) * 128]
                rest[i * 128 : (i + 1) * 128, j * 128 : (j + 1) * 128] = block.T.astype(BF)

    quarter = D // 4
    firsts = [(first, first_all, i * quarter, quarter, i < 2) for i in range(4)]
    seconds = [(rest, rest_all, i * 96, 96, i == 0) for i in range(2)]
    small = [
        (rest, rest_all, FRONT, EXTRA, True),
        (vec_ref, vec_all, 0, 8, False),
    ]
    if spread:
        share = SPREAD // layers
        at = pl.multiple_of(FRONT - SPREAD + z * share, 16)
        half = share // 32 * 16
        slices = [
            (rest, rest_all, at, half, True),
            (rest, rest_all, pl.multiple_of(at + half, 16), share - half, False),
        ]
    else:
        slices = []
        seconds = [(rest, rest_all, i * 192, 192, i % 2 == 0) for i in range(6)]
    pieces = slices + firsts + seconds + small

    def part(n, ref):
        unused, unused, row, rows, unused = pieces[n]
        return ref.at[pl.ds(row, rows), :]

    def remote(n, kind, src, dst, to):
        return pltpu.make_async_remote_copy(
            src_ref=src,
            dst_ref=dst,
            send_sem=send_sem.at[kind, n],
            recv_sem=recv_sem.at[kind, n],
            device_id=(to, b),
            device_id_type=MESH,
        )

    def direct(n, kind):
        mine, every = pieces[n][:2]
        return remote(n, kind, part(n, mine), part(n, every.at[s]), y if kind else x)

    def arrived(n, kind):
        every = pieces[n][1]
        owner = (x, y, xy)[kind]
        here = part(n, every.at[owner])
        remote(n, kind, here, here, x).wait_recv()

    def relay(n):
        every, by_x = pieces[n][1], pieces[n][4]
        source = part(n, every.at[x if by_x else y])
        return remote(n, 2, source, source, y if by_x else x)

    def pass_on(n):
        arrived(n, 0 if pieces[n][4] else 1)
        relay(n).start()

    count = len(pieces)
    front = list(range(len(slices), len(slices) + 4))
    behind = list(range(len(slices) + 4, count))

    def along_x(n):
        direct(n, 0).start()

    def along_y(n):
        direct(n, 1).start()

    z_width = SPREAD // layers if spread else 0

    def z_part(section, owner_z):
        at = pl.multiple_of(FRONT - SPREAD + owner_z * z_width, 16)
        return rest_all.at[section, pl.ds(at, z_width), :]

    def z_copy(way, step, k, owner_z, to_b):
        source = z_part((x, y, xy)[k], owner_z)
        return pltpu.make_async_remote_copy(
            src_ref=source,
            dst_ref=source,
            send_sem=z_send.at[way, step, k],
            recv_sem=z_recv.at[way, step, k],
            device_id=(s, to_b),
            device_id_type=MESH,
        )

    def z_first(k):
        @pl.when(z < layers - 1)
        def _():
            z_copy(0, 0, k, z, b + 2).start()

        @pl.when(z > 0)
        def _():
            z_copy(1, 0, k, z, b - 2).start()

    def z_step(step):
        @pl.when(z >= step)
        def _():
            for k in range(3):
                z_copy(0, step - 1, k, z - step, b).wait_recv()

                @pl.when(z < layers - 1)
                def _():
                    z_copy(0, step, k, z - step, b + 2).start()

        @pl.when(z < layers - step)
        def _():
            for k in range(3):
                z_copy(1, step - 1, k, z + step, b).wait_recv()

                @pl.when(z > 0)
                def _():
                    z_copy(1, step, k, z + step, b - 2).start()

    def z_drain():
        for step in range(layers - 1):

            @pl.when((z < layers - 1) & (z >= step))
            def _():
                for k in range(3):
                    z_copy(0, step, k, z - step, b + 2).wait_send()

            @pl.when((z > 0) & (z + step < layers))
            def _():
                for k in range(3):
                    z_copy(1, step, k, z + step, b - 2).wait_send()

    for n in range(len(slices)):
        along_x(n)
        along_y(n)
    send_features()
    @pl.loop(0, D // 96)
    def _(i):
        rows = pl.ds(pl.multiple_of(i * 96, 16), 96)
        first[rows, :] = wide[rows, 0:FRONT].astype(BF)


    along_x(front[0])
    along_y(front[2])

    if spread:
        pass_on(0)
        pass_on(1)
    along_x(front[1])
    along_y(front[3])
    if spread:
        arrived(0, 1)
        arrived(1, 0)
        z_first(0)
        z_first(1)
    @pl.when(mine)
    def _():
        own_quarter.wait()
        quarter_to_twin(3, s).start()
        for i, owner in enumerate((x, y, xy)):
            feature_copy(i, 0, owner, x).wait_recv()
            quarter_to_twin(4 + i, owner).start()

    pass_on(front[0])
    pass_on(front[2])
    along_x(front[2])
    along_y(front[0])
    if spread:
        arrived(0, 2)
        arrived(1, 2)
        z_first(2)
    pass_on(front[1])
    pass_on(front[3])
    along_x(front[3])
    along_y(front[1])
    z_at = 1
    if spread and z_at < layers - 1:
        z_step(z_at)
        z_at += 1
    for n in behind:
        if pieces[n][4]:
            along_x(n)
        else:
            along_y(n)
    for n in behind:
        if pieces[n][4]:
            along_y(n)
        else:
            along_x(n)
    arrived(front[0], 1)
    arrived(front[2], 0)
    while spread and z_at < layers - 1:
        z_step(z_at)
        z_at += 1
    arrived(front[1], 1)
    arrived(front[3], 0)
    for n in front:
        arrived(n, 2)
    swap_ints.wait()
    own_vec.wait()

    @pl.when(jnp.logical_not(mine))
    def _():
        for i, owner in enumerate((s, x, y, xy)):
            quarter_to_twin(3 + i, owner).wait_recv()

    lane = lax.broadcasted_iota(jnp.int32, (1, 128), 1)

    def entry(first_row, i):
        row = pl.ds(first_row + micro, 1)
        values = jnp.where(mine, ints_ref[row, :].astype(F32), ints_other[row, :].astype(F32))
        return jnp.sum(jnp.where(lane == i, values, 0.0), axis=1, keepdims=True)

    sizes = [entry(0, i) for i in range(PASSAGE_COUNT)]
    is_long = [
        (sizes[0] == float(PLEN)).astype(F32),
        (sizes[1] == float(PLEN)).astype(F32),
        (sizes[2] == float(PLEN)).astype(F32),
    ]
    bound = is_long[0] * sizes[1] + is_long[1] * sizes[2] + is_long[2] * sizes[0]
    long_index = is_long[1] + 2.0 * is_long[2]
    begins = is_long[1] * sizes[0] + is_long[2] * (sizes[0] + sizes[1])

    saves = []

    def save(src, dst):
        copy = pltpu.make_async_copy(src, dst, save_sem.at[len(saves)])
        copy.start()
        saves.append(copy)

    save(first_all, first_out)

    def swap_copy(t, i):
        rows = pl.ds(i * 256, 256)
        return pltpu.make_async_remote_copy(
            src_ref=part_out.at[rows, :],
            dst_ref=part_in.at[t % 2, rows, :],
            send_sem=part_send.at[t, i],
            recv_sem=part_recv.at[t, i],
            device_id=(s, twin),
            device_id_type=MESH,
        )

    hs[0, 0:QROWS, :] = mm(unit_matrix(QROWS), tokens[:, 0:QROWS], ((1,), (1,))).astype(BF)
    for i in range(PASSAGE_TOKENS // 128):
        rows = slice(QROWS + i * 128, QROWS + (i + 1) * 128)
        hs[0, rows, :] = mm(rotation(i, begins), tokens[:, QROWS:], ((1,), (1,))).astype(BF)
    save(hs.at[0], h_out.at[0])

    def norm_rows(t, i):
        bias, gain, shift = vec_all[t, 0:1, :], vec_all[t, 1:2, :], vec_all[t, 2:3, :]
        swap_copy(t, i).wait_recv()

        def body(j, unused):
            rows = pl.ds(pl.multiple_of(j * 128, 128), 128)
            u = (
                hs[t, rows, :].astype(F32)
                + part_out[rows, :].astype(F32)
                + part_in[t % 2, rows, :].astype(F32)
                + bias
            )
            centered = u - jnp.mean(u, -1, keepdims=True)
            scale = lax.rsqrt(jnp.mean(centered * centered, -1, keepdims=True) + NORM_EPSILON)
            xhat = centered * scale
            xhats[t, rows, :] = xhat.astype(BF)
            scales[t, rows, :] = jnp.broadcast_to(scale, (128, 128))
            hs[t + 1, rows, :] = (xhat * gain + shift).astype(BF)
            return unused

        lax.fori_loop(2 * i, 2 * i + 2, body, 0)

    def save_norm(t):
        save(xhats.at[t], xhat_out.at[t])
        save(scales.at[t], scale_out.at[t])
        if t < 3:
            save(hs.at[t + 1], h_out.at[t + 1])

    def attention_pair(l):
        def pair(i, unused):
            base = pl.multiple_of(i * 384, 128)
            q_at = pl.ds(base, 128)
            k_at = pl.ds(pl.multiple_of(base + 128, 128), 128)
            v_at = pl.ds(pl.multiple_of(base + 256, 128), 128)
            c_at = pl.ds(pl.multiple_of(i * 128, 128), 128)
            for which, (begin, size) in enumerate(BLOCKS):
                chunk = size
                span = slice(begin, begin + size)
                k = qkvs[l, span, k_at]
                v = qkvs[l, span, v_at]
                for at in range(begin, begin + size, chunk):
                    rows = slice(at, at + chunk)
                    q = qkvs[l, rows, q_at]
                    total = None
                    for head in range(2):
                        own = (lane < 64) if head == 0 else (lane >= 64)
                        qm = jnp.where(own, q, jnp.zeros_like(q)) * BF(0.125)
                        vm = jnp.where(own, v, jnp.zeros_like(v))
                        score = mm(k, qm, ((1,), (1,)))
                        if which != 1:
                            score = jnp.where(block_mask(which, bound, size), score, MASKED)
                        top = jnp.max(score, axis=0, keepdims=True)
                        e = jnp.exp(score - top)
                        weight = jnp.sum(e, axis=0, keepdims=True)
                        part = mm(vm, e.astype(BF), ((0,), (0,))) * (1.0 / weight)
                        total = part if total is None else total + part
                        lses[l, i, head : head + 1, rows] = top + jnp.log(weight)
                    ctxs[l, rows, c_at] = total.T.astype(BF)
            return unused

        lax.fori_loop(0, PAIRS, pair, 0)

    def attention_layer(l):
        t = 2 * l
        for i in range(3):
            rows = slice(i * 256, (i + 1) * 256)
            if t > 0:
                norm_rows(t - 1, i)
            qkvs[l, rows, :] = mm(hs[t, rows, :], first_all[t]).astype(BF)
        if t > 0:
            save_norm(t - 1)
        save(qkvs.at[l], qkv_out.at[l])
        if l == 0:
            for n in behind:
                pass_on(n)
        attention_pair(l)
        if l == 0:
            for n in behind:
                arrived(n, 1 if pieces[n][4] else 0)
                arrived(n, 2)
            if spread:
                z_step(layers - 1)
        save(ctxs.at[l], ctx_out.at[l])
        save(lses.at[l], lse_out.at[l])
        for i in range(3):
            rows = slice(i * 256, (i + 1) * 256)
            if t > 0:
                swap_copy(t - 1, i).wait_send()
            part_out[rows, :] = mm(ctxs[l, rows, :], rest_all[t, 0:HALF, :]).astype(BF)
            swap_copy(t, i).start()

    def ffn_layer(l):
        t = 2 * l + 1
        for i in range(3):
            rows = slice(i * 256, (i + 1) * 256)
            norm_rows(t - 1, i)
            x_rows = hs[t, rows, :]
            for j in range(4):
                columns = slice(j * HALF, (j + 1) * HALF)
                if j < 3:
                    value = mm(x_rows, first_all[t, :, columns])
                else:
                    value = mm(x_rows, rest_all[t, 0:HALF, :], ((1,), (1,)))
                act, slope = gelu_and_slope(value)
                acts[l, rows, columns] = act
                slopes[l, rows, columns] = slope
            swap_copy(t - 1, i).wait_send()
            part = mm(acts[l, rows, 0:D], rest_all[2 * l, HALF:FRONT, :])
            part = part + mm(acts[l, rows, D:], rest_all[2 * l + 1, HALF:FRONT, :])
            part_out[rows, :] = part.astype(BF)
            swap_copy(t, i).start()
        save_norm(t - 1)
        save(acts.at[l], act_out.at[l])
        save(slopes.at[l], slope_out.at[l])

    attention_layer(0)
    save(vec_all, vec_out)
    save(rest_all, rest_out)
    ffn_layer(0)
    attention_layer(1)
    ffn_layer(1)

    for t in range(4):
        proj[t * EXTRA : (t + 1) * EXTRA, :] = rest_all[t, FRONT : FRONT + EXTRA, :]
    for i in range(3):
        rows = slice(i * 256, (i + 1) * 256)
        norm_rows(3, i)
        w = mm(hs[4, rows, :], proj[...], ((1,), (1,)))
        r = lax.rsqrt(jnp.sum(w * w, -1, keepdims=True) + NORM_EPSILON)
        unit[rows, :] = w * r
        length[rows, :] = jnp.broadcast_to(r, (256, 128))
        embedded[rows, :] = (w * r).astype(BF)
    save_norm(3)
    queries, passages = embedded[0:QROWS, :], embedded[QROWS:, :]
    logits = mm(queries, passages, ((1,), (1,))) * (1.0 / SOFTMAX_DIVISOR)
    column = lax.broadcasted_iota(jnp.int32, (1, REST), 1).astype(F32)
    token = lax.broadcasted_iota(jnp.int32, (QROWS, 1), 0)
    before = column < bound
    softs, shares = [], []
    for p in range(3):
        if p == 0:
            score = logits[:, 0:PLEN]
            top = jnp.max(score, -1, keepdims=True)
            e = jnp.exp(score - top)
        else:
            score = logits[:, PLEN:]
            inside = before if p == 1 else jnp.logical_not(before)
            score = jnp.where(inside, score, MASKED)
            top = jnp.max(score, -1, keepdims=True)
            e = jnp.where(inside, jnp.exp(score - top), 0.0)
        weight = jnp.sum(e, -1, keepdims=True)
        softs.append(SOFTMAX_DIVISOR * (top + jnp.log(weight)))
        shares.append(e * (1.0 / weight))
    loss = jnp.zeros((1, 1), F32)
    grad_softs = [jnp.zeros((QROWS, 1), F32) for p in range(3)]
    for q in range(QUERY_COUNT):
        mine_rows = (token // QUERY_LENGTH) == q
        scores = [
            SIMILARITY_SCALE * jnp.sum(jnp.where(mine_rows, soft, 0.0), 0, keepdims=True)
            for soft in softs
        ]
        top = jnp.maximum(jnp.maximum(scores[0], scores[1]), scores[2])
        es = [jnp.exp(score - top) for score in scores]
        weight = es[0] + es[1] + es[2]
        wanted = entry(8, q) - long_index
        wanted = jnp.where(wanted < 0.0, wanted + 3.0, wanted)
        chosen = [(wanted == float(p)).astype(F32) for p in range(3)]
        picked = chosen[0] * scores[0] + chosen[1] * scores[1] + chosen[2] * scores[2]
        loss = loss + top + jnp.log(weight) - picked
        for p in range(3):
            grad = (es[p] / weight - chosen[p]) * (SIMILARITY_SCALE / queries_all)
            grad_softs[p] = jnp.where(mine_rows, grad, grad_softs[p])
    grad_logits = jnp.concatenate(
        [grad_softs[0] * shares[0], grad_softs[1] * shares[1] + grad_softs[2] * shares[2]], axis=1
    ).astype(BF)
    grad_unit[0:QROWS, :] = mm(grad_logits, passages)
    grad_unit[QROWS:, :] = mm(grad_logits, queries, ((0,), (0,)))
    for i in range(3):
        rows = slice(i * 256, (i + 1) * 256)
        n, dn = unit[rows, :], grad_unit[rows, :]
        inner = jnp.sum(n * dn, -1, keepdims=True)
        grad_low[rows, :] = (length[rows, :] * (dn - n * inner)).astype(BF)
    save(grad_low, dw_out)
    grad_proj = mm(grad_low[...], hs[4], ((0,), (0,)))
    feature = lax.broadcasted_iota(jnp.int32, (16, D), 1)
    line = lax.broadcasted_iota(jnp.int32, (16, D), 0)
    head_rows = jnp.zeros((16, D), F32)
    left = loss
    for i, step in enumerate((8.0, 0.5, 2.0**-5, 2.0**-9, 2.0**-13, 2.0**-17)):
        value = jnp.floor(left * (1.0 / step)) * step
        left = left - value
        head_rows = jnp.where((line == 3) & (feature == i), value, head_rows)
    for t in range(4):
        tails[t, 0:16, :] = head_rows.astype(BF)
        tails[t, 16:TAIL, :] = grad_proj[t * EXTRA : (t + 1) * EXTRA, :].astype(BF)
    save(tails, tails_out)
    which_row = lax.broadcasted_iota(jnp.int32, (8, 1), 0)
    unit[0:8, :] = jnp.broadcast_to(jnp.where(which_row == 0, bound, begins), (8, 128))
    save(unit.at[pl.ds(0, 8), :], bound_out)

    for copy in saves:
        copy.wait()
    for i in range(3):
        swap_copy(3, i).wait_send()
    for n in range(count):
        direct(n, 0).wait_send()
        direct(n, 1).wait_send()
        relay(n).wait_send()
    if spread:
        z_drain()

    @pl.when(mine)
    def _():
        feature_copy(1, 1 - micro, s, y).wait_send()
        for i, owner in enumerate((s, x, y, xy)):
            quarter_to_twin(3 + i, owner).wait_send()

    @pl.when(jnp.logical_not(mine))
    def _():
        feature_copy(0, micro, s, x).wait_send()
        feature_copy(2, 1 - micro, s, xy).wait_send()


def forward(w, down, slices, projection, vectors, lengths, positive, layers, queries_all):
    spread = layers > 1 and SPREAD % (16 * layers) == 0 and SPREAD >= 32 * layers
    anywhere = pl.BlockSpec(memory_space=pl.ANY)
    inside = pl.BlockSpec(memory_space=pltpu.VMEM)
    pieces = 12 if not spread else 10
    steps = max(layers - 1, 1) if spread else 1
    kept = [
        ((4, D, FRONT), BF),
        ((4, FRONT + EXTRA, D), BF),
        ((4, 8, D), F32),
        ((4, ROWS, D), BF),
        ((4, ROWS, D), BF),
        ((4, ROWS, 128), F32),
        ((2, ROWS, FRONT), BF),
        ((2, ROWS, HALF), BF),
        ((2, PAIRS, 8, ROWS), F32),
        ((2, ROWS, 2 * D), BF),
        ((2, ROWS, 2 * D), BF),
        ((ROWS, DIM), BF),
        ((4, TAIL, D), BF),
        ((8, 128), F32),
    ]
    return pl.pallas_call(
        partial(forward_kernel, layers, spread, queries_all),
        in_specs=[anywhere] * 3 + [inside] * 6,
        out_specs=[anywhere] * len(kept),
        out_shape=[jax.ShapeDtypeStruct(shape, kind) for shape, kind in kept],
        scratch_shapes=[
            pltpu.VMEM((4, D, FRONT), BF),
            pltpu.VMEM((4, FRONT + EXTRA, D), BF),
            pltpu.VMEM((4, 8, D), F32),
            pltpu.VMEM((D, ROWS), BF),
            pltpu.VMEM((16, 128), jnp.int32),
            pltpu.VMEM((16, 128), jnp.int32),
            pltpu.VMEM((8, D), F32),
            pltpu.VMEM((D, 2 * D), F32),
            pltpu.VMEM((HALF, D), F32),
            pltpu.VMEM((D, D), F32),
            pltpu.VMEM((5, ROWS, D), BF),
            pltpu.VMEM((4, ROWS, D), BF),
            pltpu.VMEM((4, ROWS, 128), F32),
            pltpu.VMEM((2, ROWS, FRONT), BF),
            pltpu.VMEM((2, ROWS, HALF), BF),
            pltpu.VMEM((2, PAIRS, 8, ROWS), F32),
            pltpu.VMEM((2, ROWS, 2 * D), BF),
            pltpu.VMEM((2, ROWS, 2 * D), BF),
            pltpu.VMEM((ROWS, D), BF),
            pltpu.VMEM((2, ROWS, D), BF),
            pltpu.VMEM((DIM, D), BF),
            pltpu.VMEM((ROWS, DIM), BF),
            pltpu.VMEM((ROWS, DIM), F32),
            pltpu.VMEM((ROWS, DIM), F32),
            pltpu.VMEM((ROWS, DIM), F32),
            pltpu.VMEM((ROWS, DIM), BF),
            pltpu.VMEM((4, TAIL, D), BF),
            pltpu.SemaphoreType.DMA((16,)),
            pltpu.SemaphoreType.DMA((3, pieces)),
            pltpu.SemaphoreType.DMA((3, pieces)),
            pltpu.SemaphoreType.DMA((2, steps, 3)),
            pltpu.SemaphoreType.DMA((2, steps, 3)),
            pltpu.SemaphoreType.DMA((8,)),
            pltpu.SemaphoreType.DMA((8,)),
            pltpu.SemaphoreType.DMA((4, 3)),
            pltpu.SemaphoreType.DMA((4, 3)),
            pltpu.SemaphoreType.DMA((32,)),
        ],
        compiler_params=pltpu.CompilerParams(
            collective_id=1, has_side_effects=True, vmem_limit_bytes=62 * 1024 * 1024
        ),
    )(w, down, slices, projection, *vectors, lengths, positive)


TAIL = 48
SIDE = HALF + TAIL
STREAMS = ((D, FRONT, 32, True), (SIDE, D, 48, False), (D, D, 32, True))
CHUNKS = tuple(rows // step for rows, unused, step, unused2 in STREAMS)
OFFSETS = (CHUNKS[2], CHUNKS[2] + CHUNKS[0], 0)
TWO_OFFSETS = (CHUNKS[2], 0, 0)
ONE_LOW, ONE_HIGH, TWO, INWARD, BACK, TWIN = 0, 3, 6, 9, 12, 15


def backward_kernel(layers, lags, *refs):
    first_all, rest_all, hs, xhats, scales, qkvs, ctxs, lses, acts, slopes, tails = refs[0:11]
    bound_ref, vec_ref, dw_ref = refs[11:14]
    outs, out_back = refs[14:17], refs[17]
    sums, ones, twos, ins, backs = refs[18:21], refs[21:24], refs[24:27], refs[27:30], refs[30:33]
    (
        h_f,
        xhat_f,
        scale_f,
        slope,
        up_first,
        up_second,
        act_ring,
        down_ring,
        h_a,
        xhat_a,
        scale_a,
        qkv,
        ctx,
        lse,
        att_first,
        att_second,
        proj,
        dy,
        dc,
        part_out,
        part_in,
        shares,
        load_sem,
        ring_sem,
        part_send,
        part_recv,
        send_sem,
        recv_sem,
        keep_sem,
        in_send,
        in_recv,
    ) = refs[33:]
    s, b, x, y, xy = neighbours()
    z, core = b // 2, b % 2
    half = s // 2
    parity = s % 2
    mine = core == parity
    twin = b + 1 - 2 * core
    middle = max(layers // 2 - 1, 0)
    upper = z // max(layers // 2, 1)
    depth = z + upper * (layers - 1 - 2 * z)
    toward = b + 2 - 4 * upper
    outward = b - 2 + 4 * upper
    lag_z, lag_step = lags

    def load(src, dst, i):
        return pltpu.make_async_copy(src, dst, load_sem.at[i])

    def loads_ffn(l, begin=0, end=6):
        t = 2 * l + 1
        copies = [
            (xhats.at[t], xhat_f, 1),
            (scales.at[t], scale_f, 2),
            (slopes.at[l], slope, 3),
            (first_all.at[t], up_first, 4),
            (rest_all.at[t, pl.ds(0, HALF), :], up_second, 5),
            (hs.at[t], h_f, 0),
        ]
        return [load(*copy) for copy in copies[begin:end]]

    def loads_attention(l, begin=0, end=8):
        t = 2 * l
        copies = [
            (xhats.at[t], xhat_a, 7),
            (scales.at[t], scale_a, 8),
            (ctxs.at[l], ctx, 10),
            (qkvs.at[l], qkv, 9),
            (lses.at[l], lse, 11),
            (rest_all.at[t, pl.ds(0, HALF), :], att_second, 13),
            (first_all.at[t], att_first, 12),
            (hs.at[t], h_a, 6),
        ]
        return [load(*copy) for copy in copies[begin:end]]

    def ring(l, j):
        slot = j % 2
        rows = pl.ds(HALF + (j % 2) * HALF, HALF)
        return (
            pltpu.make_async_copy(
                acts.at[l, :, pl.ds(j * HALF, HALF)], act_ring.at[slot], ring_sem.at[0, slot]
            ),
            pltpu.make_async_copy(
                rest_all.at[2 * l + j // 2, rows, :], down_ring.at[slot], ring_sem.at[1, slot]
            ),
        )

    def start(copies):
        for copy in copies:
            copy.start()

    def wait(copies):
        for copy in copies:
            copy.wait()

    start_loads = [
        load(rest_all.at[t, pl.ds(FRONT, EXTRA), :], proj.at[pl.ds(t * EXTRA, EXTRA), :], 14 + t)
        for t in range(4)
    ] + [load(tails.at[t], sums[1].at[t, pl.ds(HALF, TAIL), :], 18 + t) for t in range(4)]
    start(start_loads)
    start(loads_ffn(1, 0, 2))
    start(ring(1, 0))
    start(loads_ffn(1, 2, 3))
    start(ring(1, 1))
    start(loads_ffn(1, 3))
    start(loads_attention(1))
    greet(layers)
    wait(start_loads)

    def remote(kind, chunk, src, dst, to):
        return pltpu.make_async_remote_copy(
            src_ref=src,
            dst_ref=dst,
            send_sem=send_sem.at[kind, chunk],
            recv_sem=recv_sem.at[kind, chunk],
            device_id=to,
            device_id_type=MESH,
        )

    def rows_of(which, chunk):
        size = STREAMS[which][2]
        return pl.ds(pl.multiple_of(chunk * size, 16), size)

    def one(which, chunk, l):
        rows = rows_of(which, chunk)
        kind = (ONE_HIGH if l else ONE_LOW) + which
        if STREAMS[which][3]:
            src = sums[which].at[2 * l + 1 - parity, rows, :]
            return remote(kind, chunk, src, ones[which].at[l, rows, :], (x, b))
        src = sums[which].at[2 * (1 - half) + l, rows, :]
        return remote(kind, chunk, src, ones[which].at[l, rows, :], (y, b))

    def forwarded(which):
        return 2 * (1 - half) + parity if STREAMS[which][3] else 2 * half + 1 - parity

    def two(which, chunk):
        rows = rows_of(which, chunk)
        src = sums[which].at[forwarded(which), rows, :]
        to = y if STREAMS[which][3] else x
        return remote(TWO + which, chunk, src, twos[which].at[rows, :], (to, b))

    def inward(which, chunk, swap):
        rows = rows_of(which, chunk)
        src = sums[which].at[s, rows, :]
        if swap:
            return remote(BACK + which, chunk, src, backs[which].at[rows, :], (s, toward))
        return remote(INWARD + which, chunk, src, ins[which].at[rows, :], (s, toward))

    def final(which, at_middle):
        return sums[which].at[s] if at_middle else backs[which]

    def outward_copy(which, chunk, at_middle):
        rows = rows_of(which, chunk)
        src = final(which, at_middle).at[rows, :]
        return remote(BACK + which, chunk, src, backs[which].at[rows, :], (s, outward))

    def twin_copy(which, chunk, at_middle):
        rows = rows_of(which, chunk)
        src = final(which, at_middle).at[rows, :]
        return remote(TWIN + which, chunk, src, outs[which].at[core, rows, :], (s, twin))

    def keep_copy(which, chunk, at_middle):
        rows = rows_of(which, chunk)
        src = final(which, at_middle).at[rows, :]
        return pltpu.make_async_copy(
            src, outs[which].at[core, rows, :], keep_sem.at[which, chunk]
        )

    def plus(*values):
        total = values[0].astype(F32)
        for value in values[1:]:
            total = total + value.astype(F32)
        return total

    def send_block(which, t, start_row, rows):
        size = STREAMS[which][2]
        by_x = STREAMS[which][3]

        @pl.when(parity != t % 2 if by_x else half != t // 2)
        def _():
            def body(c, unused):
                one(which, c, t // 2 if by_x else t % 2).start()
                return unused

            lax.fori_loop(start_row // size, (start_row + rows) // size, body, 0)

    def swap_copy(t, i):
        rows = pl.ds(i * 256, 256)
        return pltpu.make_async_remote_copy(
            src_ref=part_out.at[rows, :],
            dst_ref=part_in.at[t % 2, rows, :],
            send_sem=part_send.at[t, i],
            recv_sem=part_recv.at[t, i],
            device_id=(s, twin),
            device_id_type=MESH,
        )

    def norm_back(t, grad_of, xhat, scale):
        gain = vec_ref[t, 1:2, :]

        def body(i, carry):
            rows = pl.ds(pl.multiple_of(i * 128, 128), 128)
            grad = grad_of(rows)
            xh = xhat[rows, :].astype(F32)
            weighted = grad * gain
            mean_1 = jnp.mean(weighted, -1, keepdims=True)
            mean_2 = jnp.mean(weighted * xh, -1, keepdims=True)
            du = scale[rows, 0:1] * (weighted - mean_1 - xh * mean_2)
            dy[rows, :] = du.astype(BF)
            return (
                carry[0] + jnp.sum(du, 0, keepdims=True),
                carry[1] + jnp.sum(grad * xh, 0, keepdims=True),
                carry[2] + jnp.sum(grad, 0, keepdims=True),
            )

        zero = jnp.zeros((1, D), F32)
        carry = (zero, zero, zero)
        for i in range(3):
            if t < 3:
                swap_copy(t + 1, i).wait_recv()
            carry = lax.fori_loop(2 * i, 2 * i + 2, body, carry)
        row = lax.broadcasted_iota(jnp.int32, (16, 1), 0)
        block = sums[1][t, HALF : HALF + 16, :].astype(F32)
        for i in range(3):
            block = jnp.where(row == i, carry[i], block)
        sums[1][t, HALF : HALF + 16, :] = block.astype(BF)

    def grad_from_head(rows):
        return mm(dw_ref[rows, :], proj[...])

    def grad_from(t):
        def grad_of(rows):
            total = plus(dy[rows, :], part_out[rows, :], part_in[t % 2, rows, :])
            return total.astype(BF).astype(F32)

        return grad_of

    def ffn_back(l):
        t = 2 * l + 1
        for j in range(4):
            wait(ring(l, j))
            slot = j % 2
            columns = slice(j * HALF, (j + 1) * HALF)
            low = dy[...]
            to = (j % 2) * HALF
            sums[2][2 * l + j // 2, to : to + HALF, :] = mm(
                act_ring[slot], low, ((0,), (0,))
            ).astype(BF)
            send_block(2, 2 * l + j // 2, to, HALF)
            if j == 0:
                wait(loads_ffn(l, 2, 3))
            for i in range(3):
                rows = slice(i * 256, (i + 1) * 256)
                grad = mm(dy[rows, :], down_ring[slot], ((1,), (1,)))
                slope[rows, columns] = (grad * slope[rows, columns].astype(F32)).astype(BF)
            if j < 2:
                start(ring(l, j + 2))
        wait(loads_ffn(l, 3))
        for i in range(3):
            rows = slice(i * 256, (i + 1) * 256)
            if t < 3:
                swap_copy(t + 1, i).wait_send()
            part = mm(slope[rows, 0:FRONT], up_first[...], ((1,), (1,)))
            part = part + mm(slope[rows, FRONT:], up_second[...])
            part_out[rows, :] = part.astype(BF)
            swap_copy(t, i).start()
        for i in range(3):
            rows = slice(i * 256, (i + 1) * 256)
            sums[0][t, rows, :] = mm(h_f[:, rows], slope[:, 0:FRONT], ((0,), (0,))).astype(BF)
        sums[1][t, 0:HALF, :] = mm(slope[:, FRONT:], h_f[...], ((0,), (0,))).astype(BF)

    def attention_pair(i, unused):
        lane = lax.broadcasted_iota(jnp.int32, (1, 128), 1)
        base = pl.multiple_of(i * 384, 128)
        q_at, k_at, v_at = (
            pl.ds(base, 128),
            pl.ds(pl.multiple_of(base + 128, 128), 128),
            pl.ds(pl.multiple_of(base + 256, 128), 128),
        )
        c_at = pl.ds(pl.multiple_of(i * 128, 128), 128)
        for which, (begin, size) in enumerate(BLOCKS):
            chunk = size
            span = slice(begin, begin + size)
            k = qkv[span, k_at]
            v = qkv[span, v_at]
            dk = jnp.zeros((size, 128), F32)
            dv = jnp.zeros((size, 128), F32)
            for at in range(begin, begin + size, chunk):
                rows = slice(at, at + chunk)
                q = qkv[rows, q_at]
                dcs = dc[rows, c_at]
                dq = None
                for head in range(2):
                    own = (lane < 64) if head == 0 else (lane >= 64)
                    qm = jnp.where(own, q, jnp.zeros_like(q)) * BF(0.125)
                    dcm = jnp.where(own, dcs, jnp.zeros_like(dcs))
                    km = jnp.where(own, k, jnp.zeros_like(k))
                    score = mm(k, qm, ((1,), (1,)))
                    if which != 1:
                        score = jnp.where(block_mask(which, bound_ref[0:1, 0:1], size), score, MASKED)
                    p = jnp.exp(score - lse[i, head : head + 1, rows])
                    dp = mm(v, dcm, ((1,), (1,)))
                    inner = jnp.sum(p * dp, axis=0, keepdims=True)
                    ds = (p * (dp - inner)).astype(BF)
                    dv = dv + mm(p.astype(BF), dcm)
                    dk = dk + mm(ds, qm)
                    part = mm(km, ds, ((0,), (0,)))
                    dq = part if dq is None else dq + part
                qkv[rows, q_at] = (dq.T * 0.125).astype(BF)
            qkv[span, k_at] = dk.astype(BF)
            qkv[span, v_at] = dv.astype(BF)
        return unused

    def attention_grads(l):
        t = 2 * l
        sums[1][t, 0:HALF, :] = mm(ctx[...], dy[...], ((0,), (0,))).astype(BF)
        send_block(1, t, 0, SIDE)
        for i in range(3):
            rows = slice(i * 256, (i + 1) * 256)
            dc[rows, :] = mm(dy[rows, :], att_second[...], ((1,), (1,))).astype(BF)
        lax.fori_loop(0, PAIRS, attention_pair, 0)
        for i in range(3):
            rows = slice(i * 256, (i + 1) * 256)
            swap_copy(t + 1, i).wait_send()
            part_out[rows, :] = mm(qkv[rows, :], att_first[...], ((1,), (1,))).astype(BF)
            swap_copy(t, i).start()
        for i in range(3):
            rows = slice(i * 256, (i + 1) * 256)
            sums[0][t, rows, :] = mm(h_a[:, rows], qkv[...], ((0,), (0,))).astype(BF)

    def send_sections(t):
        if t % 2 == 1:
            send_block(1, t, 0, SIDE)
        send_block(0, t, 0, D)

    def came_one(which, chunk, l):
        one(which, chunk, l).wait_recv()

    def start_two(which, chunk):
        rows = rows_of(which, chunk)
        t = forwarded(which)
        if STREAMS[which][3]:
            came_one(which, chunk, 0)
            came_one(which, chunk, 1)
            got = ones[which][1 - half, rows, :]
        else:
            came_one(which, chunk, 0)
            came_one(which, chunk, 1)
            got = ones[which][1 - parity, rows, :]
        sums[which][t, rows, :] = plus(sums[which][t, rows, :], got).astype(BF)
        two(which, chunk).start()

    wait(loads_ffn(1, 0, 2))
    norm_back(3, grad_from_head, xhat_f, scale_f)
    ffn_back(1)
    send_sections(3)
    start(loads_ffn(0))
    start(ring(0, 0))
    start(ring(0, 1))
    wait(loads_attention(1))
    norm_back(2, grad_from(3), xhat_a, scale_a)
    attention_grads(1)
    send_sections(2)
    start(loads_attention(0))
    wait(loads_ffn(0, 0, 2))
    norm_back(1, grad_from(2), xhat_f, scale_f)
    ffn_back(0)
    send_sections(1)
    wait(loads_attention(0))
    norm_back(0, grad_from(1), xhat_a, scale_a)

    attention_grads(0)
    send_sections(0)

    def start_z(which, chunk):
        rows = rows_of(which, chunk)
        two(which, chunk).wait_recv()
        got = ones[which][half if STREAMS[which][3] else parity, rows, :]
        total = plus(sums[which][s, rows, :], got, twos[which][rows, :])
        if layers == 1:
            sums[which][s, rows, :] = total.astype(BF)
            twin_copy(which, chunk, True).start()
            keep_copy(which, chunk, True).start()
            return
        if middle > 0:

            @pl.when(depth > 0)
            def _():
                inward(which, chunk, False).wait_recv()
                sums[which][s, rows, :] = plus(total, ins[which][rows, :]).astype(BF)

            @pl.when(depth == 0)
            def _():
                sums[which][s, rows, :] = total.astype(BF)

            @pl.when(depth < middle)
            def _():
                inward(which, chunk, False).start()

        else:
            sums[which][s, rows, :] = total.astype(BF)

        @pl.when(depth == middle)
        def _():
            inward(which, chunk, True).start()

    def finish(which, chunk):
        rows = rows_of(which, chunk)
        inward(which, chunk, True).wait_recv()

        @pl.when(depth == middle)
        def _():
            inward(which, chunk, True).wait_send()
            sums[which][s, rows, :] = plus(
                sums[which][s, rows, :], backs[which][rows, :]
            ).astype(BF)
            if middle > 0:
                outward_copy(which, chunk, True).start()
            twin_copy(which, chunk, True).start()
            keep_copy(which, chunk, True).start()

        if middle > 0:

            @pl.when(depth < middle)
            def _():
                @pl.when(depth > 0)
                def _():
                    outward_copy(which, chunk, False).start()

                twin_copy(which, chunk, False).start()
                keep_copy(which, chunk, False).start()

    lag3 = lag_z + lag_step * depth
    lag5 = lag_z + lag_step * (middle + 1) + lag_step * (middle - depth)
    slots = sum(CHUNKS) + lag_z + (lag_step * (2 * middle + 1) if layers > 1 else 0)

    def guarded(position, step, offsets=OFFSETS):
        for which, count in enumerate(CHUNKS):
            chunk = position - offsets[which]

            @pl.when((chunk >= 0) & (chunk < count))
            def _():
                step(which, chunk)

    def slot(k, unused):
        guarded(k, start_two, TWO_OFFSETS)
        guarded(k - lag3, start_z)
        if layers > 1:
            guarded(k - lag5, finish)
        return unused

    lax.fori_loop(0, 48, slot, 0)
    for i in range(3):
        swap_copy(0, i).wait_recv()

        def body(j, unused):
            rows = pl.ds(pl.multiple_of(j * 64, 64), 64)
            dy[rows, :] = plus(dy[rows, :], part_out[rows, :], part_in[0, rows, :]).astype(BF)
            return unused

        lax.fori_loop(4 * i, 4 * i + 4, body, 0)
    back = -bound_ref[1:2, 0:1]
    for i in range(6):
        rows = slice(i * 128, (i + 1) * 128)
        if i == 0:
            total = dy[rows, :].astype(F32)
        else:
            total = mm(rotation(i - 1, back), dy[QROWS:, :])
        shares[:, rows] = total.T.astype(BF)

    def features(section):
        size = out_back.shape[1]
        return shares.at[pl.ds(pl.multiple_of(section * size, 16), size), :]

    def back_to(i, to):
        return pltpu.make_async_remote_copy(
            src_ref=features(to),
            dst_ref=out_back.at[i],
            send_sem=in_send.at[i],
            recv_sem=in_recv.at[i],
            device_id=(to, b),
            device_id_type=MESH,
        )

    own_share = pltpu.make_async_copy(features(s), out_back.at[3], in_send.at[3])
    own_share.start()

    @pl.when(mine)
    def _():
        for i, to in enumerate((x, y, xy)):
            back_to(i, to).start()

    lax.fori_loop(48, slots, slot, 0)

    def drain(which, chunk):
        twin_copy(which, chunk, True).wait_recv()
        twin_copy(which, chunk, True).wait_send()
        keep_copy(which, chunk, True).wait()
        if STREAMS[which][3]:
            one(which, chunk, 0).wait_send()
            one(which, chunk, 1).wait_send()
        else:
            one(which, chunk, 0).wait_send()
            one(which, chunk, 1).wait_send()
        two(which, chunk).wait_send()
        if layers > 1 and middle > 0:

            @pl.when(depth < middle)
            def _():
                inward(which, chunk, False).wait_send()

            @pl.when(depth > 0)
            def _():
                outward_copy(which, chunk, True).wait_send()

    def last(k, unused):
        guarded(k, drain)
        return unused

    lax.fori_loop(0, sum(CHUNKS), last, 0)
    for i in range(3):
        swap_copy(0, i).wait_send()
    own_share.wait()

    @pl.when(mine)
    def _():
        for i, to in enumerate((x, y, xy)):
            back_to(i, to).wait_send()
        back_to(1, y).wait_recv()

    @pl.when(jnp.logical_not(mine))
    def _():
        back_to(0, x).wait_recv()
        back_to(2, xy).wait_recv()


def backward(first_all, rest_all, vec, kept, dw, tails, bound, width, layers, lags=(3, 2)):
    anywhere = pl.BlockSpec(memory_space=pl.ANY)
    inside = pl.BlockSpec(memory_space=pltpu.VMEM)
    shapes = [(rows, columns) for rows, columns, unused, unused2 in STREAMS]
    most = max(CHUNKS)
    return pl.pallas_call(
        partial(backward_kernel, layers, lags),
        in_specs=[anywhere] * 11 + [inside] * 3,
        out_specs=[anywhere] * 4,
        out_shape=[jax.ShapeDtypeStruct((2,) + shape, BF) for shape in shapes]
        + [jax.ShapeDtypeStruct((4, width, ROWS), BF)],
        scratch_shapes=[pltpu.VMEM((4,) + shape, BF) for shape in shapes]
        + [pltpu.VMEM((2,) + shape, BF) for shape in shapes]
        + [pltpu.VMEM(shape, BF) for shape in shapes] * 3
        + [
            pltpu.VMEM((ROWS, D), BF),
            pltpu.VMEM((ROWS, D), BF),
            pltpu.VMEM((ROWS, 128), F32),
            pltpu.VMEM((ROWS, 2 * D), BF),
            pltpu.VMEM((D, FRONT), BF),
            pltpu.VMEM((HALF, D), BF),
            pltpu.VMEM((2, ROWS, HALF), BF),
            pltpu.VMEM((2, HALF, D), BF),
            pltpu.VMEM((ROWS, D), BF),
            pltpu.VMEM((ROWS, D), BF),
            pltpu.VMEM((ROWS, 128), F32),
            pltpu.VMEM((ROWS, FRONT), BF),
            pltpu.VMEM((ROWS, HALF), BF),
            pltpu.VMEM((PAIRS, 8, ROWS), F32),
            pltpu.VMEM((D, FRONT), BF),
            pltpu.VMEM((HALF, D), BF),
            pltpu.VMEM((4 * EXTRA, D), BF),
            pltpu.VMEM((ROWS, D), BF),
            pltpu.VMEM((ROWS, HALF), BF),
            pltpu.VMEM((ROWS, D), BF),
            pltpu.VMEM((2, ROWS, D), BF),
            pltpu.VMEM((D, ROWS), BF),
            pltpu.SemaphoreType.DMA((22,)),
            pltpu.SemaphoreType.DMA((2, 2)),
            pltpu.SemaphoreType.DMA((4, 3)),
            pltpu.SemaphoreType.DMA((4, 3)),
            pltpu.SemaphoreType.DMA((18, most)),
            pltpu.SemaphoreType.DMA((18, most)),
            pltpu.SemaphoreType.DMA((3, most)),
            pltpu.SemaphoreType.DMA((4,)),
            pltpu.SemaphoreType.DMA((4,)),
        ],
        compiler_params=pltpu.CompilerParams(
            collective_id=2, has_side_effects=True, vmem_limit_bytes=62 * 1024 * 1024
        ),
    )(first_all, rest_all, *kept, tails, bound, vec, dw)


def assemble_kernel(
    queries_all,
    first_ref,
    side_ref,
    down_ref,
    back_ref,
    out_ref,
    down_out,
    input_out,
    bias_out,
    gain_out,
    shift_out,
    projection_out,
    loss_out,
):
    s, b = lax.axis_index("section"), lax.axis_index("batch")
    row = pl.program_id(0)

    @pl.when(s % 2 == 0)
    def _():
        for core in range(2):
            for i in range(PAIRS):
                for t in range(3):
                    to = t * D + core * HALF + i * 128
                    at = (3 * i + t) * 128
                    out_ref[:, to : to + 128] = first_ref[core, :, at : at + 128].astype(F32)
        from_core = row // 3
        at = pl.multiple_of((row % 3) * 128, 128)
        out_ref[:, 3 * D :] = side_ref[from_core, pl.ds(at, 128), :].astype(F32)

    @pl.when(s % 2 == 1)
    def _():
        lanes = pl.ds(pl.multiple_of(row * 128, 128), 128)
        for core in range(2):
            out_ref[:, core * D : (core + 1) * D] = first_ref[core, :, 0:D].astype(F32)
            at = 2 * D + core * D
            out_ref[:, at : at + HALF] = first_ref[core, :, D:].astype(F32)
            out_ref[:, at + HALF : at + D] = side_ref[core, 0:HALF, lanes].astype(F32).T

    down_out[...] = down_ref[...].astype(F32)
    mine = b % 2 == s % 2
    same = jnp.where(mine, back_ref[3].astype(F32), back_ref[0].astype(F32))
    other = jnp.where(mine, back_ref[1].astype(F32), back_ref[2].astype(F32))
    for m in range(2):
        input_out[m] = jnp.where(s // 2 == m, same, other)

    @pl.when(row == 0)
    def _():
        vectors = side_ref[0, HALF : HALF + 16, :].astype(F32)
        bias_out[...] = vectors[0:1]
        gain_out[...] = vectors[1:2]
        shift_out[...] = vectors[2:3]
        loss_out[...] = jnp.sum(vectors[3:4], axis=1, keepdims=True) * (1.0 / queries_all)
        projection_out[...] = side_ref[0, HALF + 16 :, :].astype(F32)


def assemble(first_sum, side_sum, down_sum, back, queries_all):
    width = back.shape[1]
    steps = D // 128

    def whole(shape):
        return pl.BlockSpec(shape, lambda i: (0,) * len(shape))

    return pl.pallas_call(
        partial(assemble_kernel, queries_all),
        grid=(steps,),
        in_specs=[
            pl.BlockSpec((2, 128, FRONT), lambda i: (0, i, 0)),
            whole((2, SIDE, D)),
            pl.BlockSpec((256, D), lambda i: (i, 0)),
            pl.BlockSpec((4, width, 128), lambda i: (0, 0, i)),
        ],
        out_specs=[
            pl.BlockSpec((128, 4 * D), lambda i: (i, 0)),
            pl.BlockSpec((256, D), lambda i: (i, 0)),
            pl.BlockSpec((2, width, 128), lambda i: (0, 0, i)),
            whole((1, D)),
            whole((1, D)),
            whole((1, D)),
            whole((EXTRA, D)),
            whole((1, 1)),
        ],
        out_shape=[
            jax.ShapeDtypeStruct(shape, F32)
            for shape in (
                (D, 4 * D),
                (2 * D, D),
                (2, width, ROWS),
                (1, D),
                (1, D),
                (1, D),
                (EXTRA, D),
                (1, 1),
            )
        ],
        compiler_params=pltpu.CompilerParams(vmem_limit_bytes=60 * 1024 * 1024),
    )(first_sum, side_sum, down_sum.reshape(2 * D, D), back)


def gelu_and_slope(z):
    upper = 0.5 * (1.0 + lax.erf(z * 0.7071067811865476))
    density = jnp.exp(-0.5 * z * z) * 0.3989422804014327
    return (z * upper).astype(BF), (upper + z * density).astype(BF)


def on_device(
    inputs,
    in_weight,
    down_weight,
    out_bias,
    norm_gains,
    norm_shifts,
    projection,
    passage_lengths,
    positive,
):
    batches = lax.axis_size("batch")
    layers = batches // 2
    queries_all = inputs.shape[0] * batches * QUERY_COUNT
    first_all, rest_all, vectors, *kept, dw, tails, bound = forward(
        in_weight[0],
        down_weight,
        inputs.transpose(0, 2, 1),
        projection.T,
        (out_bias, norm_gains, norm_shifts),
        passage_lengths[:, 0],
        positive,
        layers,
        queries_all,
    )
    first_sum, side_sum, down_sum, back = backward(
        first_all, rest_all, vectors, kept, dw, tails, bound, inputs.shape[2], layers
    )
    in_grad, down_grad, input_grad, bias_grad, gain_grad, shift_grad, projection_grad, loss = (
        assemble(first_sum, side_sum, down_sum, back, queries_all)
    )
    return (
        loss[0, 0],
        input_grad.transpose(0, 2, 1),
        in_grad[None],
        down_grad,
        bias_grad,
        gain_grad,
        shift_grad,
        projection_grad.T,
    )


def solution(mesh):
    in_specs = (
        P(None, "batch", "section"),
        P("section", None, None),
        P("section", None),
        P("section", None),
        P("section", None),
        P("section", None),
        P(None, "section"),
        P(None, "batch", None),
        P(None, "batch"),
    )
    out_specs = (
        P(),
        P(None, "batch", "section"),
        P("section", None, None),
        P("section", None),
        P("section", None),
        P("section", None),
        P("section", None),
        P(None, "section"),
    )
    return jax.shard_map(
        on_device, mesh=mesh, in_specs=in_specs, out_specs=out_specs, check_vma=False
    )
```
